32 devices in a mesh: section: 4 (over y, x), slab: 8 (over z, core).
Axes of the slice: x: 2, y: 2, z: 4, core: 2. Of those that a mesh axis runs over, the one named last changes fastest.
Arguments:
- features: bfloat16 [4, 8, 16, 2, 8, 256], P('section', None, 'slab'), may hold values from -40 to 40
- vae_weight: bfloat16 [3, 3, 3, 256, 256], replicated, may hold values from -0.078125 to 0.078125
- vae_gain: float32 [256], replicated, may hold values from 0.25 to 1.75
- vae_shift: float32 [256], replicated, may hold values from -3 to 3
- vae_bias: float32 [256], replicated, may hold values from -3 to 3
- latent_weight: bfloat16 [256, 16], replicated, may hold values from -0.375 to 0.375
- latent_bias: float32 [16], replicated, may hold values from -3 to 3
- slot_clips: int32 [4, 8], replicated, may hold values from 0 to 7, each once within a row
- row_offsets: int32 [4, 8], replicated, may hold values from 0 to 120
- in_weight: bfloat16 [3, 3, 16, 320], replicated, may hold values from -0.5 to 0.5
- in_bias: float32 [320], replicated, may hold values from -3 to 3
- pos_table: bfloat16 [128, 320], replicated, may hold values from -3 to 3
- unet_gain: float32 [4, 320], P('section'), may hold values from 0.25 to 1.75
- unet_shift: float32 [4, 320], P('section'), may hold values from -3 to 3
- unet_weight: bfloat16 [4, 3, 3, 320, 320], P('section'), may hold values from -0.109375 to 0.109375
- unet_bias: float32 [4, 320], P('section'), may hold values from -3 to 3
Outputs:
- layer_outputs: bfloat16 [4, 4, 8, 8, 2, 1280], P('section', None, 'slab')
The draws below stay inside these ranges and needn't reach their ends.
Inputs may be any that keep to these rules, and one draw needn't show every extreme that they name: Each row of slot_clips is a permutation of 0 to 7.
All inputs are finite; a program needn't handle non-finite values.
Results may differ from the reference program's by a relative error of at most 0.025.
Values may be sent and summed in bfloat16 or wider, within the bound.
No kernel may reach another device: no remote copies, remote signals or barrier semaphores. Data moves between devices by JAX's collectives and lax.ppermute only.
A program may use at most 64 MiB of HBM per device.

```python
import jax
import jax.numpy as jnp
from jax import lax

CV = 256
CL = 16
CU = 320
GROUPS = 32
FRAMES = 2
FRAME_ROWS = 128
COLS = 8
MICRO = 4
LAYERS = 4
CLIPS = 8
ROWS = 16
LAT_ROWS = 8
LAT_COLS = 4


def draw_features(key, part):
    first_key, second_key = jax.random.split(key, 2)
    full_shape = (MICRO, CLIPS, ROWS, FRAMES, COLS, CV)
    row_frac = jnp.arange(ROWS, dtype=jnp.float32) / ROWS
    channel_draw = jax.random.uniform(second_key, (CV,), jnp.float32)
    basic_draw = jnp.clip(jax.random.normal(first_key, full_shape, jnp.float32), -6.0, 6.0)
    row_scale = 10.0 ** (row_frac - 0.5)
    channel_scale = 10.0 ** (0.5 * (channel_draw - 0.5))
    return (basic_draw * row_scale[:, None, None, None] * channel_scale).astype(jnp.bfloat16)


def set_ends(entries, rng, smallest, high):
    shape = entries.shape
    index_at = [jax.random.randint(jax.random.fold_in(rng, axis), (), 0, shape[axis]) for axis in range(len(shape))]
    entries = entries.at[tuple(index_at)].set(smallest)
    longest = shape.index(max(shape))
    index_at[longest] = (index_at[longest] + 1) % shape[longest]
    return entries.at[tuple(index_at)].set(high)


def block_levels(own_key, extent, cuts, low, largest):
    factor_of = 1.0
    for dim, shards_of in cuts:
        heights = jax.random.uniform(jax.random.fold_in(jax.random.fold_in(own_key, 6), dim), (shards_of,), jnp.float32, low / len(cuts), largest / len(cuts))
        factor_of = factor_of * jnp.repeat(jnp.exp(heights), extent[dim] // shards_of).reshape((-1,) + (1,) * (len(extent) - 1 - dim))
    return factor_of


def centred(key, extent, width, limit, cuts=(), kind=jnp.bfloat16):
    drawn = jax.random.normal(key, extent, jnp.float32) * width
    if len(cuts) > 0:
        drawn = block_levels(key, extent, cuts, -0.22, 0.18) * drawn
    return jnp.clip(drawn, min=-limit, max=limit).astype(kind)


def setup_inputs(seed: int = 0) -> dict:
    arg_keys = jax.random.split(jax.random.key(seed), 17)
    return {
        "features": draw_features(jax.random.fold_in(arg_keys[16], 71), 0),
        "vae_weight": centred(arg_keys[1], (3, 3, 3, CV, CV), (27 * CV) ** -0.5, 0.078125),
        "vae_gain": jnp.clip(1.0 + 0.15 * jax.random.normal(arg_keys[2], (CV,), jnp.float32), 0.25, 1.75),
        "vae_shift": centred(arg_keys[3], (CV,), 0.5, 3.0, (), jnp.float32),
        "vae_bias": centred(arg_keys[4], (CV,), 0.5, 3.0, (), jnp.float32),
        "latent_weight": centred(arg_keys[5], (CV, CL), CV ** -0.5, 0.375),
        "latent_bias": centred(arg_keys[6], (CL,), 0.5, 3.0, (), jnp.float32),
        "slot_clips": jax.vmap(lambda own: jax.random.permutation(own, CLIPS))(jax.random.split(arg_keys[7], MICRO)).reshape((MICRO, CLIPS)).astype(jnp.int32),
        "row_offsets": set_ends(jax.random.randint(arg_keys[8], (MICRO, CLIPS), 0, FRAME_ROWS - LAT_ROWS + 1), jax.random.fold_in(arg_keys[8], 1), 0, FRAME_ROWS - LAT_ROWS).astype(jnp.int32),
        "in_weight": centred(arg_keys[9], (3, 3, CL, CU), (9 * CL) ** -0.5, 0.5),
        "in_bias": centred(arg_keys[10], (CU,), 0.5, 3.0, (), jnp.float32),
        "pos_table": centred(arg_keys[11], (FRAME_ROWS, CU), 0.5, 3.0),
        "unet_gain": jnp.clip(1.0 + 0.15 * jax.random.normal(arg_keys[12], (LAYERS, CU), jnp.float32), 0.25, 1.75),
        "unet_shift": centred(arg_keys[13], (LAYERS, CU), 0.5, 3.0, ((0, 4),), jnp.float32),
        "unet_weight": centred(arg_keys[14], (LAYERS, 3, 3, CU, CU), (9 * CU) ** -0.5, 0.109375, ((0, 4),)),
        "unet_bias": centred(arg_keys[15], (LAYERS, CU), 0.5, 3.0, ((0, 4),), jnp.float32),
    }


norm_eps = 1e-06

def group_stats(values, groups):
    full_shape = values.shape
    grouped = values.reshape(full_shape[0], -1, groups, full_shape[-1] // groups)
    return (lax.optimization_barrier(jnp.sum(grouped, axis=(1, 3))), lax.optimization_barrier(jnp.sum(grouped * grouped, axis=(1, 3))))

def normalize(values, sums, squares, cell_count, gain, shift, groups):
    mean_value = sums / cell_count
    variance = squares / cell_count - mean_value * mean_value
    inverse = lax.rsqrt(variance + norm_eps)
    full_shape = values.shape
    grouped = values.reshape(full_shape[0], -1, groups, full_shape[-1] // groups)
    normed = (grouped - mean_value[:, None, :, None]) * inverse[:, None, :, None]
    return normed.reshape(full_shape) * gain + shift

def keep_stats(stats_pair):
    return stats_pair

def zero_rows(active):
    return jnp.pad(active, ((0, 0), (1, 1), (0, 0), (0, 0), (0, 0)))

def encode(features, rows_total, reduce_stats, extend_rows, encoder):
    vae_weight, vae_gain, vae_shift, vae_bias, latent_weight, latent_bias = encoder
    clip_count, rows_here, frame_count, col_count, channels = features.shape
    values = features.astype(jnp.float32)
    sums, squares = reduce_stats(group_stats(values, GROUPS))
    cell_count = rows_total * frame_count * col_count * (channels // GROUPS)
    normed = normalize(values, sums, squares, cell_count, vae_gain, vae_shift, GROUPS)
    active = jax.nn.silu(normed).astype(jnp.bfloat16)
    extended = extend_rows(active)
    first_frame = extended[:, :, :1]
    timed = jnp.concatenate([first_frame, first_frame, extended], axis=2)
    padded = jnp.pad(timed, ((0, 0), (0, 0), (0, 0), (1, 1), (0, 0)))
    mixed = jnp.zeros((clip_count * rows_here * frame_count * col_count, channels), jnp.float32)
    for time_tap in range(3):
        for row_tap in range(3):
            for col_tap in range(3):
                window = padded[:, row_tap:row_tap + rows_here, time_tap:time_tap + frame_count, col_tap:col_tap + col_count, :]
                mixed = mixed + jnp.dot(window.reshape(-1, channels), vae_weight[time_tap, row_tap, col_tap], preferred_element_type=jnp.float32)
    summed = values + mixed.reshape(values.shape) + vae_bias
    pooled = summed.reshape(clip_count, rows_here // 2, 2, frame_count, col_count // 2, 2, channels).mean(axis=(2, 5)).astype(jnp.bfloat16)
    latent = jnp.dot(pooled.reshape(-1, channels), latent_weight, preferred_element_type=jnp.float32) + latent_bias
    return latent.astype(jnp.bfloat16).reshape(clip_count, rows_here // 2, frame_count, col_count // 2, -1)

def spatial_conv(active, weight):
    clip_count, row_count, frame_count, col_count, channels = active.shape
    padded = jnp.pad(active, ((0, 0), (1, 1), (0, 0), (1, 1), (0, 0)))
    total = jnp.zeros((clip_count * row_count * frame_count * col_count, weight.shape[-1]), jnp.float32)
    for row_tap in range(3):
        for col_tap in range(3):
            window = padded[:, row_tap:row_tap + row_count, :, col_tap:col_tap + col_count, :]
            total = total + jnp.dot(window.reshape(-1, channels), weight[row_tap, col_tap], preferred_element_type=jnp.float32)
    return total.reshape(clip_count, row_count, frame_count, col_count, -1)

def embed(latent, offsets_now, in_weight, in_bias, pos_table):
    projected = spatial_conv(latent, in_weight) + in_bias
    row_count = latent.shape[1]
    table_rows = pos_table.shape[0]
    wanted = offsets_now[:, None] + jnp.arange(row_count, dtype=jnp.int32)[None, :]
    one_hot = (wanted[:, :, None] == jnp.arange(table_rows, dtype=jnp.int32)[None, None, :]).astype(jnp.bfloat16)
    placed = jnp.dot(one_hot.reshape(-1, table_rows), pos_table, preferred_element_type=jnp.float32)
    placed = placed.reshape(latent.shape[0], row_count, 1, 1, -1)
    return (projected + placed).astype(jnp.bfloat16)

def unet_layer(state, gain, shift, weight, bias):
    values = state.astype(jnp.float32)
    sums, squares = group_stats(values, GROUPS)
    cell_count = values.shape[1] * values.shape[2] * values.shape[3] * (values.shape[4] // GROUPS)
    normed = normalize(values, sums, squares, cell_count, gain, shift, GROUPS)
    active = jax.nn.silu(normed).astype(jnp.bfloat16)
    return (values + spatial_conv(active, weight) + bias).astype(jnp.bfloat16)

def reference(features, vae_weight, vae_gain, vae_shift, vae_bias, latent_weight, latent_bias, slot_clips, row_offsets, in_weight, in_bias, pos_table, unet_gain, unet_shift, unet_weight, unet_bias):
    encoder = (vae_weight, vae_gain, vae_shift, vae_bias, latent_weight, latent_bias)

    def per_micro(micro_index):
        micro_batch = lax.dynamic_index_in_dim(features, micro_index, 0, keepdims=False)
        latent = encode(micro_batch, micro_batch.shape[1], keep_stats, zero_rows, encoder)
        order = lax.dynamic_index_in_dim(slot_clips, micro_index, 0, keepdims=False)
        ordered = jnp.take(latent, order, axis=0)
        offsets_row = lax.dynamic_index_in_dim(row_offsets, micro_index, 0, keepdims=False)
        state = embed(ordered, jnp.take(offsets_row, order), in_weight, in_bias, pos_table)
        outputs = []
        for layer_index in range(LAYERS):
            state = unet_layer(state, unet_gain[layer_index], unet_shift[layer_index], unet_weight[layer_index], unet_bias[layer_index])
            outputs.append(state)
        return jnp.stack(outputs)
    stacked = lax.map(per_micro, jnp.arange(MICRO, dtype=jnp.int32))
    stacked = jnp.transpose(stacked, (1, 0, 2, 3, 4, 5, 6))
    return stacked.reshape(LAYERS, MICRO, CLIPS, LAT_ROWS, FRAMES, LAT_COLS * CU)
```

```python
import functools

import jax
import jax.numpy as jnp
from jax import lax
from jax.experimental import pallas as pl
from jax.experimental.pallas import tpu as pltpu
from jax.sharding import PartitionSpec as P

GROUPS = 32
LANES = 128
EPS = 1e-06
VMEM_LIMIT = 48 * 1024 * 1024
F32 = jnp.float32
BF16 = jnp.bfloat16


def vmem():
    return pl.BlockSpec(memory_space=pltpu.VMEM)


def smem():
    return pl.BlockSpec(memory_space=pltpu.SMEM)


def params():
    return pltpu.CompilerParams(vmem_limit_bytes=VMEM_LIMIT)


def group_sums(rows, channels):
    size = channels // GROUPS
    count = rows.shape[0]

    def group_of(axis):
        index = lax.broadcasted_iota(jnp.int32, (channels, channels), axis).astype(F32)
        return jnp.floor((index + 0.5) * (1.0 / size))

    same = (group_of(0) == group_of(1)).astype(BF16)
    high = rows.astype(BF16)
    rest = rows - high.astype(F32)
    middle = rest.astype(BF16)
    low = (rest - middle.astype(F32)).astype(BF16)
    total = jnp.dot(high, same, preferred_element_type=F32)
    total += jnp.dot(middle, same, preferred_element_type=F32)
    total += jnp.dot(low, same, preferred_element_type=F32)
    return total.reshape(count, channels)


def silu(value):
    return value / (1.0 + jnp.exp(-value))


def encode_kernel(
    x_ref, weight_ref, gain_ref, shift_ref, bias_ref, lat_weight_ref, lat_bias_ref,
    out_ref, dup_ref, act_ref, pool_ref,
):
    row_count, frames, cols, channels = x_ref.shape[1:]
    plane = frames * cols
    size = row_count * plane
    lat_rows, lat_cols = row_count // 2, cols // 2
    for item in range(x_ref.shape[0]):
        x = x_ref[item].astype(F32).reshape(size, channels)
        sums = jnp.concatenate(
            [jnp.sum(x, axis=0, keepdims=True), jnp.sum(x * x, axis=0, keepdims=True)]
            + [jnp.zeros((6, channels), F32)],
            axis=0,
        )
        sums = group_sums(sums, channels) * (1.0 / (size * (channels // GROUPS)))
        mean = sums[0:1]
        inverse = lax.rsqrt(sums[1:2] - mean * mean + EPS)
        act = silu((x - mean) * inverse * gain_ref[...] + shift_ref[...])
        column = lax.broadcasted_iota(jnp.int32, (size, 1), 0) & (cols - 1)
        for tap in range(3):
            if tap == 0:
                moved = jnp.where(column == 0, 0.0, pltpu.roll(act, 1, 0))
            elif tap == 2:
                moved = jnp.where(column == cols - 1, 0.0, pltpu.roll(act, size - 1, 0))
            else:
                moved = act
            lanes = pl.ds(tap * channels, channels)
            first = moved.reshape(row_count, frames, cols, channels)[:, 0:1]
            first = jnp.broadcast_to(first, (row_count, frames, cols, channels))
            act_ref[pl.ds(plane, size), lanes] = moved.astype(BF16)
            dup_ref[pl.ds(plane, size), lanes] = first.reshape(size, channels).astype(BF16)
        for ref in (act_ref, dup_ref):
            ref[pl.ds(0, plane), :] = jnp.zeros((plane, 3 * channels), BF16)
            ref[pl.ds(plane + size, plane), :] = jnp.zeros((plane, 3 * channels), BF16)
        total = x + bias_ref[...]
        for time_tap in range(3):
            source = act_ref if time_tap == 2 else dup_ref
            for row_tap in range(3):
                weight = weight_ref[time_tap, row_tap].reshape(3 * channels, channels)
                window = source[pl.ds(row_tap * plane, size), :]
                total += jnp.dot(window, weight, preferred_element_type=F32)
        paired = total.reshape(lat_rows, 2, plane, channels)
        merged = (paired[:, 0] + paired[:, 1]).reshape(lat_rows * plane, channels)
        halves = []
        for part in range(channels // LANES):
            pool_ref[part] = merged[:, part * LANES : (part + 1) * LANES]
            picked = []
            for col in range(lat_cols):
                left = pool_ref[part, pl.ds(2 * col, lat_rows * frames, stride=cols), :]
                right = pool_ref[part, pl.ds(2 * col + 1, lat_rows * frames, stride=cols), :]
                picked.append((left + right) * 0.25)
            halves.append(jnp.concatenate(picked, axis=0))
        pooled = jnp.concatenate(halves, axis=1).astype(BF16)
        latent = jnp.dot(pooled, lat_weight_ref[...], preferred_element_type=F32)
        out_ref[item] = (latent + lat_bias_ref[...]).astype(BF16)


def encode(clips, vae_weight, gain, shift, bias, lat_weight, lat_bias):
    items, row_count, frames, cols, channels = clips.shape
    plane = frames * cols
    lat_rows, lat_cols = row_count // 2, cols // 2
    padded = pltpu.VMEM(((row_count + 2) * plane, 3 * channels), BF16)
    return pl.pallas_call(
        encode_kernel,
        out_shape=jax.ShapeDtypeStruct(
            (items, lat_cols * lat_rows * frames, lat_weight.shape[1]), BF16
        ),
        in_specs=[vmem()] * 7,
        out_specs=vmem(),
        scratch_shapes=[padded, padded, pltpu.VMEM((channels // LANES, lat_rows * plane, LANES), F32)],
        compiler_params=params(),
        name="encode",
    )(
        clips, vae_weight, gain.reshape(1, -1), shift.reshape(1, -1), bias.reshape(1, -1),
        lat_weight, lat_bias.reshape(1, -1),
    )


def fill_taps(value, taps_ref, block, frames):
    size, channels = value.shape
    unit = block[1]
    edge = block[0] * unit
    place = lax.broadcasted_iota(jnp.int32, (size, 1), 0) & (unit - 1)
    for tap in range(3):
        if tap == 0:
            moved = jnp.where(place < frames, 0.0, pltpu.roll(value, frames, 0))
        elif tap == 2:
            moved = jnp.where(place >= unit - frames, 0.0, pltpu.roll(value, size - frames, 0))
        else:
            moved = value
        taps_ref[tap, pl.ds(edge, size), :] = moved.astype(BF16)
        taps_ref[tap, pl.ds(0, edge), :] = jnp.zeros((edge, channels), BF16)
        taps_ref[tap, pl.ds(edge + size, edge), :] = jnp.zeros((edge, channels), BF16)


def conv_taps(total, taps_ref, weight_ref, block):
    size = total.shape[0]
    edge = block[0] * block[1]
    for row_tap in range(3):
        for col_tap in range(3):
            window = taps_ref[row_tap, pl.ds(col_tap * edge, size), :]
            total += jnp.dot(window, weight_ref[row_tap, col_tap], preferred_element_type=F32)
    return total


def unet_layer(state, weight_ref, gain, shift, bias, taps_ref, block, frames):
    streams, unit = block
    size, channels = state.shape
    cols = size // (streams * unit)
    values = state.reshape(cols, streams, unit, channels)
    rows = []
    for item in range(streams):
        own = values[:, item].reshape(cols * unit, channels)
        rows.append(jnp.sum(own, axis=0, keepdims=True))
        rows.append(jnp.sum(own * own, axis=0, keepdims=True))
    rows.extend([jnp.zeros((1, channels), F32)] * (-len(rows) % 8))
    sums = group_sums(jnp.concatenate(rows, axis=0), channels)
    sums = sums * (1.0 / (cols * unit * (channels // GROUPS)))
    normed = []
    for item in range(streams):
        mean = sums[2 * item : 2 * item + 1]
        inverse = lax.rsqrt(sums[2 * item + 1 : 2 * item + 2] - mean * mean + EPS)
        normed.append((values[:, item : item + 1] - mean) * inverse * gain + shift)
    act = silu(jnp.concatenate(normed, axis=1).reshape(size, channels))
    fill_taps(act, taps_ref, block, frames)
    return conv_taps(state + bias, taps_ref, weight_ref, block).astype(BF16)


def write_output(out_ref, state, block):
    streams, unit = block
    channels = state.shape[1]
    cols = state.shape[0] // (streams * unit)
    values = state.reshape(cols, streams, unit, channels)
    for item in range(streams):
        for col in range(cols):
            out_ref[item, :, pl.ds(col * channels, channels)] = values[col, item]


def first_kernel(
    block, frames, slab, owned, section_axis,
    *refs,
):
    streams, unit = block
    latent_refs = refs[: streams // owned]
    (
        clips_ref, offsets_ref, in_weight_ref, in_bias_ref, table_ref, weight_ref, gain_ref, shift_ref, bias_ref,
        state_ref, out_ref, lat_taps_ref, taps_ref,
    ) = refs[streams // owned :]
    table_rows, width = table_ref.shape

    @pl.when(lax.axis_index(section_axis) == 0)
    def _():
        cols = state_ref.shape[0] // (streams * unit)
        first = lax.axis_index(slab) * owned
        parts = []
        for col in range(cols):
            for ref in latent_refs:
                for item in range(owned):
                    parts.append(ref[item, pl.ds(col * unit, unit), :])
        fill_taps(jnp.concatenate(parts, axis=0).astype(F32), lat_taps_ref, block, frames)
        size = cols * streams * unit
        total = jnp.broadcast_to(in_bias_ref[...], (size, width))
        total = conv_taps(total, lat_taps_ref, in_weight_ref, block)
        row = lax.broadcasted_iota(jnp.int32, (unit, table_rows), 0)
        row = lax.div(row, frames)
        wanted = lax.broadcasted_iota(jnp.int32, (unit, table_rows), 1)
        hot = []
        for item in range(streams):
            micro = item // owned
            offset = offsets_ref[micro, clips_ref[micro, first + item % owned]]
            hot.append((wanted - row == offset).astype(F32))
        placed = jnp.dot(
            jnp.concatenate(hot, axis=0).astype(BF16), table_ref[...], preferred_element_type=F32
        )
        placed = placed.reshape(1, streams * unit, width)
        total = (total.reshape(cols, streams * unit, width) + placed).reshape(size, width)
        state = total.astype(BF16).astype(F32)
        state = unet_layer(
            state, weight_ref, gain_ref[...], shift_ref[...], bias_ref[...], taps_ref, block, frames
        )
        state_ref[...] = state
        write_output(out_ref, state, block)


def later_kernel(
    stage, block, frames, section_axis,
    before_ref, out_in_ref, weight_ref, gain_ref, shift_ref, bias_ref, state_ref, out_ref, taps_ref,
):
    del out_in_ref

    @pl.when(lax.axis_index(section_axis) == stage)
    def _():
        state = unet_layer(
            before_ref[...].astype(F32), weight_ref, gain_ref[...], shift_ref[...], bias_ref[...],
            taps_ref, block, frames,
        )
        state_ref[...] = state
        write_output(out_ref, state, block)


def select_kernel(section_axis, clips_ref, features_ref, out_ref):
    section = lax.axis_index(section_axis)
    for slot in range(out_ref.shape[0]):
        out_ref[slot] = features_ref[clips_ref[section, slot]]


def per_device(
    features, vae_weight, vae_gain, vae_shift, vae_bias, latent_weight, latent_bias, slot_clips, row_offsets,
    in_weight, in_bias, pos_table, unet_gain, unet_shift, unet_weight, unet_bias,
):
    section_count = lax.axis_size("section")
    slab_count = lax.axis_size("slab")
    _, clip_total, slab_rows, frames, cols, channels = features.shape
    owned = clip_total // slab_count
    row_total = slab_rows * slab_count
    width = unet_weight.shape[-1]

    ordered = pl.pallas_call(
        functools.partial(select_kernel, "section"),
        out_shape=jax.ShapeDtypeStruct(features.shape[1:], BF16),
        in_specs=[smem(), vmem()],
        out_specs=vmem(),
        name="select",
    )(slot_clips, features[0])
    shaped = ordered.reshape(slab_count, owned, slab_rows, frames, cols, channels)
    whole = lax.all_to_all(shaped, "slab", split_axis=0, concat_axis=0)
    whole = jnp.swapaxes(whole, 0, 1).reshape(owned, row_total, frames, cols, channels)
    latent = encode(
        whole, vae_weight, vae_gain, vae_shift, vae_bias, latent_weight, latent_bias
    )

    latents = [latent]
    for other in range(1, section_count):
        latents.append(lax.ppermute(latent, "section", [(other, 0)]))

    lat_rows, lat_cols = row_total // 2, cols // 2
    unit = lat_rows * frames
    streams = section_count * owned
    block = (streams, unit)
    size = lat_cols * streams * unit
    taps = pltpu.VMEM((3, size + 2 * streams * unit, width), BF16)
    lat_taps = pltpu.VMEM((3, size + 2 * streams * unit, latent.shape[-1]), BF16)
    result_shapes = [
        jax.ShapeDtypeStruct((size, width), BF16),
        jax.ShapeDtypeStruct((streams, unit, lat_cols * width), BF16),
    ]
    weight = unet_weight[0]
    state, out = pl.pallas_call(
        functools.partial(first_kernel, block, frames, "slab", owned, "section"),
        out_shape=result_shapes,
        in_specs=[vmem()] * section_count + [smem()] * 2 + [vmem()] * 7,
        out_specs=[vmem()] * 2,
        scratch_shapes=[lat_taps, taps],
        compiler_params=params(),
        name="first_block",
    )(
        *latents, slot_clips, row_offsets, in_weight, in_bias.reshape(1, -1), pos_table,
        weight, unet_gain, unet_shift, unet_bias,
    )
    for stage in range(1, section_count):
        arrived = lax.ppermute(state, "section", [(stage - 1, stage)])
        state, out = pl.pallas_call(
            functools.partial(later_kernel, stage, block, frames, "section"),
            out_shape=result_shapes,
            in_specs=[vmem()] * 6,
            out_specs=[vmem()] * 2,
            scratch_shapes=[taps],
            input_output_aliases={1: 1},
            compiler_params=params(),
            name="later_block",
        )(arrived, out, weight, unet_gain, unet_shift, unet_bias)
    return out.reshape(1, section_count, owned, lat_rows, frames, lat_cols * width)


def solution(mesh):
    return jax.shard_map(
        per_device,
        mesh=mesh,
        in_specs=(
            P("section", None, "slab", None, None, None),
            P(),
            P(),
            P(),
            P(),
            P(),
            P(),
            P(),
            P(),
            P(),
            P(),
            P(),
            P("section", None),
            P("section", None),
            P("section", None, None, None, None),
            P("section", None),
        ),
        out_specs=P("section", None, "slab", None, None, None),
        check_vma=False,
    )
```

```python
import functools

import jax
import jax.numpy as jnp
from jax import lax
from jax.experimental import pallas as pl
from jax.experimental.pallas import tpu as pltpu
from jax.sharding import PartitionSpec as P

GROUPS = 32
LANES = 128
PLACE_FLOPS = 6_000_000_000
EPS = 1e-06
VMEM_LIMIT = 32 * 1024 * 1024
PLACE_VMEM = 8 * 1024 * 1024
F32 = jnp.float32
BF16 = jnp.bfloat16


def vmem():
    return pl.BlockSpec(memory_space=pltpu.VMEM)


def smem():
    return pl.BlockSpec(memory_space=pltpu.SMEM)


def params(limit=VMEM_LIMIT):
    return pltpu.CompilerParams(vmem_limit_bytes=limit)


def same_group(channels):
    size = channels // GROUPS

    def group_of(axis):
        index = lax.broadcasted_iota(jnp.int32, (channels, channels), axis).astype(F32)
        return jnp.floor((index + 0.5) * (1.0 / size))

    return jnp.where(group_of(0) == group_of(1), 1.0, 0.0).astype(BF16)


def group_sums(rows, same):
    high = rows.astype(BF16)
    rest = rows - high.astype(F32)
    middle = rest.astype(BF16)
    low = (rest - middle.astype(F32)).astype(BF16)
    total = jnp.dot(high, same, preferred_element_type=F32)
    total += jnp.dot(middle, same, preferred_element_type=F32)
    total += jnp.dot(low, same, preferred_element_type=F32)
    return total


def dot_last(left, right):
    return lax.dot_general(left, right, (((1,), (1,)), ((), ())), preferred_element_type=F32)


def silu(value):
    return value / (1.0 + jnp.exp(-value))


def encode_kernel(
    x_ref, weight_ref, gain_ref, shift_ref, bias_ref, lat_weight_ref, lat_bias_ref, after_ref,
    out_ref, dup_ref, act_ref, pool_ref,
):
    del after_ref
    row_count, frames, cols, channels = x_ref.shape[1:]
    plane = frames * cols
    size = row_count * plane
    lat_rows, lat_cols = row_count // 2, cols // 2
    same = same_group(channels)
    for item in range(x_ref.shape[0]):
        x = x_ref[item].astype(F32).reshape(size, channels)
        sums = jnp.concatenate(
            [jnp.sum(x, axis=0, keepdims=True), jnp.sum(x * x, axis=0, keepdims=True)]
            + [jnp.zeros((6, channels), F32)],
            axis=0,
        )
        sums = group_sums(sums, same) * (1.0 / (size * (channels // GROUPS)))
        mean = sums[0:1]
        inverse = lax.rsqrt(sums[1:2] - mean * mean + EPS)
        act = silu((x - mean) * inverse * gain_ref[...] + shift_ref[...])
        column = lax.broadcasted_iota(jnp.int32, (size, 1), 0) & (cols - 1)
        for tap in range(3):
            if tap == 0:
                moved = jnp.where(column == 0, 0.0, pltpu.roll(act, 1, 0))
            elif tap == 2:
                moved = jnp.where(column == cols - 1, 0.0, pltpu.roll(act, size - 1, 0))
            else:
                moved = act
            lanes = pl.ds(tap * channels, channels)
            first = moved.reshape(row_count, frames, cols, channels)[:, 0:1]
            first = jnp.broadcast_to(first, (row_count, frames, cols, channels))
            act_ref[pl.ds(plane, size), lanes] = moved.astype(BF16)
            dup_ref[pl.ds(plane, size), lanes] = first.reshape(size, channels).astype(BF16)
        for ref in (act_ref, dup_ref):
            ref[pl.ds(0, plane), :] = jnp.zeros((plane, 3 * channels), BF16)
            ref[pl.ds(plane + size, plane), :] = jnp.zeros((plane, 3 * channels), BF16)
        total = x + bias_ref[...]
        for time_tap in range(3):
            source = act_ref if time_tap == 2 else dup_ref
            for row_tap in range(3):
                weight = weight_ref[time_tap, row_tap].reshape(3 * channels, channels)
                window = source[pl.ds(row_tap * plane, size), :]
                total += jnp.dot(window, weight, preferred_element_type=F32)
        paired = total.reshape(lat_rows, 2, plane, channels)
        merged = (paired[:, 0] + paired[:, 1]).reshape(lat_rows * plane, channels)
        halves = []
        for part in range(channels // LANES):
            pool_ref[part] = merged[:, part * LANES : (part + 1) * LANES]
            picked = []
            for col in range(lat_cols):
                left = pool_ref[part, pl.ds(2 * col, lat_rows * frames, stride=cols), :]
                right = pool_ref[part, pl.ds(2 * col + 1, lat_rows * frames, stride=cols), :]
                picked.append((left + right) * 0.25)
            halves.append(jnp.concatenate(picked, axis=0))
        pooled = jnp.concatenate(halves, axis=1).astype(BF16)
        latent = dot_last(pooled, lat_weight_ref[...])
        out_ref[item] = (latent + lat_bias_ref[...]).astype(BF16)


def encode(clips, *operands):
    items, row_count, frames, cols, channels = clips.shape
    plane = frames * cols
    lat_rows, lat_cols = row_count // 2, cols // 2
    padded = pltpu.VMEM(((row_count + 2) * plane, 3 * channels), BF16)
    return pl.pallas_call(
        encode_kernel,
        out_shape=jax.ShapeDtypeStruct((items, lat_cols * lat_rows * frames, operands[-2].shape[1]), BF16),
        in_specs=[vmem()] * len(operands) + [pl.BlockSpec(memory_space=pl.ANY)],
        out_specs=vmem(),
        scratch_shapes=[
            padded,
            padded,
            pltpu.VMEM((channels // LANES, lat_rows * plane, LANES), F32),
        ],
        compiler_params=params(),
        name="encode",
    )(clips, *operands)


def shifted(value, unit, frames):
    size = value.shape[0]
    place = lax.broadcasted_iota(jnp.int32, (size, 1), 0) & (unit - 1)
    return (
        jnp.where(place < frames, 0.0, pltpu.roll(value, frames, 0)),
        value,
        jnp.where(place >= unit - frames, 0.0, pltpu.roll(value, size - frames, 0)),
    )


def conv3(value, weight_ref, taps_ref, block, frames):
    streams, unit = block
    size, channels = value.shape
    edge = streams * unit
    zeros = jnp.zeros((edge, channels), BF16)
    total = None
    for row_tap, moved in enumerate(shifted(value, unit, frames)):
        taps_ref[row_tap, pl.ds(edge, size), :] = moved.astype(BF16)
        taps_ref[row_tap, pl.ds(0, edge), :] = zeros
        taps_ref[row_tap, pl.ds(edge + size, edge), :] = zeros
        for col_tap in range(3):
            window = taps_ref[row_tap, pl.ds(col_tap * edge, size), :]
            term = jnp.dot(window, weight_ref[row_tap, col_tap], preferred_element_type=F32)
            total = term if total is None else total + term
    return total


def conv3_narrow(value, weight, block, frames):
    streams, unit = block
    size, channels = value.shape
    edge = streams * unit
    zeros = jnp.zeros((edge, channels), F32)
    windows = []
    for moved in shifted(value, unit, frames):
        padded = jnp.concatenate([zeros, moved, zeros], axis=0)
        for col_tap in range(3):
            windows.append(padded[col_tap * edge : col_tap * edge + size])
    window = jnp.concatenate(windows, axis=1).astype(BF16)
    return jnp.dot(window, weight, preferred_element_type=F32)


def unet_layer(state, operands, taps_ref, block, frames):
    weight_ref, gain_ref, shift_ref, bias_ref = operands
    streams, unit = block
    size, channels = state.shape
    cols = size // (streams * unit)
    values = state.reshape(cols, streams, unit, channels)
    rows = []
    for item in range(streams):
        own = values[:, item].reshape(cols * unit, channels)
        rows.append(jnp.sum(own, axis=0, keepdims=True))
        rows.append(jnp.sum(own * own, axis=0, keepdims=True))
    rows.extend([jnp.zeros((1, channels), F32)] * (-len(rows) % 8))
    sums = group_sums(jnp.concatenate(rows, axis=0), same_group(channels))
    sums = sums * (1.0 / (cols * unit * (channels // GROUPS)))
    normed = []
    for item in range(streams):
        mean = sums[2 * item : 2 * item + 1]
        inverse = lax.rsqrt(sums[2 * item + 1 : 2 * item + 2] - mean * mean + EPS)
        scaled = (values[:, item : item + 1] - mean) * inverse * gain_ref[...]
        normed.append(scaled + shift_ref[...])
    act = silu(jnp.concatenate(normed, axis=1).reshape(size, channels))
    total = conv3(act, weight_ref, taps_ref, block, frames)
    return (state + total + bias_ref[...]).astype(BF16)


def write_output(out_ref, state, first, block, frames):
    streams, unit = block
    channels = state.shape[1]
    cols = state.shape[0] // (streams * unit)
    values = state.astype(F32).reshape(cols, streams, unit, channels)
    for item in range(streams):
        wide = jnp.concatenate([values[col, item] for col in range(cols)], axis=1)
        wide = wide.astype(BF16).reshape(unit // frames, frames, cols * channels)
        out_ref[first + item] = wide


def place_kernel(slab, owned, frames, clips_ref, offsets_ref, table_ref, bias_ref, kept_ref, out_ref):
    del kept_ref
    streams, unit, _ = out_ref.shape
    first = lax.axis_index(slab) * owned
    table_rows = table_ref.shape[1]
    row = lax.broadcasted_iota(jnp.int32, (unit, table_rows), 0)
    row = lax.div(row, jnp.int32(frames))
    wanted = lax.broadcasted_iota(jnp.int32, (unit, table_rows), 1) - row
    for stream in range(streams):
        micro = stream // owned
        offset = offsets_ref[micro, clips_ref[micro, first + stream % owned]]
        hot = jnp.where(wanted == offset, 1.0, 0.0).astype(BF16)
        out_ref[stream] = dot_last(hot, table_ref[...]) + bias_ref[...]


def first_kernel(block, frames, count, chunk, section_axis, *refs):
    streams, unit = block
    latent_refs = refs[:count]
    place_ref, in_weight_ref, *operands = refs[count:-3]
    state_ref, out_ref, taps_ref = refs[-3:]

    @pl.when(lax.axis_index(section_axis) == 0)
    def _():
        size, width = state_ref.shape
        cols = size // (streams * unit)
        parts = []
        for col in range(cols):
            for ref in latent_refs:
                for item in range(ref.shape[0]):
                    parts.append(ref[item, pl.ds(col * unit, unit), :].astype(F32))
        total = conv3_narrow(jnp.concatenate(parts, axis=0), in_weight_ref[...], block, frames)
        placed = place_ref[pl.ds(chunk * streams, streams)].reshape(1, streams * unit, width)
        total = (total.reshape(cols, streams * unit, width) + placed).reshape(size, width)
        state = total.astype(BF16).astype(F32)
        state = unet_layer(state, operands, taps_ref, block, frames)
        state_ref[...] = state
        write_output(out_ref, state, 0, block, frames)


def later_kernel(
    stage_index, block, frames, section_axis,
    before_ref, out_in_ref, weight_ref, gain_ref, shift_ref, bias_ref, state_ref, out_ref, taps_ref,
):
    del out_in_ref

    @pl.when(lax.axis_index(section_axis) == stage_index)
    def _():
        state = unet_layer(
            before_ref[...].astype(F32), (weight_ref, gain_ref, shift_ref, bias_ref), taps_ref, block, frames
        )
        state_ref[...] = state
        write_output(out_ref, state, 0, block, frames)


def last_kernel(block, frames, section_axis, chunks, *refs):
    streams = block[0]
    before_ref = refs[0]
    parts = refs[1 : 1 + chunks]
    operands = refs[1 + chunks : -2]
    out_ref, taps_ref = refs[-2:]
    last = lax.axis_index(section_axis) == lax.axis_size(section_axis) - 1
    for chunk in range(chunks - 1):
        out_ref[pl.ds(chunk * streams, streams)] = parts[chunk][...]

    @pl.when(last)
    def _():
        state = unet_layer(before_ref[...].astype(F32), operands, taps_ref, block, frames)
        write_output(out_ref, state, (chunks - 1) * streams, block, frames)

    @pl.when(jnp.logical_not(last))
    def _():
        out_ref[pl.ds((chunks - 1) * streams, streams)] = parts[chunks - 1][...]


def select_kernel(section_axis, clips_ref, features_ref, out_ref):
    section = lax.axis_index(section_axis)
    for slot in range(out_ref.shape[0]):
        out_ref[slot] = features_ref[clips_ref[section, slot]]


def hop(value, source, target):
    count = lax.axis_size("section")
    if count & (count - 1):
        return lax.ppermute(value, "section", [(source, target)])
    return lax.ppermute(value, "section", [(s, s ^ source ^ target) for s in range(count)])


def gather_first(value):
    count = lax.axis_size("section")
    if count & (count - 1):
        return [value] + [hop(value, other, 0) for other in range(1, count)]
    parts = [value]
    step = 1
    while step < count:
        held = parts[0] if len(parts) == 1 else jnp.concatenate(parts, axis=0)
        parts.append(lax.ppermute(held, "section", [(s, s ^ step) for s in range(count)]))
        step *= 2
    return parts


def per_device(
    features, vae_weight, vae_gain, vae_shift, vae_bias, latent_weight, latent_bias, slot_clips, row_offsets,
    in_weight, in_bias, pos_table, unet_gain, unet_shift, unet_weight, unet_bias,
):
    section_count = lax.axis_size("section")
    slab_count = lax.axis_size("slab")
    _, clip_total, slab_rows, frames, cols, channels = features.shape
    owned = clip_total // slab_count
    row_total = slab_rows * slab_count
    width = unet_weight.shape[-1]
    lat_rows, lat_cols = row_total // 2, cols // 2
    unit = lat_rows * frames

    ordered = pl.pallas_call(
        functools.partial(select_kernel, "section"),
        out_shape=jax.ShapeDtypeStruct(features.shape[1:], BF16),
        in_specs=[smem(), vmem()],
        out_specs=vmem(),
        name="select",
    )(slot_clips, features[0])
    shaped = ordered.reshape(slab_count, owned, slab_rows, frames, cols, channels)
    whole = lax.all_to_all(shaped, "slab", split_axis=0, concat_axis=0)
    whole = jnp.swapaxes(whole, 0, 1).reshape(owned, row_total, frames, cols, channels)
    place = pl.pallas_call(
        functools.partial(place_kernel, "slab", owned, frames),
        out_shape=jax.ShapeDtypeStruct((section_count * owned, unit, width), F32),
        in_specs=[smem()] * 2 + [vmem()] * 2 + [pl.BlockSpec(memory_space=pl.ANY)],
        out_specs=vmem(),
        compiler_params=params(PLACE_VMEM),
        cost_estimate=pl.CostEstimate(flops=PLACE_FLOPS, bytes_accessed=0, transcendentals=0),
        name="place",
    )(slot_clips, row_offsets, pos_table.T, in_bias.reshape(1, -1), vae_weight)
    latent = encode(
        whole, vae_weight, vae_gain.reshape(1, -1), vae_shift.reshape(1, -1), vae_bias.reshape(1, -1),
        latent_weight.T, latent_bias.reshape(1, -1), place,
    )
    latents = gather_first(latent)

    chunks = 2 if section_count % 2 == 0 else 1
    per_chunk = section_count // chunks
    streams = per_chunk * owned
    block = (streams, unit)
    size = lat_cols * streams * unit
    taps = pltpu.VMEM((3, size + 2 * streams * unit, width), BF16)
    layer = [unet_weight[0], unet_gain, unet_shift, unet_bias]
    result_shapes = [
        jax.ShapeDtypeStruct((size, width), BF16),
        jax.ShapeDtypeStruct((streams, lat_rows, frames, lat_cols * width), BF16),
    ]
    arrived = [None] * chunks
    outs = [None] * chunks
    for chunk in range(chunks):
        mine = latents
        if chunks == 2:
            mine = latents[-1:] if chunk else latents[:-1]
        operands = mine + [place, in_weight.reshape(-1, width)] + layer
        state, outs[chunk] = pl.pallas_call(
            functools.partial(first_kernel, block, frames, len(mine), chunk, "section"),
            out_shape=result_shapes,
            in_specs=[vmem()] * len(operands),
            out_specs=[vmem()] * 2,
            scratch_shapes=[taps],
            compiler_params=params(),
            name="first_block",
        )(*operands)
        if section_count > 1:
            arrived[chunk] = hop(state, 0, 1)
    for index in range(1, section_count):
        for chunk in range(chunks):
            if index == section_count - 1 and chunk == chunks - 1:
                break
            state, outs[chunk] = pl.pallas_call(
                functools.partial(later_kernel, index, block, frames, "section"),
                out_shape=result_shapes,
                in_specs=[vmem()] * 6,
                out_specs=[vmem()] * 2,
                scratch_shapes=[taps],
                input_output_aliases={1: 1},
                compiler_params=params(),
                name="later_block",
            )(arrived[chunk], outs[chunk], *layer)
            if index < section_count - 1:
                arrived[chunk] = hop(state, index, index + 1)
    operands = [arrived[-1]] + outs + layer
    out = pl.pallas_call(
        functools.partial(last_kernel, block, frames, "section", chunks),
        out_shape=jax.ShapeDtypeStruct(
            (section_count * owned, lat_rows, frames, lat_cols * width), BF16
        ),
        in_specs=[vmem()] * len(operands),
        out_specs=vmem(),
        scratch_shapes=[taps],
        compiler_params=params(),
        name="last_block",
    )(*operands)
    return out.reshape(1, section_count, owned, lat_rows, frames, lat_cols * width)


def solution(mesh):
    return jax.shard_map(
        per_device,
        mesh=mesh,
        in_specs=(
            P("section", None, "slab", None, None, None),
            P(),
            P(),
            P(),
            P(),
            P(),
            P(),
            P(),
            P(),
            P(),
            P(),
            P(),
            P("section", None),
            P("section", None),
            P("section", None, None, None, None),
            P("section", None),
        ),
        out_specs=P("section", None, "slab", None, None, None),
        check_vma=False,
    )
```

```python
import functools

import jax
import jax.numpy as jnp
from jax import lax
from jax.experimental import pallas as pl
from jax.experimental.pallas import tpu as pltpu
from jax.sharding import PartitionSpec as P

GROUPS = 32
LANES = 128
EPS = 1e-06
VMEM_LIMIT = 32 * 1024 * 1024
GROUPS_VMEM = 4 * 1024 * 1024
GROUPS_FLOPS = 12_000_000_000
F32 = jnp.float32
BF16 = jnp.bfloat16


def vmem():
    return pl.BlockSpec(memory_space=pltpu.VMEM)


def smem():
    return pl.BlockSpec(memory_space=pltpu.SMEM)


def params(limit=VMEM_LIMIT):
    return pltpu.CompilerParams(vmem_limit_bytes=limit)


def same_group(channels):
    size = channels // GROUPS

    def group_of(axis):
        index = lax.broadcasted_iota(jnp.int32, (channels, channels), axis).astype(F32)
        return jnp.floor((index + 0.5) * (1.0 / size))

    return jnp.where(group_of(0) == group_of(1), 1.0, 0.0).astype(BF16)


def groups_kernel(after_ref, *out_refs):
    del after_ref
    for out_ref in out_refs:
        out_ref[...] = same_group(out_ref.shape[0])


def group_sums(rows, same):
    high = rows.astype(BF16)
    rest = rows - high.astype(F32)
    middle = rest.astype(BF16)
    low = (rest - middle.astype(F32)).astype(BF16)
    total = jnp.dot(high, same, preferred_element_type=F32)
    total += jnp.dot(middle, same, preferred_element_type=F32)
    total += jnp.dot(low, same, preferred_element_type=F32)
    return total


def dot_last(left, right):
    return lax.dot_general(left, right, (((1,), (1,)), ((), ())), preferred_element_type=F32)


def silu(value):
    return value / (1.0 + jnp.exp(-value))


def encode_kernel(
    slab_axis, *refs
):
    (
        weight_ref, gain_ref, shift_ref, bias_ref, lat_weight_ref, lat_bias_ref, same_ref,
        out_ref, dup_ref, act_ref, pool_ref, x_ref,
    ) = refs[-12:]
    slab_rows = refs[0].shape[2]
    for step, piece_ref in enumerate(refs[:-12]):
        for half in range(2):
            source = lax.axis_index(slab_axis) ^ (2 * step + half)
            x_ref[:, pl.ds(source * slab_rows, slab_rows)] = piece_ref[half]
    row_count, frames, cols, channels = x_ref.shape[1:]
    plane = frames * cols
    size = row_count * plane
    lat_rows, lat_cols = row_count // 2, cols // 2
    same = same_ref[...]
    for item in range(x_ref.shape[0]):
        x = x_ref[item].astype(F32).reshape(size, channels)
        sums = jnp.concatenate(
            [jnp.sum(x, axis=0, keepdims=True), jnp.sum(x * x, axis=0, keepdims=True)]
            + [jnp.zeros((6, channels), F32)],
            axis=0,
        )
        sums = group_sums(sums, same) * (1.0 / (size * (channels // GROUPS)))
        mean = sums[0:1]
        inverse = lax.rsqrt(sums[1:2] - mean * mean + EPS)
        act = silu((x - mean) * inverse * gain_ref[...] + shift_ref[...])
        column = lax.broadcasted_iota(jnp.int32, (size, 1), 0) & (cols - 1)
        for tap in range(3):
            if tap == 0:
                moved = jnp.where(column == 0, 0.0, pltpu.roll(act, 1, 0))
            elif tap == 2:
                moved = jnp.where(column == cols - 1, 0.0, pltpu.roll(act, size - 1, 0))
            else:
                moved = act
            lanes = pl.ds(tap * channels, channels)
            first = moved.reshape(row_count, frames, cols, channels)[:, 0:1]
            first = jnp.broadcast_to(first, (row_count, frames, cols, channels))
            act_ref[pl.ds(plane, size), lanes] = moved.astype(BF16)
            dup_ref[pl.ds(plane, size), lanes] = first.reshape(size, channels).astype(BF16)
        for ref in (act_ref, dup_ref):
            ref[pl.ds(0, plane), :] = jnp.zeros((plane, 3 * channels), BF16)
            ref[pl.ds(plane + size, plane), :] = jnp.zeros((plane, 3 * channels), BF16)
        total = x + bias_ref[...]
        for time_tap in range(3):
            source = act_ref if time_tap == 2 else dup_ref
            for row_tap in range(3):
                weight = weight_ref[time_tap, row_tap].reshape(3 * channels, channels)
                window = source[pl.ds(row_tap * plane, size), :]
                total += jnp.dot(window, weight, preferred_element_type=F32)
        paired = total.reshape(lat_rows, 2, plane, channels)
        merged = (paired[:, 0] + paired[:, 1]).reshape(lat_rows * plane, channels)
        halves = []
        for part in range(channels // LANES):
            pool_ref[part] = merged[:, part * LANES : (part + 1) * LANES]
            picked = []
            for col in range(lat_cols):
                left = pool_ref[part, pl.ds(2 * col, lat_rows * frames, stride=cols), :]
                right = pool_ref[part, pl.ds(2 * col + 1, lat_rows * frames, stride=cols), :]
                picked.append((left + right) * 0.25)
            halves.append(jnp.concatenate(picked, axis=0))
        pooled = jnp.concatenate(halves, axis=1).astype(BF16)
        latent = dot_last(pooled, lat_weight_ref[...])
        out_ref[item] = (latent + lat_bias_ref[...]).astype(BF16)


def encode(pieces, *operands):
    _, items, slab_rows, frames, cols, channels = pieces[0].shape
    row_count = 2 * len(pieces) * slab_rows
    plane = frames * cols
    lat_rows, lat_cols = row_count // 2, cols // 2
    padded = pltpu.VMEM(((row_count + 2) * plane, 3 * channels), BF16)
    return pl.pallas_call(
        functools.partial(encode_kernel, "slab"),
        out_shape=jax.ShapeDtypeStruct((items, lat_cols * lat_rows * frames, operands[-2].shape[1]), BF16),
        in_specs=[vmem()] * (len(pieces) + len(operands)),
        out_specs=vmem(),
        scratch_shapes=[
            padded,
            padded,
            pltpu.VMEM((channels // LANES, lat_rows * plane, LANES), F32),
            pltpu.VMEM((items, row_count, frames, cols, channels), BF16),
        ],
        compiler_params=params(),
        name="encode",
    )(*pieces, *operands)


def shifted(value, unit, frames):
    size = value.shape[0]
    place = lax.broadcasted_iota(jnp.int32, (size, 1), 0) & (unit - 1)
    return (
        jnp.where(place < frames, 0.0, pltpu.roll(value, frames, 0)),
        value,
        jnp.where(place >= unit - frames, 0.0, pltpu.roll(value, size - frames, 0)),
    )


def conv3(value, weight_ref, taps_ref, block, frames):
    streams, unit = block
    size, channels = value.shape
    edge = streams * unit
    zeros = jnp.zeros((edge, channels), BF16)
    total = None
    for row_tap, moved in enumerate(shifted(value, unit, frames)):
        taps_ref[row_tap, pl.ds(edge, size), :] = moved.astype(BF16)
        taps_ref[row_tap, pl.ds(0, edge), :] = zeros
        taps_ref[row_tap, pl.ds(edge + size, edge), :] = zeros
        for col_tap in range(3):
            window = taps_ref[row_tap, pl.ds(col_tap * edge, size), :]
            term = jnp.dot(window, weight_ref[row_tap, col_tap], preferred_element_type=F32)
            total = term if total is None else total + term
    return total


def conv3_narrow(value, weight, block, frames):
    streams, unit = block
    size, channels = value.shape
    edge = streams * unit
    zeros = jnp.zeros((edge, channels), F32)
    windows = []
    for moved in shifted(value, unit, frames):
        padded = jnp.concatenate([zeros, moved, zeros], axis=0)
        for col_tap in range(3):
            windows.append(padded[col_tap * edge : col_tap * edge + size])
    window = jnp.concatenate(windows, axis=1).astype(BF16)
    return jnp.dot(window, weight, preferred_element_type=F32)


def unet_layer(state, operands, taps_ref, block, frames):
    weight_ref, gain_ref, shift_ref, bias_ref, same_ref = operands
    streams, unit = block
    size, channels = state.shape
    cols = size // (streams * unit)
    values = state.reshape(cols, streams, unit, channels)
    rows = []
    for item in range(streams):
        own = values[:, item].reshape(cols * unit, channels)
        rows.append(jnp.sum(own, axis=0, keepdims=True))
        rows.append(jnp.sum(own * own, axis=0, keepdims=True))
    rows.extend([jnp.zeros((1, channels), F32)] * (-len(rows) % 8))
    sums = group_sums(jnp.concatenate(rows, axis=0), same_ref[...])
    sums = sums * (1.0 / (cols * unit * (channels // GROUPS)))
    normed = []
    for item in range(streams):
        mean = sums[2 * item : 2 * item + 1]
        inverse = lax.rsqrt(sums[2 * item + 1 : 2 * item + 2] - mean * mean + EPS)
        scaled = (values[:, item : item + 1] - mean) * inverse * gain_ref[...]
        normed.append(scaled + shift_ref[...])
    act = silu(jnp.concatenate(normed, axis=1).reshape(size, channels))
    total = conv3(act, weight_ref, taps_ref, block, frames)
    return (state + total + bias_ref[...]).astype(BF16)


def write_output(out_ref, state, first, block, frames):
    streams, unit = block
    channels = state.shape[1]
    cols = state.shape[0] // (streams * unit)
    values = state.astype(F32).reshape(cols, streams, unit, channels)
    for item in range(streams):
        wide = jnp.concatenate([values[col, item] for col in range(cols)], axis=1)
        wide = wide.astype(BF16).reshape(unit // frames, frames, cols * channels)
        out_ref[first + item] = wide


def place_rows(clips_ref, offsets_ref, table, bias, out_ref, slab, owned, frames):
    streams, unit, _ = out_ref.shape
    table_rows = table.shape[1]
    row = lax.div(lax.broadcasted_iota(jnp.int32, (unit, table_rows), 0), jnp.int32(frames))
    wanted = lax.broadcasted_iota(jnp.int32, (unit, table_rows), 1) - row
    for stream in range(streams):
        micro = stream // owned
        offset = offsets_ref[micro, clips_ref[micro, slab * owned + stream % owned]]
        hot = jnp.where(wanted == offset, 1.0, 0.0).astype(BF16)
        out_ref[stream] = dot_last(hot, table) + bias


def first_kernel(block, frames, count, chunk, *refs):
    streams, unit = block
    latent_refs = refs[:count]
    place_ref, in_weight_ref, *operands = refs[count:-3]
    state_ref, out_ref, taps_ref = refs[-3:]

    @pl.when(lax.axis_index("section") == 0)
    def _():
        size, width = state_ref.shape
        cols = size // (streams * unit)
        parts = []
        for col in range(cols):
            for ref in latent_refs:
                for item in range(ref.shape[0]):
                    parts.append(ref[item, pl.ds(col * unit, unit), :].astype(F32))
        total = conv3_narrow(jnp.concatenate(parts, axis=0), in_weight_ref[...], block, frames)
        placed = place_ref[pl.ds(chunk * streams, streams)]
        placed = placed.reshape(1, streams * unit, width)
        total = (total.reshape(cols, streams * unit, width) + placed).reshape(size, width)
        state = total.astype(BF16).astype(F32)
        state = unet_layer(state, operands, taps_ref, block, frames)
        state_ref[...] = state
        write_output(out_ref, state, 0, block, frames)


def later_kernel(
    stage_index, block, frames, section_axis,
    before_ref, out_in_ref, *refs
):
    del out_in_ref
    *operands, state_ref, out_ref, taps_ref = refs

    @pl.when(lax.axis_index(section_axis) == stage_index)
    def _():
        state = unet_layer(
            before_ref[...].astype(F32), operands, taps_ref, block, frames
        )
        state_ref[...] = state
        write_output(out_ref, state, 0, block, frames)


def last_kernel(block, frames, section_axis, chunks, *refs):
    streams = block[0]
    before_ref = refs[0]
    parts = refs[1 : 1 + chunks]
    operands = refs[1 + chunks : -2]
    out_ref, taps_ref = refs[-2:]
    last = lax.axis_index(section_axis) == lax.axis_size(section_axis) - 1
    for chunk in range(chunks - 1):
        out_ref[pl.ds(chunk * streams, streams)] = parts[chunk][...]

    @pl.when(last)
    def _():
        state = unet_layer(before_ref[...].astype(F32), operands, taps_ref, block, frames)
        write_output(out_ref, state, (chunks - 1) * streams, block, frames)

    @pl.when(jnp.logical_not(last))
    def _():
        out_ref[pl.ds((chunks - 1) * streams, streams)] = parts[chunks - 1][...]


def select_kernel(
    section_axis, slab_axis, owned,
    clips_ref, offsets_ref, features_ref, table_ref, bias_ref, keep_ref, give_ref, place_ref,
):
    section = lax.axis_index(section_axis)
    slab = lax.axis_index(slab_axis)
    for step in range(keep_ref.shape[0]):
        for half, out_ref in enumerate((keep_ref, give_ref)):
            for item in range(owned):
                slot = (slab ^ (2 * step + half)) * owned + item
                out_ref[step, item] = features_ref[clips_ref[section, slot]]
    bias = bias_ref[...].reshape(1, -1)
    frames = features_ref.shape[2]
    place_rows(clips_ref, offsets_ref, table_ref[...], bias, place_ref, slab, owned, frames)


def exchange(features, slot_clips, row_offsets, table, bias, place_shape, slab_count, owned):
    steps = slab_count // 2
    shape = jax.ShapeDtypeStruct((steps, owned) + features.shape[1:], BF16)
    keep, give, place = pl.pallas_call(
        functools.partial(select_kernel, "section", "slab", owned),
        out_shape=[shape, shape, jax.ShapeDtypeStruct(place_shape, F32)],
        in_specs=[smem()] * 2 + [vmem()] * 3,
        out_specs=[vmem()] * 3,
        name="select",
    )(slot_clips, row_offsets, features, table, bias)
    got = lax.ppermute(give, "slab", [(slab, slab ^ 1) for slab in range(slab_count)])
    pieces = [jnp.stack([keep[step], got[step]]) for step in range(steps)]
    for step in range(1, steps):
        pairs = [(slab, slab ^ (2 * step)) for slab in range(slab_count)]
        pieces[step] = lax.ppermute(pieces[step], "slab", pairs)
    return pieces, got, place


CYCLES = {
    (0, 1): ((0, 1), (1, 3), (3, 2), (2, 0)),
    (1, 2): ((1, 2), (2, 0), (0, 3), (3, 1)),
    (2, 3): ((2, 3),),
}


def hop(value, source, target):
    count = lax.axis_size("section")
    if count == 4 and (source, target) in CYCLES:
        return lax.ppermute(value, "section", list(CYCLES[source, target]))
    if count & (count - 1):
        return lax.ppermute(value, "section", [(source, target)])
    return lax.ppermute(value, "section", [(s, s ^ source ^ target) for s in range(count)])


def gather_first(value):
    count = lax.axis_size("section")
    if count & (count - 1):
        return [value] + [hop(value, other, 0) for other in range(1, count)]
    parts = [value]
    step = 1
    while step < count:
        held = parts[0] if len(parts) == 1 else jnp.concatenate(parts, axis=0)
        parts.append(lax.ppermute(held, "section", [(s, s ^ step) for s in range(count)]))
        step *= 2
    return parts


def per_device(
    features, vae_weight, vae_gain, vae_shift, vae_bias, latent_weight, latent_bias, slot_clips, row_offsets,
    in_weight, in_bias, pos_table, unet_gain, unet_shift, unet_weight, unet_bias,
):
    section_count = lax.axis_size("section")
    slab_count = lax.axis_size("slab")
    _, clip_total, slab_rows, frames, cols, channels = features.shape
    owned = clip_total // slab_count
    row_total = slab_rows * slab_count
    width = unet_weight.shape[-1]
    lat_rows, lat_cols = row_total // 2, cols // 2
    unit = lat_rows * frames

    place_shape = (section_count * owned, unit, width)
    pieces, got, place = exchange(
        features[0], slot_clips, row_offsets, pos_table.T, in_bias, place_shape, slab_count, owned
    )
    vae_same, unet_same = pl.pallas_call(
        groups_kernel,
        out_shape=[jax.ShapeDtypeStruct((size, size), BF16) for size in (channels, width)],
        in_specs=[pl.BlockSpec(memory_space=pl.ANY)],
        out_specs=[vmem()] * 2,
        compiler_params=params(GROUPS_VMEM),
        cost_estimate=pl.CostEstimate(flops=GROUPS_FLOPS, bytes_accessed=0, transcendentals=0),
        name="groups",
    )(got)
    latent = encode(
        pieces, vae_weight, vae_gain.reshape(1, -1), vae_shift.reshape(1, -1), vae_bias.reshape(1, -1),
        latent_weight.T, latent_bias.reshape(1, -1), vae_same,
    )
    latents = gather_first(latent)

    chunks = 2 if section_count % 2 == 0 else 1
    per_chunk = section_count // chunks
    streams = per_chunk * owned
    block = (streams, unit)
    size = lat_cols * streams * unit
    taps = pltpu.VMEM((3, size + 2 * streams * unit, width), BF16)
    layer = [unet_weight[0], unet_gain, unet_shift, unet_bias, unet_same]
    result_shapes = [
        jax.ShapeDtypeStruct((size, width), BF16),
        jax.ShapeDtypeStruct((streams, lat_rows, frames, lat_cols * width), BF16),
    ]
    arrived = [None] * chunks
    outs = [None] * chunks
    for chunk in range(chunks):
        mine = latents
        if chunks == 2:
            mine = latents[-1:] if chunk else latents[:-1]
        operands = mine + [place, in_weight.reshape(-1, width)] + layer
        state, outs[chunk] = pl.pallas_call(
            functools.partial(first_kernel, block, frames, len(mine), chunk),
            out_shape=result_shapes,
            in_specs=[vmem()] * len(operands),
            out_specs=[vmem()] * 2,
            scratch_shapes=[taps],
            compiler_params=params(),
            name="first_block",
        )(*operands)
        if section_count > 1:
            arrived[chunk] = hop(state, 0, 1)
    for index in range(1, section_count):
        for chunk in range(chunks):
            if index == section_count - 1 and chunk == chunks - 1:
                break
            state, outs[chunk] = pl.pallas_call(
                functools.partial(later_kernel, index, block, frames, "section"),
                out_shape=result_shapes,
                in_specs=[vmem()] * (2 + len(layer)),
                out_specs=[vmem()] * 2,
                scratch_shapes=[taps],
                input_output_aliases={1: 1},
                compiler_params=params(),
                name="later_block",
            )(arrived[chunk], outs[chunk], *layer)
            if index < section_count - 1:
                arrived[chunk] = hop(state, index, index + 1)
    operands = [arrived[-1]] + outs + layer
    out = pl.pallas_call(
        functools.partial(last_kernel, block, frames, "section", chunks),
        out_shape=jax.ShapeDtypeStruct(
            (section_count * owned, lat_rows, frames, lat_cols * width), BF16
        ),
        in_specs=[vmem()] * len(operands),
        out_specs=vmem(),
        scratch_shapes=[taps],
        compiler_params=params(),
        name="last_block",
    )(*operands)
    return out.reshape(1, section_count, owned, lat_rows, frames, lat_cols * width)


def solution(mesh):
    return jax.shard_map(
        per_device,
        mesh=mesh,
        in_specs=(
            P("section", None, "slab", None, None, None),
            P(),
            P(),
            P(),
            P(),
            P(),
            P(),
            P(),
            P(),
            P(),
            P(),
            P(),
            P("section", None),
            P("section", None),
            P("section", None, None, None, None),
            P("section", None),
        ),
        out_specs=P("section", None, "slab", None, None, None),
        check_vma=False,
    )
```

```python
import functools

import jax
import jax.numpy as jnp
from jax import lax
from jax.experimental import pallas as pl
from jax.experimental.pallas import tpu as pltpu
from jax.sharding import PartitionSpec as P

GROUPS = 32
LANES = 128
EPS = 1e-06
VMEM_LIMIT = 32 * 1024 * 1024
GROUPS_VMEM = 4 * 1024 * 1024
GROUPS_FLOPS = 12_000_000_000
F32 = jnp.float32
BF16 = jnp.bfloat16


def vmem():
    return pl.BlockSpec(memory_space=pltpu.VMEM)


def smem():
    return pl.BlockSpec(memory_space=pltpu.SMEM)


def params(limit=VMEM_LIMIT):
    return pltpu.CompilerParams(vmem_limit_bytes=limit)


def same_group(channels):
    size = channels // GROUPS

    def group_of(axis):
        index = lax.broadcasted_iota(jnp.int32, (channels, channels), axis).astype(F32)
        return jnp.floor((index + 0.5) * (1.0 / size))

    return jnp.where(group_of(0) == group_of(1), 1.0, 0.0).astype(BF16)


def groups_kernel(after_ref, *out_refs):
    del after_ref
    for out_ref in out_refs:
        out_ref[...] = same_group(out_ref.shape[0])


def group_sums(rows, same):
    high = rows.astype(BF16)
    rest = rows - high.astype(F32)
    middle = rest.astype(BF16)
    low = (rest - middle.astype(F32)).astype(BF16)
    total = jnp.dot(high, same, preferred_element_type=F32)
    total += jnp.dot(middle, same, preferred_element_type=F32)
    total += jnp.dot(low, same, preferred_element_type=F32)
    return total


def dot_last(left, right):
    return lax.dot_general(left, right, (((1,), (1,)), ((), ())), preferred_element_type=F32)


def silu(value):
    return 0.5 * value * (1.0 + jnp.tanh(0.5 * value))


def encode_kernel(slab_axis, *refs):
    (
        weight_ref, gain_ref, shift_ref, bias_ref, lat_weight_ref, lat_bias_ref, same_ref,
        out_ref, x_ref, pool_ref,
    ) = refs[-10:]
    pieces = refs[:-10]
    slab_rows = pieces[0].shape[2]
    items, frames, row_count, cols, channels = x_ref.shape
    for step, piece_ref in enumerate(pieces[::-1]):
        for half in range(2):
            source = lax.axis_index(slab_axis) ^ (2 * step + half)
            for item in range(items):
                for frame in range(frames):
                    piece = piece_ref[half, item, :, frame].astype(F32)
                    x_ref[item, frame, pl.ds(source * slab_rows, slab_rows)] = piece
    size = frames * row_count * cols
    plane = row_count * cols
    lat_rows, lat_cols = row_count // 2, cols // 2
    for item in range(items):
        x = x_ref[item].reshape(size, channels)
        sums = jnp.concatenate(
            [jnp.sum(x, axis=0, keepdims=True), jnp.sum(x * x, axis=0, keepdims=True)]
            + [jnp.zeros((6, channels), F32)],
            axis=0,
        )
        sums = group_sums(sums, same_ref[...]) * (1.0 / (size * (channels // GROUPS)))
        mean = sums[0:1]
        inverse = lax.rsqrt(sums[1:2] - mean * mean + EPS)
        act = silu((x - mean) * inverse * gain_ref[...] + shift_ref[...])
        column = lax.broadcasted_iota(jnp.int32, (size, 1), 0) & (cols - 1)
        taps = [
            jnp.where(column == 0, 0.0, pltpu.roll(act, 1, 0)),
            act,
            jnp.where(column == cols - 1, 0.0, pltpu.roll(act, size - 1, 0)),
        ]
        wide = jnp.concatenate(taps, axis=1).reshape(frames, row_count, cols, 3 * channels)
        edge = jnp.zeros((frames, 1, cols, 3 * channels), F32)
        wide = jnp.concatenate([edge, wide, edge], axis=1)
        total, still = x + bias_ref[...], None
        for row_tap in range(3):
            window = wide[:, row_tap : row_tap + row_count].reshape(size, 3 * channels).astype(BF16)
            weights = [weight_ref[time, row_tap].reshape(3 * channels, channels) for time in range(3)]
            total += jnp.dot(window, weights[2], preferred_element_type=F32)
            for weight in weights[:2]:
                term = jnp.dot(window[:plane], weight, preferred_element_type=F32)
                still = term if still is None else still + term
        paired = total.reshape(frames, lat_rows, 2, cols, channels)
        paired = paired + still.reshape(1, lat_rows, 2, cols, channels)
        merged = paired[:, :, 0] + paired[:, :, 1]
        halves = []
        for part in range(channels // LANES):
            for row in range(lat_rows):
                for frame in range(frames):
                    block = merged[frame, row, :, part * LANES : (part + 1) * LANES]
                    pool_ref[part, pl.ds((row * frames + frame) * cols, cols), :] = block
            picked = []
            for col in range(lat_cols):
                left = pool_ref[part, pl.ds(2 * col, lat_rows * frames, stride=cols), :]
                right = pool_ref[part, pl.ds(2 * col + 1, lat_rows * frames, stride=cols), :]
                picked.append((left + right) * 0.25)
            halves.append(jnp.concatenate(picked, axis=0))
        pooled = jnp.concatenate(halves, axis=1).astype(BF16)
        latent = dot_last(pooled, lat_weight_ref[...])
        out_ref[item] = (latent + lat_bias_ref[...]).astype(BF16)


def encode(pieces, *operands):
    _, items, slab_rows, frames, cols, channels = pieces[0].shape
    row_count = 2 * len(pieces) * slab_rows
    lat_rows, lat_cols = row_count // 2, cols // 2
    return pl.pallas_call(
        functools.partial(encode_kernel, "slab"),
        out_shape=jax.ShapeDtypeStruct((items, lat_cols * lat_rows * frames, operands[-2].shape[1]), BF16),
        in_specs=[vmem()] * (len(pieces) + len(operands)),
        out_specs=vmem(),
        scratch_shapes=[
            pltpu.VMEM((items, frames, row_count, cols, channels), F32),
            pltpu.VMEM((channels // LANES, lat_rows * frames * cols, LANES), F32),
        ],
        compiler_params=params(),
        name="encode",
    )(*pieces[::-1], *operands)


def shifted(value, unit, frames):
    size = value.shape[0]
    place = lax.broadcasted_iota(jnp.int32, (size, 1), 0) & (unit - 1)
    return (
        jnp.where(place < frames, 0.0, pltpu.roll(value, frames, 0)),
        value,
        jnp.where(place >= unit - frames, 0.0, pltpu.roll(value, size - frames, 0)),
    )


def conv3(value, weight_ref, block, frames):
    streams, unit = block
    edge = streams * unit
    wide = jnp.concatenate(shifted(value, unit, frames), axis=1).astype(BF16)
    terms = []
    for col_tap, window in enumerate((wide[:-edge], wide, wide[edge:])):
        weight = jnp.concatenate([weight_ref[row_tap, col_tap] for row_tap in range(3)], axis=0)
        terms.append(jnp.dot(window, weight, preferred_element_type=F32))
    left, total, right = terms
    zeros = jnp.zeros((edge, total.shape[1]), F32)
    return total + jnp.concatenate([zeros, left], axis=0) + jnp.concatenate([right, zeros], axis=0)


def conv3_narrow(value, weight, block, frames):
    streams, unit = block
    size, channels = value.shape
    edge = streams * unit
    zeros = jnp.zeros((edge, channels), F32)
    windows = []
    for moved in shifted(value, unit, frames):
        padded = jnp.concatenate([zeros, moved, zeros], axis=0)
        for col_tap in range(3):
            windows.append(padded[col_tap * edge : col_tap * edge + size])
    window = jnp.concatenate(windows, axis=1).astype(BF16)
    return jnp.dot(window, weight, preferred_element_type=F32)


def unet_layer(state, operands, block, frames):
    weight_ref, gain_ref, shift_ref, bias_ref, same_ref = operands
    streams, unit = block
    size, channels = state.shape
    cols = size // (streams * unit)
    values = state.reshape(cols, streams, unit, channels)
    rows = []
    for item in range(streams):
        own = values[:, item].reshape(cols * unit, channels)
        rows.append(jnp.sum(own, axis=0, keepdims=True))
        rows.append(jnp.sum(own * own, axis=0, keepdims=True))
    rows.extend([jnp.zeros((1, channels), F32)] * (-len(rows) % 8))
    sums = group_sums(jnp.concatenate(rows, axis=0), same_ref[...])
    sums = sums * (1.0 / (cols * unit * (channels // GROUPS)))
    normed = []
    for item in range(streams):
        mean = sums[2 * item : 2 * item + 1]
        inverse = lax.rsqrt(sums[2 * item + 1 : 2 * item + 2] - mean * mean + EPS)
        scaled = (values[:, item : item + 1] - mean) * inverse * gain_ref[...]
        normed.append(scaled + shift_ref[...])
    act = silu(jnp.concatenate(normed, axis=1).reshape(size, channels))
    total = conv3(act, weight_ref, block, frames)
    return (state + total + bias_ref[...]).astype(BF16)


def write_output(out_ref, state, first, block, frames):
    streams, unit = block
    channels = state.shape[1]
    cols = state.shape[0] // (streams * unit)
    values = state.astype(F32).reshape(cols, streams, unit, channels)
    for item in range(streams):
        wide = jnp.concatenate([values[col, item] for col in range(cols)], axis=1)
        wide = wide.astype(BF16).reshape(unit // frames, frames, cols * channels)
        out_ref[first + item] = wide


def place_rows(clips_ref, offsets_ref, table, bias, out_ref, slab, owned, frames):
    streams, unit, _ = out_ref.shape
    table_rows = table.shape[1]
    row = lax.div(lax.broadcasted_iota(jnp.int32, (unit, table_rows), 0), jnp.int32(frames))
    wanted = lax.broadcasted_iota(jnp.int32, (unit, table_rows), 1) - row
    for stream in range(streams):
        micro = stream // owned
        offset = offsets_ref[micro, clips_ref[micro, slab * owned + stream % owned]]
        hot = jnp.where(wanted == offset, 1.0, 0.0).astype(BF16)
        out_ref[stream] = dot_last(hot, table) + bias


def first_kernel(block, frames, count, chunk, *refs):
    streams, unit = block
    latent_refs = refs[:count]
    place_ref, in_weight_ref, *operands = refs[count:-1]
    state_ref = refs[-1]

    @pl.when(lax.axis_index("section") == 0)
    def _():
        size, width = state_ref.shape
        cols = size // (streams * unit)
        parts = []
        for col in range(cols):
            for ref in latent_refs:
                for item in range(ref.shape[0]):
                    parts.append(ref[item, pl.ds(col * unit, unit), :].astype(F32))
        total = conv3_narrow(jnp.concatenate(parts, axis=0), in_weight_ref[...], block, frames)
        placed = place_ref[pl.ds(chunk * streams, streams)]
        placed = placed.reshape(1, streams * unit, width)
        total = (total.reshape(cols, streams * unit, width) + placed).reshape(size, width)
        state = total.astype(BF16).astype(F32)
        state_ref[...] = unet_layer(state, operands, block, frames)


def later_kernel(index, block, frames, before_ref, kept_ref, *refs):
    del kept_ref
    *operands, state_ref = refs

    @pl.when(lax.axis_index("section") == index)
    def _():
        state_ref[...] = unet_layer(before_ref[...].astype(F32), operands, block, frames)


def last_kernel(block, frames, chunk, chunks, before_ref, *refs):
    streams = block[0]
    kept = refs[:chunks] if chunk == 0 else []
    operands = refs[chunks:-4] if chunk == 0 else refs[1:-4]
    out_ref, wide_ref, store_sem, _ = refs[-4:]
    last = lax.axis_index("section") == lax.axis_size("section") - 1

    def store(part, sem):
        rows = pl.ds(part * streams, streams)
        return pltpu.make_async_copy(wide_ref.at[rows], out_ref.at[rows], sem)

    @pl.when(last)
    def _():
        state = unet_layer(before_ref[...].astype(F32), operands, block, frames)
        write_output(wide_ref, state, chunk * streams, block, frames)
        copy = store(chunk, store_sem)
        copy.start()
        copy.wait()

    if chunk == 0:

        @pl.when(jnp.logical_not(last))
        def _():
            for part in range(chunks):
                write_output(wide_ref, kept[part][...], part * streams, block, frames)
                copy = store(part, store_sem)
                copy.start()
                copy.wait()


def select_kernel(
    section_axis, slab_axis, owned,
    clips_ref, offsets_ref, features_ref, table_ref, bias_ref, keep_ref, give_ref, place_ref,
):
    section = lax.axis_index(section_axis)
    slab = lax.axis_index(slab_axis)
    for step in range(keep_ref.shape[0]):
        for half, out_ref in enumerate((keep_ref, give_ref)):
            for item in range(owned):
                slot = (slab ^ (2 * step + half)) * owned + item
                out_ref[step, item] = features_ref[clips_ref[section, slot]]
    bias = bias_ref[...].reshape(1, -1)
    frames = features_ref.shape[2]
    place_rows(clips_ref, offsets_ref, table_ref[...], bias, place_ref, slab, owned, frames)


def exchange(features, slot_clips, row_offsets, table, bias, place_shape, slab_count, owned):
    steps = slab_count // 2
    shape = jax.ShapeDtypeStruct((steps, owned) + features.shape[1:], BF16)
    keep, give, place = pl.pallas_call(
        functools.partial(select_kernel, "section", "slab", owned),
        out_shape=[shape, shape, jax.ShapeDtypeStruct(place_shape, F32)],
        in_specs=[smem()] * 2 + [vmem()] * 3,
        out_specs=[vmem()] * 3,
        name="select",
    )(slot_clips, row_offsets, features, table, bias)
    got = lax.ppermute(give, "slab", [(slab, slab ^ 1) for slab in range(slab_count)])
    pieces = [jnp.stack([keep[step], got[step]]) for step in range(steps)]
    for step in range(1, steps):
        pairs = [(slab, slab ^ (2 * step)) for slab in range(slab_count)]
        pieces[step] = lax.ppermute(pieces[step], "slab", pairs)
    return pieces, got, place


CYCLES = {
    (0, 1): ((0, 1), (1, 3), (3, 2), (2, 0)),
    (1, 2): ((1, 2), (2, 0), (0, 3), (3, 1)),
    (2, 3): ((0, 1), (1, 0), (2, 3), (3, 2)),
}


def hop(value, source, target):
    count = lax.axis_size("section")
    if count == 4 and (source, target) in CYCLES:
        return lax.ppermute(value, "section", list(CYCLES[source, target]))
    if count & (count - 1):
        return lax.ppermute(value, "section", [(source, target)])
    return lax.ppermute(value, "section", [(s, s ^ source ^ target) for s in range(count)])


def gather_first(value):
    count = lax.axis_size("section")
    if count & (count - 1):
        return [value] + [hop(value, other, 0) for other in range(1, count)]
    if count == 4:
        return [value] + [lax.ppermute(value, "section", [(s, s ^ k) for s in range(4)]) for k in (1, 2, 3)]
    parts = [value]
    step = 1
    while step < count:
        held = parts[0] if len(parts) == 1 else jnp.concatenate(parts, axis=0)
        parts.append(lax.ppermute(held, "section", [(s, s ^ step) for s in range(count)]))
        step *= 2
    return parts


def per_device(
    features, vae_weight, vae_gain, vae_shift, vae_bias, latent_weight, latent_bias, slot_clips, row_offsets,
    in_weight, in_bias, pos_table, unet_gain, unet_shift, unet_weight, unet_bias,
):
    section_count = lax.axis_size("section")
    slab_count = lax.axis_size("slab")
    _, clip_total, slab_rows, frames, cols, channels = features.shape
    owned = clip_total // slab_count
    row_total = slab_rows * slab_count
    width = unet_weight.shape[-1]
    lat_rows, lat_cols = row_total // 2, cols // 2
    unit = lat_rows * frames

    place_shape = (section_count * owned, unit, width)
    pieces, got, place = exchange(
        features[0], slot_clips, row_offsets, pos_table.T, in_bias, place_shape, slab_count, owned
    )
    vae_same, unet_same = pl.pallas_call(
        groups_kernel,
        out_shape=[jax.ShapeDtypeStruct((size, size), BF16) for size in (channels, width)],
        in_specs=[pl.BlockSpec(memory_space=pl.ANY)],
        out_specs=[vmem()] * 2,
        compiler_params=params(GROUPS_VMEM),
        cost_estimate=pl.CostEstimate(flops=GROUPS_FLOPS, bytes_accessed=0, transcendentals=0),
        name="groups",
    )(got)
    latent = encode(
        pieces, vae_weight, vae_gain.reshape(1, -1), vae_shift.reshape(1, -1), vae_bias.reshape(1, -1),
        latent_weight.T, latent_bias.reshape(1, -1), vae_same,
    )
    latents = gather_first(latent)

    chunks = 2 if section_count % 2 == 0 else 1
    per_chunk = section_count // chunks
    streams = per_chunk * owned
    block = (streams, unit)
    state_shape = jax.ShapeDtypeStruct((lat_cols * streams * unit, width), BF16)
    layer = [unet_weight[0], unet_gain, unet_shift, unet_bias, unet_same]
    states = [None] * chunks
    arrived = [None] * chunks
    for chunk in range(chunks):
        mine = latents
        if chunks == 2:
            cut = len(latents) // 2 if section_count == 4 else -1
            mine = latents[cut:] if chunk else latents[:cut]
        operands = mine + [place, in_weight.reshape(-1, width)] + layer
        states[chunk] = pl.pallas_call(
            functools.partial(first_kernel, block, frames, len(mine), chunk),
            out_shape=state_shape,
            in_specs=[vmem()] * len(operands),
            out_specs=vmem(),
            compiler_params=params(),
            name="first_block",
        )(*operands)
        arrived[chunk] = hop(states[chunk], 0, 1)
    for index in range(1, section_count - 1):
        for chunk in range(chunks):
            states[chunk] = pl.pallas_call(
                functools.partial(later_kernel, index, block, frames),
                out_shape=state_shape,
                in_specs=[vmem()] * (2 + len(layer)),
                out_specs=vmem(),
                input_output_aliases={1: 0},
                compiler_params=params(),
                name="later_block",
            )(arrived[chunk], states[chunk], *layer)
            arrived[chunk] = hop(states[chunk], index, index + 1)
    hbm = pl.BlockSpec(memory_space=pltpu.HBM)
    out_shape = jax.ShapeDtypeStruct((section_count * owned, lat_rows, frames, lat_cols * width), BF16)
    out = None
    for chunk in range(chunks):
        operands = [arrived[chunk]] + (states if chunk == 0 else [out]) + layer
        specs = [vmem()] * len(operands)
        if chunk:
            specs[1] = hbm
        out = pl.pallas_call(
            functools.partial(last_kernel, block, frames, chunk, chunks),
            out_shape=out_shape,
            in_specs=specs,
            out_specs=hbm,
            scratch_shapes=[
                pltpu.VMEM(out_shape.shape, BF16),
                pltpu.SemaphoreType.DMA,
                pltpu.SemaphoreType.DMA,
            ],
            input_output_aliases={1: 0} if chunk else {},
            compiler_params=params(),
            name="last_block",
        )(*operands)
    return out.reshape(1, section_count, owned, lat_rows, frames, lat_cols * width)


def solution(mesh):
    return jax.shard_map(
        per_device,
        mesh=mesh,
        in_specs=(
            P("section", None, "slab", None, None, None),
            P(),
            P(),
            P(),
            P(),
            P(),
            P(),
            P(),
            P(),
            P(),
            P(),
            P(),
            P("section", None),
            P("section", None),
            P("section", None, None, None, None),
            P("section", None),
        ),
        out_specs=P("section", None, "slab", None, None, None),
        check_vma=False,
    )
```

```python
import functools

import jax
import jax.numpy as jnp
from jax import lax
from jax.experimental import pallas as pl
from jax.experimental.pallas import tpu as pltpu
from jax.sharding import PartitionSpec as P

GROUPS = 32
LANES = 128
EPS = 1e-06
VMEM_LIMIT = 32 * 1024 * 1024
GROUPS_VMEM = 4 * 1024 * 1024
GROUPS_FLOPS = 12_000_000_000
F32 = jnp.float32
BF16 = jnp.bfloat16


def vmem():
    return pl.BlockSpec(memory_space=pltpu.VMEM)


def smem():
    return pl.BlockSpec(memory_space=pltpu.SMEM)


def params(limit=VMEM_LIMIT):
    return pltpu.CompilerParams(vmem_limit_bytes=limit)


def same_group(channels):
    size = channels // GROUPS

    def group_of(axis):
        index = lax.broadcasted_iota(jnp.int32, (channels, channels), axis).astype(F32)
        return jnp.floor((index + 0.5) * (1.0 / size))

    return jnp.where(group_of(0) == group_of(1), 1.0, 0.0).astype(BF16)


def groups_kernel(after_ref, *out_refs):
    del after_ref
    for out_ref in out_refs:
        out_ref[...] = same_group(out_ref.shape[0])


def group_sums(rows, same):
    high = rows.astype(BF16)
    rest = rows - high.astype(F32)
    middle = rest.astype(BF16)
    low = (rest - middle.astype(F32)).astype(BF16)
    total = jnp.dot(high, same, preferred_element_type=F32)
    total += jnp.dot(middle, same, preferred_element_type=F32)
    total += jnp.dot(low, same, preferred_element_type=F32)
    return total


def dot_last(left, right):
    return lax.dot_general(left, right, (((1,), (1,)), ((), ())), preferred_element_type=F32)


def silu(value):
    return 0.5 * value * (1.0 + jnp.tanh(0.5 * value))


def encode_kernel(slab_axis, *refs):
    (
        weight_ref, gain_ref, shift_ref, bias_ref, lat_weight_ref, lat_bias_ref, same_ref,
        out_ref, x_ref, pool_ref,
    ) = refs[-10:]
    pieces = refs[:-10]
    slab_rows = pieces[0].shape[2]
    items, frames, row_count, cols, channels = x_ref.shape
    for step, piece_ref in enumerate(pieces[::-1]):
        for half in range(2):
            source = lax.axis_index(slab_axis) ^ (2 * step + half)
            for item in range(items):
                for frame in range(frames):
                    piece = piece_ref[half, item, :, frame].astype(F32)
                    x_ref[item, frame, pl.ds(source * slab_rows, slab_rows)] = piece
    size = frames * row_count * cols
    plane = row_count * cols
    lat_rows, lat_cols = row_count // 2, cols // 2
    for item in range(items):
        x = x_ref[item].reshape(size, channels)
        sums = jnp.concatenate(
            [jnp.sum(x, axis=0, keepdims=True), jnp.sum(x * x, axis=0, keepdims=True)]
            + [jnp.zeros((6, channels), F32)],
            axis=0,
        )
        sums = group_sums(sums, same_ref[...]) * (1.0 / (size * (channels // GROUPS)))
        mean = sums[0:1]
        inverse = lax.rsqrt(sums[1:2] - mean * mean + EPS)
        act = silu((x - mean) * inverse * gain_ref[...] + shift_ref[...])
        column = lax.broadcasted_iota(jnp.int32, (size, 1), 0) & (cols - 1)
        taps = [
            jnp.where(column == 0, 0.0, pltpu.roll(act, 1, 0)),
            act,
            jnp.where(column == cols - 1, 0.0, pltpu.roll(act, size - 1, 0)),
        ]
        wide = jnp.concatenate(taps, axis=1).reshape(frames, row_count, cols, 3 * channels)
        edge = jnp.zeros((frames, 1, cols, 3 * channels), F32)
        wide = jnp.concatenate([edge, wide, edge], axis=1)
        total, still = x + bias_ref[...], None
        for row_tap in range(3):
            window = wide[:, row_tap : row_tap + row_count].reshape(size, 3 * channels).astype(BF16)
            weights = [weight_ref[time, row_tap].reshape(3 * channels, channels) for time in range(3)]
            total += jnp.dot(window, weights[2], preferred_element_type=F32)
            for weight in weights[:2]:
                term = jnp.dot(window[:plane], weight, preferred_element_type=F32)
                still = term if still is None else still + term
        paired = total.reshape(frames, lat_rows, 2, cols, channels)
        paired = paired + still.reshape(1, lat_rows, 2, cols, channels)
        merged = paired[:, :, 0] + paired[:, :, 1]
        halves = []
        for part in range(channels // LANES):
            for row in range(lat_rows):
                for frame in range(frames):
                    block = merged[frame, row, :, part * LANES : (part + 1) * LANES]
                    pool_ref[part, pl.ds((row * frames + frame) * cols, cols), :] = block
            picked = []
            for col in range(lat_cols):
                left = pool_ref[part, pl.ds(2 * col, lat_rows * frames, stride=cols), :]
                right = pool_ref[part, pl.ds(2 * col + 1, lat_rows * frames, stride=cols), :]
                picked.append((left + right) * 0.25)
            halves.append(jnp.concatenate(picked, axis=0))
        pooled = jnp.concatenate(halves, axis=1).astype(BF16)
        latent = dot_last(pooled, lat_weight_ref[...])
        out_ref[item] = (latent + lat_bias_ref[...]).astype(BF16)


def encode(pieces, *operands):
    _, items, slab_rows, frames, cols, channels = pieces[0].shape
    row_count = 2 * len(pieces) * slab_rows
    lat_rows, lat_cols = row_count // 2, cols // 2
    return pl.pallas_call(
        functools.partial(encode_kernel, "slab"),
        out_shape=jax.ShapeDtypeStruct((items, lat_cols * lat_rows * frames, operands[-2].shape[1]), BF16),
        in_specs=[vmem()] * (len(pieces) + len(operands)),
        out_specs=vmem(),
        scratch_shapes=[
            pltpu.VMEM((items, frames, row_count, cols, channels), F32),
            pltpu.VMEM((channels // LANES, lat_rows * frames * cols, LANES), F32),
        ],
        compiler_params=params(),
        name="encode",
    )(*pieces[::-1], *operands)


def shifted(value, unit, frames):
    size = value.shape[0]
    place = lax.broadcasted_iota(jnp.int32, (size, 1), 0) & (unit - 1)
    return (
        jnp.where(place < frames, 0.0, pltpu.roll(value, frames, 0)),
        value,
        jnp.where(place >= unit - frames, 0.0, pltpu.roll(value, size - frames, 0)),
    )


def conv3(value, weight_ref, block, frames):
    streams, unit = block
    edge = streams * unit
    wide = jnp.concatenate(shifted(value, unit, frames), axis=1).astype(BF16)
    terms = []
    for col_tap, window in enumerate((wide[:-edge], wide, wide[edge:])):
        weight = jnp.concatenate([weight_ref[row_tap, col_tap] for row_tap in range(3)], axis=0)
        terms.append(jnp.dot(window, weight, preferred_element_type=F32))
    left, total, right = terms
    zeros = jnp.zeros((edge, total.shape[1]), F32)
    return total + jnp.concatenate([zeros, left], axis=0) + jnp.concatenate([right, zeros], axis=0)


def conv3_narrow(value, weight, block, frames):
    streams, unit = block
    size, channels = value.shape
    edge = streams * unit
    zeros = jnp.zeros((edge, channels), F32)
    windows = []
    for moved in shifted(value, unit, frames):
        padded = jnp.concatenate([zeros, moved, zeros], axis=0)
        for col_tap in range(3):
            windows.append(padded[col_tap * edge : col_tap * edge + size])
    window = jnp.concatenate(windows, axis=1).astype(BF16)
    return jnp.dot(window, weight, preferred_element_type=F32)


def unet_layer(state, operands, block, frames):
    weight_ref, gain_ref, shift_ref, bias_ref, same_ref = operands
    streams, unit = block
    size, channels = state.shape
    cols = size // (streams * unit)
    values = state.reshape(cols, streams, unit, channels)
    rows = []
    for item in range(streams):
        own = values[:, item].reshape(cols * unit, channels)
        rows.append(jnp.sum(own, axis=0, keepdims=True))
        rows.append(jnp.sum(own * own, axis=0, keepdims=True))
    rows.extend([jnp.zeros((1, channels), F32)] * (-len(rows) % 8))
    sums = group_sums(jnp.concatenate(rows, axis=0), same_ref[...])
    sums = sums * (1.0 / (cols * unit * (channels // GROUPS)))
    normed = []
    for item in range(streams):
        mean = sums[2 * item : 2 * item + 1]
        inverse = lax.rsqrt(sums[2 * item + 1 : 2 * item + 2] - mean * mean + EPS)
        scaled = (values[:, item : item + 1] - mean) * inverse * gain_ref[...]
        normed.append(scaled + shift_ref[...])
    act = silu(jnp.concatenate(normed, axis=1).reshape(size, channels))
    total = conv3(act, weight_ref, block, frames)
    return (state + total + bias_ref[...]).astype(BF16)


def write_output(out_ref, state, first, block, frames):
    streams, unit = block
    channels = state.shape[1]
    cols = state.shape[0] // (streams * unit)
    values = state.astype(F32).reshape(cols, streams, unit, channels)
    for item in range(streams):
        wide = jnp.concatenate([values[col, item] for col in range(cols)], axis=1)
        wide = wide.astype(BF16).reshape(unit // frames, frames, cols * channels)
        out_ref[first + item] = wide


def place_rows(clips_ref, offsets_ref, table, bias, out_ref, slab, owned, frames):
    streams, unit, _ = out_ref.shape
    table_rows = table.shape[1]
    row = lax.div(lax.broadcasted_iota(jnp.int32, (unit, table_rows), 0), jnp.int32(frames))
    wanted = lax.broadcasted_iota(jnp.int32, (unit, table_rows), 1) - row
    for stream in range(streams):
        micro = stream // owned
        offset = offsets_ref[micro, clips_ref[micro, slab * owned + stream % owned]]
        hot = jnp.where(wanted == offset, 1.0, 0.0).astype(BF16)
        out_ref[stream] = dot_last(hot, table) + bias


def first_kernel(block, frames, count, chunk, *refs):
    streams, unit = block
    latent_refs = refs[:count]
    place_ref, in_weight_ref, *operands = refs[count:-1]
    state_ref = refs[-1]

    @pl.when(lax.axis_index("section") == 0)
    def _():
        size, width = state_ref.shape
        cols = size // (streams * unit)
        parts = []
        for col in range(cols):
            for ref in latent_refs:
                for item in range(ref.shape[0]):
                    parts.append(ref[item, pl.ds(col * unit, unit), :].astype(F32))
        total = conv3_narrow(jnp.concatenate(parts, axis=0), in_weight_ref[...], block, frames)
        placed = place_ref[pl.ds(chunk * streams, streams)]
        placed = placed.reshape(1, streams * unit, width)
        total = (total.reshape(cols, streams * unit, width) + placed).reshape(size, width)
        state = total.astype(BF16).astype(F32)
        state_ref[...] = unet_layer(state, operands, block, frames)


def later_kernel(index, block, frames, before_ref, kept_ref, *refs):
    del kept_ref
    *operands, state_ref = refs

    @pl.when(lax.axis_index("section") == index)
    def _():
        state_ref[...] = unet_layer(before_ref[...].astype(F32), operands, block, frames)


def last_kernel(block, frames, chunk, chunks, before_ref, *refs):
    streams = block[0]
    count = 2 * chunks if chunk == 0 else 1
    kept, operands = refs[:count], refs[count:-4]
    out_ref, wide_ref, store_sem, _ = refs[-4:]
    last = lax.axis_index("section") == lax.axis_size("section") - 1

    def store(part, sem):
        rows = pl.ds(part * streams, streams)
        return pltpu.make_async_copy(wide_ref.at[rows], out_ref.at[rows], sem)

    @pl.when(last)
    def _():
        state = unet_layer(before_ref[...].astype(F32), operands, block, frames)
        write_output(wide_ref, state, chunk * streams, block, frames)
        copy = store(chunk, store_sem)
        copy.start()
        copy.wait()

    if chunk == 0:

        @pl.when(jnp.logical_not(last))
        def _():
            early = lax.axis_index("section") < 2
            for part in range(chunks):
                state = jnp.where(early, kept[chunks + part][...].astype(F32), kept[part][...].astype(F32))
                write_output(wide_ref, state, part * streams, block, frames)
                copy = store(part, store_sem)
                copy.start()
                copy.wait()


def select_kernel(
    section_axis, slab_axis, owned, crossed,
    clips_ref, offsets_ref, features_ref, table_ref, bias_ref, keep_ref, give_ref, place_ref,
):
    section = lax.axis_index(section_axis)
    slab = lax.axis_index(slab_axis)
    for step in range(keep_ref.shape[0]):
        for half, out_ref in enumerate((keep_ref, give_ref)):
            for item in range(owned):
                slot = (slab ^ (2 * step + half)) * owned + item
                out_ref[step, item] = features_ref[clips_ref[section, slot]]
    bias = bias_ref[...].reshape(1, -1)
    frames = features_ref.shape[2]
    worker = slab ^ 1 if crossed else slab
    place_rows(clips_ref, offsets_ref, table_ref[...], bias, place_ref, worker, owned, frames)


def exchange(features, slot_clips, row_offsets, table, bias, place_shape, slab_count, owned):
    steps = slab_count // 2
    shape = jax.ShapeDtypeStruct((steps, owned) + features.shape[1:], BF16)
    keep, give, place = pl.pallas_call(
        functools.partial(select_kernel, "section", "slab", owned, crosses()),
        out_shape=[shape, shape, jax.ShapeDtypeStruct(place_shape, F32)],
        in_specs=[smem()] * 2 + [vmem()] * 3,
        out_specs=[vmem()] * 3,
        name="select",
    )(slot_clips, row_offsets, features, table, bias)
    got = swap_cores(give)
    pieces = [jnp.stack([keep[step], got[step]]) for step in range(steps)]
    for step in range(1, steps):
        pairs = [(slab, slab ^ (2 * step)) for slab in range(slab_count)]
        pieces[step] = lax.ppermute(pieces[step], "slab", pairs)
    return pieces, got, place


CYCLES = {
    (0, 1): ((0, 1), (1, 3), (3, 2), (2, 0)),
    (1, 2): ((1, 2), (2, 0), (0, 3), (3, 1)),
    (2, 3): ((0, 1), (1, 0), (2, 3), (3, 2)),
}


def crosses():
    return lax.axis_size("section") == 4 and lax.axis_size("slab") % 2 == 0


def send(value, pairs, cross):
    if not cross:
        return lax.ppermute(value, "section", pairs)
    slabs = lax.axis_size("slab")
    joint = [(s * slabs + slab, t * slabs + (slab ^ 1)) for s, t in pairs for slab in range(slabs)]
    return lax.ppermute(value, ("section", "slab"), joint)


def swap_cores(value):
    return lax.ppermute(value, "slab", [(slab, slab ^ 1) for slab in range(lax.axis_size("slab"))])


def hop(value, source, target):
    count = lax.axis_size("section")
    if count == 4 and (source, target) in CYCLES:
        return send(value, CYCLES[source, target], crosses() and source == 1)
    if count & (count - 1):
        return lax.ppermute(value, "section", [(source, target)])
    return lax.ppermute(value, "section", [(s, s ^ source ^ target) for s in range(count)])


def gather_first(value):
    count = lax.axis_size("section")
    if count & (count - 1):
        return [value] + [hop(value, other, 0) for other in range(1, count)]
    if count == 4:
        own = swap_cores(value) if crosses() else value
        return [own] + [send(value, [(s, s ^ k) for s in range(4)], crosses()) for k in (1, 2, 3)]
    parts = [value]
    step = 1
    while step < count:
        held = parts[0] if len(parts) == 1 else jnp.concatenate(parts, axis=0)
        parts.append(lax.ppermute(held, "section", [(s, s ^ step) for s in range(count)]))
        step *= 2
    return parts


def per_device(
    features, vae_weight, vae_gain, vae_shift, vae_bias, latent_weight, latent_bias, slot_clips, row_offsets,
    in_weight, in_bias, pos_table, unet_gain, unet_shift, unet_weight, unet_bias,
):
    section_count = lax.axis_size("section")
    slab_count = lax.axis_size("slab")
    _, clip_total, slab_rows, frames, cols, channels = features.shape
    owned = clip_total // slab_count
    row_total = slab_rows * slab_count
    width = unet_weight.shape[-1]
    lat_rows, lat_cols = row_total // 2, cols // 2
    unit = lat_rows * frames

    place_shape = (section_count * owned, unit, width)
    pieces, got, place = exchange(
        features[0], slot_clips, row_offsets, pos_table.T, in_bias, place_shape, slab_count, owned
    )
    vae_same, unet_same = pl.pallas_call(
        groups_kernel,
        out_shape=[jax.ShapeDtypeStruct((size, size), BF16) for size in (channels, width)],
        in_specs=[pl.BlockSpec(memory_space=pl.ANY)],
        out_specs=[vmem()] * 2,
        compiler_params=params(GROUPS_VMEM),
        cost_estimate=pl.CostEstimate(flops=GROUPS_FLOPS, bytes_accessed=0, transcendentals=0),
        name="groups",
    )(got)
    latent = encode(
        pieces, vae_weight, vae_gain.reshape(1, -1), vae_shift.reshape(1, -1), vae_bias.reshape(1, -1),
        latent_weight.T, latent_bias.reshape(1, -1), vae_same,
    )
    latents = gather_first(latent)

    chunks = 2 if section_count % 2 == 0 else 1
    per_chunk = section_count // chunks
    streams = per_chunk * owned
    block = (streams, unit)
    state_shape = jax.ShapeDtypeStruct((lat_cols * streams * unit, width), BF16)
    layer = [unet_weight[0], unet_gain, unet_shift, unet_bias, unet_same]
    states = [None] * chunks
    arrived = [None] * chunks
    for chunk in range(chunks):
        mine = latents
        if chunks == 2:
            cut = len(latents) // 2 if section_count == 4 else -1
            mine = latents[cut:] if chunk else latents[:cut]
        operands = mine + [place, in_weight.reshape(-1, width)] + layer
        states[chunk] = pl.pallas_call(
            functools.partial(first_kernel, block, frames, len(mine), chunk),
            out_shape=state_shape,
            in_specs=[vmem()] * len(operands),
            out_specs=vmem(),
            compiler_params=params(),
            name="first_block",
        )(*operands)
        arrived[chunk] = hop(states[chunk], 0, 1)
    for index in range(1, section_count - 1):
        for chunk in range(chunks):
            states[chunk] = pl.pallas_call(
                functools.partial(later_kernel, index, block, frames),
                out_shape=state_shape,
                in_specs=[vmem()] * (2 + len(layer)),
                out_specs=vmem(),
                input_output_aliases={1: 0},
                compiler_params=params(),
                name="later_block",
            )(arrived[chunk], states[chunk], *layer)
            arrived[chunk] = hop(states[chunk], index, index + 1)
    hbm = pl.BlockSpec(memory_space=pltpu.HBM)
    out_shape = jax.ShapeDtypeStruct((section_count * owned, lat_rows, frames, lat_cols * width), BF16)
    out = None
    early = [swap_cores(state) if crosses() else state for state in states]
    for chunk in range(chunks):
        operands = [arrived[chunk]] + (states + early if chunk == 0 else [out]) + layer
        specs = [vmem()] * len(operands)
        if chunk:
            specs[1] = hbm
        out = pl.pallas_call(
            functools.partial(last_kernel, block, frames, chunk, chunks),
            out_shape=out_shape,
            in_specs=specs,
            out_specs=hbm,
            scratch_shapes=[
                pltpu.VMEM(out_shape.shape, BF16),
                pltpu.SemaphoreType.DMA,
                pltpu.SemaphoreType.DMA,
            ],
            input_output_aliases={1: 0} if chunk else {},
            compiler_params=params(),
            name="last_block",
        )(*operands)
    return out.reshape(1, section_count, owned, lat_rows, frames, lat_cols * width)


def solution(mesh):
    return jax.shard_map(
        per_device,
        mesh=mesh,
        in_specs=(
            P("section", None, "slab", None, None, None),
            P(),
            P(),
            P(),
            P(),
            P(),
            P(),
            P(),
            P(),
            P(),
            P(),
            P(),
            P("section", None),
            P("section", None),
            P("section", None, None, None, None),
            P("section", None),
        ),
        out_specs=P("section", None, "slab", None, None, None),
        check_vma=False,
    )
```

```python
import functools

import jax
import jax.numpy as jnp
from jax import lax
from jax.experimental import pallas as pl
from jax.experimental.pallas import tpu as pltpu
from jax.sharding import PartitionSpec as P

GROUPS = 32
LANES = 128
EPS = 1e-06
VMEM_LIMIT = 32 * 1024 * 1024
GROUPS_VMEM = 4 * 1024 * 1024
GROUPS_FLOPS = 12_000_000_000
F32 = jnp.float32
BF16 = jnp.bfloat16


def vmem():
    return pl.BlockSpec(memory_space=pltpu.VMEM)


def smem():
    return pl.BlockSpec(memory_space=pltpu.SMEM)


def params(limit=VMEM_LIMIT):
    return pltpu.CompilerParams(vmem_limit_bytes=limit)


def same_group(channels):
    size = channels // GROUPS

    def group_of(axis):
        index = lax.broadcasted_iota(jnp.int32, (channels, channels), axis).astype(F32)
        return jnp.floor((index + 0.5) * (1.0 / size))

    return jnp.where(group_of(0) == group_of(1), 1.0, 0.0).astype(BF16)


def groups_kernel(after_ref, *out_refs):
    del after_ref
    for out_ref in out_refs:
        out_ref[...] = same_group(out_ref.shape[0])


def group_sums(rows, same):
    high = rows.astype(BF16)
    rest = rows - high.astype(F32)
    middle = rest.astype(BF16)
    low = (rest - middle.astype(F32)).astype(BF16)
    total = jnp.dot(high, same, preferred_element_type=F32)
    total += jnp.dot(middle, same, preferred_element_type=F32)
    total += jnp.dot(low, same, preferred_element_type=F32)
    return total


def dot_last(left, right):
    return lax.dot_general(left, right, (((1,), (1,)), ((), ())), preferred_element_type=F32)


def silu(value):
    return 0.5 * value * (1.0 + jnp.tanh(0.5 * value))


def encode_kernel(slab_axis, *refs):
    (
        weight_ref, gain_ref, shift_ref, bias_ref, lat_weight_ref, lat_bias_ref, same_ref,
        out_ref, x_ref, pool_ref,
    ) = refs[-10:]
    pieces = refs[:-10]
    slab_rows = pieces[0].shape[2]
    items, frames, row_count, cols, channels = x_ref.shape
    for step, piece_ref in enumerate(pieces[::-1]):
        for half in range(2):
            source = lax.axis_index(slab_axis) ^ (2 * step + half)
            for item in range(items):
                for frame in range(frames):
                    piece = piece_ref[half, item, :, frame].astype(F32)
                    x_ref[item, frame, pl.ds(source * slab_rows, slab_rows)] = piece
    size = frames * row_count * cols
    plane = row_count * cols
    lat_rows, lat_cols = row_count // 2, cols // 2
    for item in range(items):
        x = x_ref[item].reshape(size, channels)
        sums = jnp.concatenate(
            [jnp.sum(x, axis=0, keepdims=True), jnp.sum(x * x, axis=0, keepdims=True)]
            + [jnp.zeros((6, channels), F32)],
            axis=0,
        )
        sums = group_sums(sums, same_ref[...]) * (1.0 / (size * (channels // GROUPS)))
        mean = sums[0:1]
        inverse = lax.rsqrt(sums[1:2] - mean * mean + EPS)
        act = silu((x - mean) * inverse * gain_ref[...] + shift_ref[...])
        column = lax.broadcasted_iota(jnp.int32, (size, 1), 0) & (cols - 1)
        taps = [
            jnp.where(column == 0, 0.0, pltpu.roll(act, 1, 0)),
            act,
            jnp.where(column == cols - 1, 0.0, pltpu.roll(act, size - 1, 0)),
        ]
        wide = jnp.concatenate(taps, axis=1).reshape(frames, row_count, cols, 3 * channels)
        edge = jnp.zeros((frames, 1, cols, 3 * channels), F32)
        wide = jnp.concatenate([edge, wide, edge], axis=1)
        total, still = x + bias_ref[...], None
        for row_tap in range(3):
            window = wide[:, row_tap : row_tap + row_count].reshape(size, 3 * channels).astype(BF16)
            weights = [weight_ref[time, row_tap].reshape(3 * channels, channels) for time in range(3)]
            total += jnp.dot(window, weights[2], preferred_element_type=F32)
            for weight in weights[:2]:
                term = jnp.dot(window[:plane], weight, preferred_element_type=F32)
                still = term if still is None else still + term
        paired = total.reshape(frames, lat_rows, 2, cols, channels)
        paired = paired + still.reshape(1, lat_rows, 2, cols, channels)
        merged = paired[:, :, 0] + paired[:, :, 1]
        halves = []
        for part in range(channels // LANES):
            for row in range(lat_rows):
                for frame in range(frames):
                    block = merged[frame, row, :, part * LANES : (part + 1) * LANES]
                    pool_ref[part, pl.ds((row * frames + frame) * cols, cols), :] = block
            picked = []
            for col in range(lat_cols):
                left = pool_ref[part, pl.ds(2 * col, lat_rows * frames, stride=cols), :]
                right = pool_ref[part, pl.ds(2 * col + 1, lat_rows * frames, stride=cols), :]
                picked.append((left + right) * 0.25)
            halves.append(jnp.concatenate(picked, axis=0))
        pooled = jnp.concatenate(halves, axis=1).astype(BF16)
        latent = dot_last(pooled, lat_weight_ref[...])
        out_ref[item] = (latent + lat_bias_ref[...]).astype(BF16)


def encode(pieces, *operands):
    _, items, slab_rows, frames, cols, channels = pieces[0].shape
    row_count = 2 * len(pieces) * slab_rows
    lat_rows, lat_cols = row_count // 2, cols // 2
    return pl.pallas_call(
        functools.partial(encode_kernel, "slab"),
        out_shape=jax.ShapeDtypeStruct((items, lat_cols * lat_rows * frames, operands[-2].shape[1]), BF16),
        in_specs=[vmem()] * (len(pieces) + len(operands)),
        out_specs=vmem(),
        scratch_shapes=[
            pltpu.VMEM((items, frames, row_count, cols, channels), F32),
            pltpu.VMEM((channels // LANES, lat_rows * frames * cols, LANES), F32),
        ],
        compiler_params=params(),
        name="encode",
    )(*pieces[::-1], *operands)


def shifted(value, unit, frames):
    size = value.shape[0]
    place = lax.broadcasted_iota(jnp.int32, (size, 1), 0) & (unit - 1)
    return (
        jnp.where(place < frames, 0.0, pltpu.roll(value, frames, 0)),
        value,
        jnp.where(place >= unit - frames, 0.0, pltpu.roll(value, size - frames, 0)),
    )


def conv3(value, weight_ref, block, frames):
    streams, unit = block
    edge = streams * unit
    wide = jnp.concatenate(shifted(value, unit, frames), axis=1).astype(BF16)
    terms = []
    for col_tap, window in enumerate((wide[:-edge], wide, wide[edge:])):
        weight = jnp.concatenate([weight_ref[row_tap, col_tap] for row_tap in range(3)], axis=0)
        terms.append(jnp.dot(window, weight, preferred_element_type=F32))
    left, total, right = terms
    zeros = jnp.zeros((edge, total.shape[1]), F32)
    return total + jnp.concatenate([zeros, left], axis=0) + jnp.concatenate([right, zeros], axis=0)


def conv3_narrow(value, weight, block, frames):
    streams, unit = block
    size, channels = value.shape
    edge = streams * unit
    zeros = jnp.zeros((edge, channels), F32)
    windows = []
    for moved in shifted(value, unit, frames):
        padded = jnp.concatenate([zeros, moved, zeros], axis=0)
        for col_tap in range(3):
            windows.append(padded[col_tap * edge : col_tap * edge + size])
    window = jnp.concatenate(windows, axis=1).astype(BF16)
    return jnp.dot(window, weight, preferred_element_type=F32)


def unet_layer(state, operands, block, frames):
    weight_ref, gain_ref, shift_ref, bias_ref, same_ref = operands
    streams, unit = block
    size, channels = state.shape
    cols = size // (streams * unit)
    values = state.reshape(cols, streams, unit, channels)
    rows = []
    for item in range(streams):
        own = values[:, item].reshape(cols * unit, channels)
        rows.append(jnp.sum(own, axis=0, keepdims=True))
        rows.append(jnp.sum(own * own, axis=0, keepdims=True))
    rows.extend([jnp.zeros((1, channels), F32)] * (-len(rows) % 8))
    sums = group_sums(jnp.concatenate(rows, axis=0), same_ref[...])
    sums = sums * (1.0 / (cols * unit * (channels // GROUPS)))
    normed = []
    for item in range(streams):
        mean = sums[2 * item : 2 * item + 1]
        inverse = lax.rsqrt(sums[2 * item + 1 : 2 * item + 2] - mean * mean + EPS)
        scaled = (values[:, item : item + 1] - mean) * inverse * gain_ref[...]
        normed.append(scaled + shift_ref[...])
    act = silu(jnp.concatenate(normed, axis=1).reshape(size, channels))
    total = conv3(act, weight_ref, block, frames)
    return (state + total + bias_ref[...]).astype(BF16)


def write_output(out_ref, state, first, block, frames):
    streams, unit = block
    channels = state.shape[1]
    cols = state.shape[0] // (streams * unit)
    values = state.astype(F32).reshape(cols, streams, unit, channels)
    for item in range(streams):
        wide = jnp.concatenate([values[col, item] for col in range(cols)], axis=1)
        wide = wide.astype(BF16).reshape(unit // frames, frames, cols * channels)
        out_ref[first + item] = wide


def place_rows(clips_ref, offsets_ref, table, bias, out_ref, slab, owned, frames):
    streams, unit, _ = out_ref.shape
    table_rows = table.shape[1]
    row = lax.div(lax.broadcasted_iota(jnp.int32, (unit, table_rows), 0), jnp.int32(frames))
    wanted = lax.broadcasted_iota(jnp.int32, (unit, table_rows), 1) - row
    for stream in range(streams):
        micro = stream // owned
        offset = offsets_ref[micro, clips_ref[micro, slab * owned + stream % owned]]
        hot = jnp.where(wanted == offset, 1.0, 0.0).astype(BF16)
        out_ref[stream] = dot_last(hot, table) + bias


def first_kernel(block, frames, count, chunk, *refs):
    streams, unit = block
    latent_refs = refs[:count]
    place_ref, in_weight_ref, *operands = refs[count:-1]
    state_ref = refs[-1]

    @pl.when(lax.axis_index("section") == 0)
    def _():
        size, width = state_ref.shape
        cols = size // (streams * unit)
        parts = []
        for col in range(cols):
            for ref in latent_refs:
                for item in range(ref.shape[0]):
                    parts.append(ref[item, pl.ds(col * unit, unit), :].astype(F32))
        total = conv3_narrow(jnp.concatenate(parts, axis=0), in_weight_ref[...], block, frames)
        placed = place_ref[pl.ds(chunk * streams, streams)]
        placed = placed.reshape(1, streams * unit, width)
        total = (total.reshape(cols, streams * unit, width) + placed).reshape(size, width)
        state = total.astype(BF16).astype(F32)
        state_ref[...] = unet_layer(state, operands, block, frames)


def later_kernel(index, block, frames, before_ref, kept_ref, *refs):
    del kept_ref
    *operands, state_ref = refs

    @pl.when(lax.axis_index("section") == index)
    def _():
        state_ref[...] = unet_layer(before_ref[...].astype(F32), operands, block, frames)


def last_kernel(block, frames, chunk, crossed, before_ref, kept_ref, *refs):
    streams = block[0]
    operands = refs[1:-3] if chunk else refs[:-3]
    out_ref, wide_ref, sem = refs[-3:]
    section = lax.axis_index("section")
    last = section == lax.axis_size("section") - 1

    @pl.when(last)
    def _():
        state = unet_layer(before_ref[...].astype(F32), operands, block, frames)
        write_output(wide_ref, state, 0, block, frames)

    @pl.when(jnp.logical_not(last))
    def _():
        state = kept_ref[...].astype(F32)
        if crossed:
            state = jnp.where(section < 2, before_ref[...].astype(F32), state)
        write_output(wide_ref, state, 0, block, frames)

    copy = pltpu.make_async_copy(wide_ref, out_ref.at[pl.ds(chunk * streams, streams)], sem)
    copy.start()
    copy.wait()


def select_kernel(
    section_axis, slab_axis, owned, crossed,
    clips_ref, offsets_ref, features_ref, table_ref, bias_ref, keep_ref, give_ref, place_ref,
):
    section = lax.axis_index(section_axis)
    slab = lax.axis_index(slab_axis)
    for step in range(keep_ref.shape[0]):
        for half, out_ref in enumerate((keep_ref, give_ref)):
            for item in range(owned):
                slot = (slab ^ (2 * step + half)) * owned + item
                out_ref[step, item] = features_ref[clips_ref[section, slot]]
    bias = bias_ref[...].reshape(1, -1)
    frames = features_ref.shape[2]
    worker = slab ^ 1 if crossed else slab
    place_rows(clips_ref, offsets_ref, table_ref[...], bias, place_ref, worker, owned, frames)


def exchange(features, slot_clips, row_offsets, table, bias, place_shape, slab_count, owned):
    steps = slab_count // 2
    shape = jax.ShapeDtypeStruct((steps, owned) + features.shape[1:], BF16)
    keep, give, place = pl.pallas_call(
        functools.partial(select_kernel, "section", "slab", owned, crosses()),
        out_shape=[shape, shape, jax.ShapeDtypeStruct(place_shape, F32)],
        in_specs=[smem()] * 2 + [vmem()] * 3,
        out_specs=[vmem()] * 3,
        name="select",
    )(slot_clips, row_offsets, features, table, bias)
    got = swap_cores(give)
    pieces = [jnp.stack([keep[step], got[step]]) for step in range(steps)]
    for step in range(1, steps):
        pairs = [(slab, slab ^ (2 * step)) for slab in range(slab_count)]
        pieces[step] = lax.ppermute(pieces[step], "slab", pairs)
    return pieces, got, place


ROUTES = {
    (0, 1): ((1, False), (3, False), (0, False), (2, False)),
    (1, 2): ((3, True), (2, True), (0, True), (1, True)),
    (2, 3): ((0, True), (1, True), (3, False), (2, False)),
}


def crosses():
    return lax.axis_size("section") == 4 and lax.axis_size("slab") % 2 == 0


def send(value, routes):
    if not any(cross for _, cross in routes):
        return lax.ppermute(value, "section", [(s, target) for s, (target, _) in enumerate(routes)])
    slabs = lax.axis_size("slab")
    pairs = []
    for s, (target, cross) in enumerate(routes):
        pairs += [(s * slabs + slab, target * slabs + (slab ^ 1 if cross else slab)) for slab in range(slabs)]
    return lax.ppermute(value, ("section", "slab"), pairs)


def swap_cores(value):
    return lax.ppermute(value, "slab", [(slab, slab ^ 1) for slab in range(lax.axis_size("slab"))])


def hop(value, source, target):
    count = lax.axis_size("section")
    if crosses():
        return send(value, ROUTES[source, target])
    if count & (count - 1):
        return lax.ppermute(value, "section", [(source, target)])
    return lax.ppermute(value, "section", [(s, s ^ source ^ target) for s in range(count)])


def gather_first(value):
    count = lax.axis_size("section")
    if count & (count - 1):
        return [value] + [hop(value, other, 0) for other in range(1, count)]
    if count == 4:
        own = swap_cores(value) if crosses() else value
        return [own] + [send(value, [(s ^ k, crosses()) for s in range(4)]) for k in (1, 2, 3)]
    parts = [value]
    step = 1
    while step < count:
        held = parts[0] if len(parts) == 1 else jnp.concatenate(parts, axis=0)
        parts.append(lax.ppermute(held, "section", [(s, s ^ step) for s in range(count)]))
        step *= 2
    return parts


def per_device(
    features, vae_weight, vae_gain, vae_shift, vae_bias, latent_weight, latent_bias, slot_clips, row_offsets,
    in_weight, in_bias, pos_table, unet_gain, unet_shift, unet_weight, unet_bias,
):
    section_count = lax.axis_size("section")
    slab_count = lax.axis_size("slab")
    _, clip_total, slab_rows, frames, cols, channels = features.shape
    owned = clip_total // slab_count
    row_total = slab_rows * slab_count
    width = unet_weight.shape[-1]
    lat_rows, lat_cols = row_total // 2, cols // 2
    unit = lat_rows * frames

    place_shape = (section_count * owned, unit, width)
    pieces, got, place = exchange(
        features[0], slot_clips, row_offsets, pos_table.T, in_bias, place_shape, slab_count, owned
    )
    vae_same, unet_same = pl.pallas_call(
        groups_kernel,
        out_shape=[jax.ShapeDtypeStruct((size, size), BF16) for size in (channels, width)],
        in_specs=[pl.BlockSpec(memory_space=pl.ANY)],
        out_specs=[vmem()] * 2,
        compiler_params=params(GROUPS_VMEM),
        cost_estimate=pl.CostEstimate(flops=GROUPS_FLOPS, bytes_accessed=0, transcendentals=0),
        name="groups",
    )(got)
    latent = encode(
        pieces, vae_weight, vae_gain.reshape(1, -1), vae_shift.reshape(1, -1), vae_bias.reshape(1, -1),
        latent_weight.T, latent_bias.reshape(1, -1), vae_same,
    )
    latents = gather_first(latent)

    chunks = 2 if section_count % 2 == 0 else 1
    per_chunk = section_count // chunks
    streams = per_chunk * owned
    block = (streams, unit)
    state_shape = jax.ShapeDtypeStruct((lat_cols * streams * unit, width), BF16)
    layer = [unet_weight[0], unet_gain, unet_shift, unet_bias, unet_same]
    states = [None] * chunks
    arrived = [None] * chunks
    for chunk in range(chunks):
        mine = latents
        if chunks == 2:
            cut = len(latents) // 2 if section_count == 4 else -1
            mine = latents[cut:] if chunk else latents[:cut]
        operands = mine + [place, in_weight.reshape(-1, width)] + layer
        states[chunk] = pl.pallas_call(
            functools.partial(first_kernel, block, frames, len(mine), chunk),
            out_shape=state_shape,
            in_specs=[vmem()] * len(operands),
            out_specs=vmem(),
            compiler_params=params(),
            name="first_block",
        )(*operands)
        arrived[chunk] = hop(states[chunk], 0, 1)
    for index in range(1, section_count - 1):
        for chunk in range(chunks):
            states[chunk] = pl.pallas_call(
                functools.partial(later_kernel, index, block, frames),
                out_shape=state_shape,
                in_specs=[vmem()] * (2 + len(layer)),
                out_specs=vmem(),
                input_output_aliases={1: 0},
                compiler_params=params(),
                name="later_block",
            )(arrived[chunk], states[chunk], *layer)
            arrived[chunk] = hop(states[chunk], index, index + 1)
    hbm = pl.BlockSpec(memory_space=pltpu.HBM)
    out_shape = jax.ShapeDtypeStruct((section_count * owned, lat_rows, frames, lat_cols * width), BF16)
    out = None
    for chunk in range(chunks):
        operands = [arrived[chunk], states[chunk]] + ([out] if chunk else []) + layer
        specs = [vmem()] * len(operands)
        if chunk:
            specs[2] = hbm
        out = pl.pallas_call(
            functools.partial(last_kernel, block, frames, chunk, crosses()),
            out_shape=out_shape,
            in_specs=specs,
            out_specs=hbm,
            scratch_shapes=[pltpu.VMEM((streams,) + out_shape.shape[1:], BF16), pltpu.SemaphoreType.DMA],
            input_output_aliases={2: 0} if chunk else {},
            compiler_params=params(),
            name="last_block",
        )(*operands)
    return out.reshape(1, section_count, owned, lat_rows, frames, lat_cols * width)


def solution(mesh):
    return jax.shard_map(
        per_device,
        mesh=mesh,
        in_specs=(
            P("section", None, "slab", None, None, None),
            P(),
            P(),
            P(),
            P(),
            P(),
            P(),
            P(),
            P(),
            P(),
            P(),
            P(),
            P("section", None),
            P("section", None),
            P("section", None, None, None, None),
            P("section", None),
        ),
        out_specs=P("section", None, "slab", None, None, None),
        check_vma=False,
    )
```

```python
import functools

import jax
import jax.numpy as jnp
from jax import lax
from jax.experimental import pallas as pl
from jax.experimental.pallas import tpu as pltpu
from jax.sharding import PartitionSpec as P

GROUPS = 32
LANES = 128
CUTS = (2,)
EPS = 1e-06
VMEM_LIMIT = 32 * 1024 * 1024
GROUPS_VMEM = 4 * 1024 * 1024
GROUPS_FLOPS = 12_000_000_000
F32 = jnp.float32
BF16 = jnp.bfloat16


def vmem():
    return pl.BlockSpec(memory_space=pltpu.VMEM)


def smem():
    return pl.BlockSpec(memory_space=pltpu.SMEM)


def params(limit=VMEM_LIMIT):
    return pltpu.CompilerParams(vmem_limit_bytes=limit)


def same_group(channels):
    size = channels // GROUPS

    def group_of(axis):
        index = lax.broadcasted_iota(jnp.int32, (channels, channels), axis).astype(F32)
        return jnp.floor((index + 0.5) * (1.0 / size))

    return jnp.where(group_of(0) == group_of(1), 1.0, 0.0).astype(BF16)


def groups_kernel(after_ref, *out_refs):
    del after_ref
    for out_ref in out_refs:
        out_ref[...] = same_group(out_ref.shape[0])


def group_sums(rows, same):
    high = rows.astype(BF16)
    rest = rows - high.astype(F32)
    middle = rest.astype(BF16)
    low = (rest - middle.astype(F32)).astype(BF16)
    total = jnp.dot(high, same, preferred_element_type=F32)
    total += jnp.dot(middle, same, preferred_element_type=F32)
    total += jnp.dot(low, same, preferred_element_type=F32)
    return total


def dot_last(left, right):
    return lax.dot_general(left, right, (((1,), (1,)), ((), ())), preferred_element_type=F32)


def silu(value):
    return 0.5 * value * (1.0 + jnp.tanh(0.5 * value))


def encode_kernel(slab_axis, *refs):
    (
        weight_ref, gain_ref, shift_ref, bias_ref, lat_weight_ref, lat_bias_ref, same_ref,
        out_ref, x_ref, pool_ref,
    ) = refs[-10:]
    pieces = refs[:-10]
    slab_rows = pieces[0].shape[2]
    items, frames, row_count, cols, channels = x_ref.shape
    for step, piece_ref in zip(piece_order(len(pieces)), pieces):
        for half in range(2):
            source = lax.axis_index(slab_axis) ^ (2 * step + half)
            for item in range(items):
                for frame in range(frames):
                    piece = piece_ref[half, item, :, frame].astype(F32)
                    x_ref[item, frame, pl.ds(source * slab_rows, slab_rows)] = piece
    size = frames * row_count * cols
    plane = row_count * cols
    lat_rows, lat_cols = row_count // 2, cols // 2
    for item in range(items):
        x = x_ref[item].reshape(size, channels)
        sums = jnp.concatenate(
            [jnp.sum(x, axis=0, keepdims=True), jnp.sum(x * x, axis=0, keepdims=True)]
            + [jnp.zeros((6, channels), F32)],
            axis=0,
        )
        sums = group_sums(sums, same_ref[...]) * (1.0 / (size * (channels // GROUPS)))
        mean = sums[0:1]
        inverse = lax.rsqrt(sums[1:2] - mean * mean + EPS)
        act = silu((x - mean) * inverse * gain_ref[...] + shift_ref[...])
        column = lax.broadcasted_iota(jnp.int32, (size, 1), 0) & (cols - 1)
        taps = [
            jnp.where(column == 0, 0.0, pltpu.roll(act, 1, 0)),
            act,
            jnp.where(column == cols - 1, 0.0, pltpu.roll(act, size - 1, 0)),
        ]
        wide = jnp.concatenate(taps, axis=1).reshape(frames, row_count, cols, 3 * channels)
        edge = jnp.zeros((frames, 1, cols, 3 * channels), F32)
        wide = jnp.concatenate([edge, wide, edge], axis=1)
        total, still = x + bias_ref[...], None
        for row_tap in range(3):
            window = wide[:, row_tap : row_tap + row_count].reshape(size, 3 * channels).astype(BF16)
            weights = [weight_ref[time, row_tap].reshape(3 * channels, channels) for time in range(3)]
            total += jnp.dot(window, weights[2], preferred_element_type=F32)
            for weight in weights[:2]:
                term = jnp.dot(window[:plane], weight, preferred_element_type=F32)
                still = term if still is None else still + term
        paired = total.reshape(frames, lat_rows, 2, cols, channels)
        paired = paired + still.reshape(1, lat_rows, 2, cols, channels)
        merged = paired[:, :, 0] + paired[:, :, 1]
        halves = []
        for part in range(channels // LANES):
            for row in range(lat_rows):
                for frame in range(frames):
                    block = merged[frame, row, :, part * LANES : (part + 1) * LANES]
                    pool_ref[part, pl.ds((row * frames + frame) * cols, cols), :] = block
            picked = []
            for col in range(lat_cols):
                left = pool_ref[part, pl.ds(2 * col, lat_rows * frames, stride=cols), :]
                right = pool_ref[part, pl.ds(2 * col + 1, lat_rows * frames, stride=cols), :]
                picked.append((left + right) * 0.25)
            halves.append(jnp.concatenate(picked, axis=0))
        pooled = jnp.concatenate(halves, axis=1).astype(BF16)
        latent = dot_last(pooled, lat_weight_ref[...])
        out_ref[item] = (latent + lat_bias_ref[...]).astype(BF16)


def piece_order(steps):
    return (2, 3, 1, 0) if steps == 4 else tuple(range(steps))[::-1]


def encode(pieces, *operands):
    _, items, slab_rows, frames, cols, channels = pieces[0].shape
    row_count = 2 * len(pieces) * slab_rows
    lat_rows, lat_cols = row_count // 2, cols // 2
    return pl.pallas_call(
        functools.partial(encode_kernel, "slab"),
        out_shape=jax.ShapeDtypeStruct((items, lat_cols * lat_rows * frames, operands[-2].shape[1]), BF16),
        in_specs=[vmem()] * (len(pieces) + len(operands)),
        out_specs=vmem(),
        scratch_shapes=[
            pltpu.VMEM((items, frames, row_count, cols, channels), F32),
            pltpu.VMEM((channels // LANES, lat_rows * frames * cols, LANES), F32),
        ],
        compiler_params=params(),
        name="encode",
    )(*[pieces[step] for step in piece_order(len(pieces))], *operands)


def shifted(value, unit, frames):
    size = value.shape[0]
    place = lax.broadcasted_iota(jnp.int32, (size, 1), 0) & (unit - 1)
    return (
        jnp.where(place < frames, 0.0, pltpu.roll(value, frames, 0)),
        value,
        jnp.where(place >= unit - frames, 0.0, pltpu.roll(value, size - frames, 0)),
    )


def conv3(value, weight_ref, block, frames):
    streams, unit = block
    edge = streams * unit
    wide = jnp.concatenate(shifted(value, unit, frames), axis=1).astype(BF16)
    terms = []
    for col_tap, window in enumerate((wide[:-edge], wide, wide[edge:])):
        weight = jnp.concatenate([weight_ref[row_tap, col_tap] for row_tap in range(3)], axis=0)
        terms.append(jnp.dot(window, weight, preferred_element_type=F32))
    left, total, right = terms
    zeros = jnp.zeros((edge, total.shape[1]), F32)
    return total + jnp.concatenate([zeros, left], axis=0) + jnp.concatenate([right, zeros], axis=0)


def conv3_narrow(value, weight, block, frames):
    streams, unit = block
    size, channels = value.shape
    edge = streams * unit
    zeros = jnp.zeros((edge, channels), F32)
    windows = []
    for moved in shifted(value, unit, frames):
        padded = jnp.concatenate([zeros, moved, zeros], axis=0)
        for col_tap in range(3):
            windows.append(padded[col_tap * edge : col_tap * edge + size])
    window = jnp.concatenate(windows, axis=1).astype(BF16)
    return jnp.dot(window, weight, preferred_element_type=F32)


def unet_layer(state, operands, block, frames):
    weight_ref, gain_ref, shift_ref, bias_ref, same_ref = operands
    streams, unit = block
    size, channels = state.shape
    cols = size // (streams * unit)
    values = state.reshape(cols, streams, unit, channels)
    rows = []
    for item in range(streams):
        own = values[:, item].reshape(cols * unit, channels)
        rows.append(jnp.sum(own, axis=0, keepdims=True))
        rows.append(jnp.sum(own * own, axis=0, keepdims=True))
    rows.extend([jnp.zeros((1, channels), F32)] * (-len(rows) % 8))
    sums = group_sums(jnp.concatenate(rows, axis=0), same_ref[...])
    sums = sums * (1.0 / (cols * unit * (channels // GROUPS)))
    normed = []
    for item in range(streams):
        mean = sums[2 * item : 2 * item + 1]
        inverse = lax.rsqrt(sums[2 * item + 1 : 2 * item + 2] - mean * mean + EPS)
        scaled = (values[:, item : item + 1] - mean) * inverse * gain_ref[...]
        normed.append(scaled + shift_ref[...])
    act = silu(jnp.concatenate(normed, axis=1).reshape(size, channels))
    total = conv3(act, weight_ref, block, frames)
    return (state + total + bias_ref[...]).astype(BF16)


def write_output(out_ref, state, first, block, frames):
    streams, unit = block
    channels = state.shape[1]
    cols = state.shape[0] // (streams * unit)
    values = state.astype(F32).reshape(cols, streams, unit, channels)
    for item in range(streams):
        wide = jnp.concatenate([values[col, item] for col in range(cols)], axis=1)
        wide = wide.astype(BF16).reshape(unit // frames, frames, cols * channels)
        out_ref[first + item] = wide


def place_rows(clips_ref, offsets_ref, table, bias, out_ref, slab, owned, frames):
    streams, unit, _ = out_ref.shape
    table_rows = table.shape[1]
    row = lax.div(lax.broadcasted_iota(jnp.int32, (unit, table_rows), 0), jnp.int32(frames))
    wanted = lax.broadcasted_iota(jnp.int32, (unit, table_rows), 1) - row
    for stream in range(streams):
        micro = stream // owned
        offset = offsets_ref[micro, clips_ref[micro, slab * owned + stream % owned]]
        hot = jnp.where(wanted == offset, 1.0, 0.0).astype(BF16)
        out_ref[stream] = dot_last(hot, table) + bias


def first_kernel(block, frames, count, first, *refs):
    streams, unit = block
    latent_refs = refs[:count]
    place_ref, in_weight_ref, *operands = refs[count:-1]
    state_ref = refs[-1]

    @pl.when(lax.axis_index("section") == 0)
    def _():
        size, width = state_ref.shape
        cols = size // (streams * unit)
        parts = []
        for col in range(cols):
            for ref in latent_refs:
                for item in range(ref.shape[0]):
                    parts.append(ref[item, pl.ds(col * unit, unit), :].astype(F32))
        total = conv3_narrow(jnp.concatenate(parts, axis=0), in_weight_ref[...], block, frames)
        placed = place_ref[pl.ds(first, streams)]
        placed = placed.reshape(1, streams * unit, width)
        total = (total.reshape(cols, streams * unit, width) + placed).reshape(size, width)
        state = total.astype(BF16).astype(F32)
        state_ref[...] = unet_layer(state, operands, block, frames)


def later_kernel(index, block, frames, before_ref, kept_ref, *refs):
    del kept_ref
    *operands, state_ref = refs

    @pl.when(lax.axis_index("section") == index)
    def _():
        state_ref[...] = unet_layer(before_ref[...].astype(F32), operands, block, frames)


def last_kernel(block, frames, first, crossed, before_ref, kept_ref, *refs):
    streams = block[0]
    operands = refs[1:-3] if first else refs[:-3]
    out_ref, wide_ref, sem = refs[-3:]
    section = lax.axis_index("section")
    last = section == lax.axis_size("section") - 1

    @pl.when(last)
    def _():
        state = unet_layer(before_ref[...].astype(F32), operands, block, frames)
        write_output(wide_ref, state, 0, block, frames)

    @pl.when(jnp.logical_not(last))
    def _():
        state = kept_ref[...].astype(F32)
        if crossed:
            state = jnp.where(section < 2, before_ref[...].astype(F32), state)
        write_output(wide_ref, state, 0, block, frames)

    copy = pltpu.make_async_copy(wide_ref, out_ref.at[pl.ds(first, streams)], sem)
    copy.start()
    copy.wait()


def select_kernel(
    section_axis, slab_axis, owned, crossed,
    clips_ref, offsets_ref, features_ref, table_ref, bias_ref, keep_ref, give_ref, place_ref,
):
    section = lax.axis_index(section_axis)
    slab = lax.axis_index(slab_axis)
    for step in range(keep_ref.shape[0]):
        for half, out_ref in enumerate((keep_ref, give_ref)):
            for item in range(owned):
                slot = (slab ^ (2 * step + half)) * owned + item
                out_ref[step, item] = features_ref[clips_ref[section, slot]]
    bias = bias_ref[...].reshape(1, -1)
    frames = features_ref.shape[2]
    worker = slab ^ 1 if crossed else slab
    place_rows(clips_ref, offsets_ref, table_ref[...], bias, place_ref, worker, owned, frames)


def exchange(features, slot_clips, row_offsets, table, bias, place_shape, slab_count, owned):
    steps = slab_count // 2
    shape = jax.ShapeDtypeStruct((steps, owned) + features.shape[1:], BF16)
    keep, give, place = pl.pallas_call(
        functools.partial(select_kernel, "section", "slab", owned, crosses()),
        out_shape=[shape, shape, jax.ShapeDtypeStruct(place_shape, F32)],
        in_specs=[smem()] * 2 + [vmem()] * 3,
        out_specs=[vmem()] * 3,
        name="select",
    )(slot_clips, row_offsets, features, table, bias)
    got = swap_cores(give)
    pieces = [jnp.stack([keep[step], got[step]]) for step in range(steps)]
    for step in range(1, steps):
        pairs = [(slab, slab ^ (2 * step)) for slab in range(slab_count)]
        pieces[step] = lax.ppermute(pieces[step], "slab", pairs)
    return pieces, got, place


ROUTES = {
    (0, 1): ((1, False), (3, False), (2, True), (0, False)),
    (1, 2): ((1, True), (2, True), (0, True), (3, True)),
    (2, 3): ((0, True), (1, True), (3, False), (2, False)),
}


def crosses():
    return lax.axis_size("section") == 4 and lax.axis_size("slab") % 2 == 0


def send(value, routes):
    if not any(cross for _, cross in routes):
        return lax.ppermute(value, "section", [(s, target) for s, (target, _) in enumerate(routes)])
    slabs = lax.axis_size("slab")
    pairs = []
    for s, (target, cross) in enumerate(routes):
        pairs += [(s * slabs + slab, target * slabs + (slab ^ 1 if cross else slab)) for slab in range(slabs)]
    return lax.ppermute(value, ("section", "slab"), pairs)


def swap_cores(value):
    return lax.ppermute(value, "slab", [(slab, slab ^ 1) for slab in range(lax.axis_size("slab"))])


def hop(value, source, target):
    count = lax.axis_size("section")
    if crosses():
        return send(value, ROUTES[source, target])
    if count & (count - 1):
        return lax.ppermute(value, "section", [(source, target)])
    return lax.ppermute(value, "section", [(s, s ^ source ^ target) for s in range(count)])


def gather_first(value):
    count = lax.axis_size("section")
    if count & (count - 1):
        return [value] + [hop(value, other, 0) for other in range(1, count)]
    if count == 4:
        own = swap_cores(value) if crosses() else value
        return [own] + [send(value, [(s ^ k, crosses()) for s in range(4)]) for k in (1, 2, 3)]
    parts = [value]
    step = 1
    while step < count:
        held = parts[0] if len(parts) == 1 else jnp.concatenate(parts, axis=0)
        parts.append(lax.ppermute(held, "section", [(s, s ^ step) for s in range(count)]))
        step *= 2
    return parts


def per_device(
    features, vae_weight, vae_gain, vae_shift, vae_bias, latent_weight, latent_bias, slot_clips, row_offsets,
    in_weight, in_bias, pos_table, unet_gain, unet_shift, unet_weight, unet_bias,
):
    section_count = lax.axis_size("section")
    slab_count = lax.axis_size("slab")
    _, clip_total, slab_rows, frames, cols, channels = features.shape
    owned = clip_total // slab_count
    row_total = slab_rows * slab_count
    width = unet_weight.shape[-1]
    lat_rows, lat_cols = row_total // 2, cols // 2
    unit = lat_rows * frames

    place_shape = (section_count * owned, unit, width)
    pieces, got, place = exchange(
        features[0], slot_clips, row_offsets, pos_table.T, in_bias, place_shape, slab_count, owned
    )
    vae_same, unet_same = pl.pallas_call(
        groups_kernel,
        out_shape=[jax.ShapeDtypeStruct((size, size), BF16) for size in (channels, width)],
        in_specs=[pl.BlockSpec(memory_space=pl.ANY)],
        out_specs=[vmem()] * 2,
        compiler_params=params(GROUPS_VMEM),
        cost_estimate=pl.CostEstimate(flops=GROUPS_FLOPS, bytes_accessed=0, transcendentals=0),
        name="groups",
    )(got)
    latent = encode(
        pieces, vae_weight, vae_gain.reshape(1, -1), vae_shift.reshape(1, -1), vae_bias.reshape(1, -1),
        latent_weight.T, latent_bias.reshape(1, -1), vae_same,
    )
    latents = gather_first(latent)

    if section_count == 4:
        parts = [latents[first:last] for first, last in zip((0,) + CUTS, CUTS + (4,))]
    elif section_count & (section_count - 1):
        parts = [latents]
    else:
        parts = [latents[:-1], latents[-1:]]
    layer = [unet_weight[0], unet_gain, unet_shift, unet_bias, unet_same]
    blocks, firsts, states, arrived = [], [], [], []
    for part in parts:
        streams = sum(array.shape[0] for array in part)
        firsts.append(sum(block[0] for block in blocks))
        blocks.append((streams, unit))
        operands = part + [place, in_weight.reshape(-1, width)] + layer
        state = pl.pallas_call(
            functools.partial(first_kernel, blocks[-1], frames, len(part), firsts[-1]),
            out_shape=jax.ShapeDtypeStruct((lat_cols * streams * unit, width), BF16),
            in_specs=[vmem()] * len(operands),
            out_specs=vmem(),
            compiler_params=params(),
            name="first_block",
        )(*operands)
        states.append(state)
        arrived.append(hop(state, 0, 1))
    for index in range(1, section_count - 1):
        for chunk, block in enumerate(blocks):
            states[chunk] = pl.pallas_call(
                functools.partial(later_kernel, index, block, frames),
                out_shape=jax.ShapeDtypeStruct(states[chunk].shape, BF16),
                in_specs=[vmem()] * (2 + len(layer)),
                out_specs=vmem(),
                input_output_aliases={1: 0},
                compiler_params=params(),
                name="later_block",
            )(arrived[chunk], states[chunk], *layer)
            arrived[chunk] = hop(states[chunk], index, index + 1)
    hbm = pl.BlockSpec(memory_space=pltpu.HBM)
    out_shape = jax.ShapeDtypeStruct((section_count * owned, lat_rows, frames, lat_cols * width), BF16)
    out = None
    for chunk, block in enumerate(blocks):
        operands = [arrived[chunk], states[chunk]] + ([out] if chunk else []) + layer
        specs = [vmem()] * len(operands)
        if chunk:
            specs[2] = hbm
        out = pl.pallas_call(
            functools.partial(last_kernel, block, frames, firsts[chunk], crosses()),
            out_shape=out_shape,
            in_specs=specs,
            out_specs=hbm,
            scratch_shapes=[pltpu.VMEM((block[0],) + out_shape.shape[1:], BF16), pltpu.SemaphoreType.DMA],
            input_output_aliases={2: 0} if chunk else {},
            compiler_params=params(),
            name="last_block",
        )(*operands)
    return out.reshape(1, section_count, owned, lat_rows, frames, lat_cols * width)


def solution(mesh):
    return jax.shard_map(
        per_device,
        mesh=mesh,
        in_specs=(
            P("section", None, "slab", None, None, None),
            P(),
            P(),
            P(),
            P(),
            P(),
            P(),
            P(),
            P(),
            P(),
            P(),
            P(),
            P("section", None),
            P("section", None),
            P("section", None, None, None, None),
            P("section", None),
        ),
        out_specs=P("section", None, "slab", None, None, None),
        check_vma=False,
    )
```

```python
import functools

import jax
import jax.numpy as jnp
from jax import lax
from jax.experimental import pallas as pl
from jax.experimental.pallas import tpu as pltpu
from jax.sharding import PartitionSpec as P

GROUPS = 32
LANES = 128
CUTS = (2,)
EPS = 1e-06
VMEM_LIMIT = 32 * 1024 * 1024
GROUPS_VMEM = 4 * 1024 * 1024
GROUPS_FLOPS = 12_000_000_000
F32 = jnp.float32
BF16 = jnp.bfloat16


def vmem():
    return pl.BlockSpec(memory_space=pltpu.VMEM)


def smem():
    return pl.BlockSpec(memory_space=pltpu.SMEM)


def params(limit=VMEM_LIMIT):
    return pltpu.CompilerParams(vmem_limit_bytes=limit)


def same_group(channels):
    size = channels // GROUPS

    def group_of(axis):
        index = lax.broadcasted_iota(jnp.int32, (channels, channels), axis).astype(F32)
        return jnp.floor((index + 0.5) * (1.0 / size))

    return jnp.where(group_of(0) == group_of(1), 1.0, 0.0).astype(BF16)


def groups_kernel(after_ref, *out_refs):
    del after_ref
    for out_ref in out_refs:
        out_ref[...] = same_group(out_ref.shape[0])


def group_sums(rows, same):
    high = rows.astype(BF16)
    rest = rows - high.astype(F32)
    middle = rest.astype(BF16)
    low = (rest - middle.astype(F32)).astype(BF16)
    total = jnp.dot(high, same, preferred_element_type=F32)
    total += jnp.dot(middle, same, preferred_element_type=F32)
    total += jnp.dot(low, same, preferred_element_type=F32)
    return total


def dot_last(left, right):
    return lax.dot_general(left, right, (((1,), (1,)), ((), ())), preferred_element_type=F32)


def silu(value):
    return 0.5 * value * (1.0 + jnp.tanh(0.5 * value))


def encode_kernel(slab_axis, *refs):
    (
        weight_ref, gain_ref, shift_ref, bias_ref, lat_weight_ref, lat_bias_ref, same_ref,
        out_ref, x_ref, pool_ref,
    ) = refs[-10:]
    pieces = refs[:-10]
    slab_rows = pieces[0].shape[2]
    items, frames, row_count, cols, channels = x_ref.shape
    for step, piece_ref in zip(piece_order(len(pieces)), pieces):
        for half in range(2):
            source = lax.axis_index(slab_axis) ^ (2 * step + (half if step == 0 else 1 - half))
            for item in range(items):
                for frame in range(frames):
                    piece = piece_ref[half, item, :, frame].astype(F32)
                    x_ref[item, frame, pl.ds(source * slab_rows, slab_rows)] = piece
    size = frames * row_count * cols
    plane = row_count * cols
    lat_rows, lat_cols = row_count // 2, cols // 2
    for item in range(items):
        x = x_ref[item].reshape(size, channels)
        sums = jnp.concatenate(
            [jnp.sum(x, axis=0, keepdims=True), jnp.sum(x * x, axis=0, keepdims=True)]
            + [jnp.zeros((6, channels), F32)],
            axis=0,
        )
        sums = group_sums(sums, same_ref[...]) * (1.0 / (size * (channels // GROUPS)))
        mean = sums[0:1]
        inverse = lax.rsqrt(sums[1:2] - mean * mean + EPS)
        act = silu((x - mean) * inverse * gain_ref[...] + shift_ref[...])
        column = lax.broadcasted_iota(jnp.int32, (size, 1), 0) & (cols - 1)
        taps = [
            jnp.where(column == 0, 0.0, pltpu.roll(act, 1, 0)),
            act,
            jnp.where(column == cols - 1, 0.0, pltpu.roll(act, size - 1, 0)),
        ]
        wide = jnp.concatenate(taps, axis=1).reshape(frames, row_count, cols, 3 * channels)
        edge = jnp.zeros((frames, 1, cols, 3 * channels), F32)
        wide = jnp.concatenate([edge, wide, edge], axis=1)
        total, still = x + bias_ref[...], None
        for row_tap in range(3):
            window = wide[:, row_tap : row_tap + row_count].reshape(size, 3 * channels).astype(BF16)
            weights = [weight_ref[time, row_tap].reshape(3 * channels, channels) for time in range(3)]
            total += jnp.dot(window, weights[2], preferred_element_type=F32)
            for weight in weights[:2]:
                term = jnp.dot(window[:plane], weight, preferred_element_type=F32)
                still = term if still is None else still + term
        paired = total.reshape(frames, lat_rows, 2, cols, channels)
        paired = paired + still.reshape(1, lat_rows, 2, cols, channels)
        merged = paired[:, :, 0] + paired[:, :, 1]
        halves = []
        for part in range(channels // LANES):
            for row in range(lat_rows):
                for frame in range(frames):
                    block = merged[frame, row, :, part * LANES : (part + 1) * LANES]
                    pool_ref[part, pl.ds((row * frames + frame) * cols, cols), :] = block
            picked = []
            for col in range(lat_cols):
                left = pool_ref[part, pl.ds(2 * col, lat_rows * frames, stride=cols), :]
                right = pool_ref[part, pl.ds(2 * col + 1, lat_rows * frames, stride=cols), :]
                picked.append((left + right) * 0.25)
            halves.append(jnp.concatenate(picked, axis=0))
        pooled = jnp.concatenate(halves, axis=1).astype(BF16)
        latent = dot_last(pooled, lat_weight_ref[...])
        out_ref[item] = (latent + lat_bias_ref[...]).astype(BF16)


def piece_order(steps):
    return (2, 3, 1, 0) if steps == 4 else tuple(range(steps))[::-1]


def encode(pieces, *operands):
    _, items, slab_rows, frames, cols, channels = pieces[0].shape
    row_count = 2 * len(pieces) * slab_rows
    lat_rows, lat_cols = row_count // 2, cols // 2
    return pl.pallas_call(
        functools.partial(encode_kernel, "slab"),
        out_shape=jax.ShapeDtypeStruct((items, lat_cols * lat_rows * frames, operands[-2].shape[1]), BF16),
        in_specs=[vmem()] * (len(pieces) + len(operands)),
        out_specs=vmem(),
        scratch_shapes=[
            pltpu.VMEM((items, frames, row_count, cols, channels), F32),
            pltpu.VMEM((channels // LANES, lat_rows * frames * cols, LANES), F32),
        ],
        compiler_params=params(),
        name="encode",
    )(*[pieces[step] for step in piece_order(len(pieces))], *operands)


def shifted(value, unit, frames):
    size = value.shape[0]
    place = lax.broadcasted_iota(jnp.int32, (size, 1), 0) & (unit - 1)
    return (
        jnp.where(place < frames, 0.0, pltpu.roll(value, frames, 0)),
        value,
        jnp.where(place >= unit - frames, 0.0, pltpu.roll(value, size - frames, 0)),
    )


def conv3(value, weight_ref, block, frames):
    streams, unit = block
    edge = streams * unit
    wide = jnp.concatenate(shifted(value, unit, frames), axis=1).astype(BF16)
    terms = []
    for col_tap, window in enumerate((wide[:-edge], wide, wide[edge:])):
        weight = jnp.concatenate([weight_ref[row_tap, col_tap] for row_tap in range(3)], axis=0)
        terms.append(jnp.dot(window, weight, preferred_element_type=F32))
    left, total, right = terms
    zeros = jnp.zeros((edge, total.shape[1]), F32)
    return total + jnp.concatenate([zeros, left], axis=0) + jnp.concatenate([right, zeros], axis=0)


def conv3_narrow(value, weight, block, frames):
    streams, unit = block
    size, channels = value.shape
    edge = streams * unit
    zeros = jnp.zeros((edge, channels), F32)
    windows = []
    for moved in shifted(value, unit, frames):
        padded = jnp.concatenate([zeros, moved, zeros], axis=0)
        for col_tap in range(3):
            windows.append(padded[col_tap * edge : col_tap * edge + size])
    window = jnp.concatenate(windows, axis=1).astype(BF16)
    return jnp.dot(window, weight, preferred_element_type=F32)


def unet_layer(state, operands, block, frames):
    weight_ref, gain_ref, shift_ref, bias_ref, same_ref = operands
    streams, unit = block
    size, channels = state.shape
    cols = size // (streams * unit)
    values = state.reshape(cols, streams, unit, channels)
    rows = []
    for item in range(streams):
        own = values[:, item].reshape(cols * unit, channels)
        rows.append(jnp.sum(own, axis=0, keepdims=True))
        rows.append(jnp.sum(own * own, axis=0, keepdims=True))
    rows.extend([jnp.zeros((1, channels), F32)] * (-len(rows) % 8))
    sums = group_sums(jnp.concatenate(rows, axis=0), same_ref[...])
    sums = sums * (1.0 / (cols * unit * (channels // GROUPS)))
    normed = []
    for item in range(streams):
        mean = sums[2 * item : 2 * item + 1]
        inverse = lax.rsqrt(sums[2 * item + 1 : 2 * item + 2] - mean * mean + EPS)
        scaled = (values[:, item : item + 1] - mean) * inverse * gain_ref[...]
        normed.append(scaled + shift_ref[...])
    act = silu(jnp.concatenate(normed, axis=1).reshape(size, channels))
    total = conv3(act, weight_ref, block, frames)
    return (state + total + bias_ref[...]).astype(BF16)


def write_output(out_ref, state, first, block, frames):
    streams, unit = block
    channels = state.shape[1]
    cols = state.shape[0] // (streams * unit)
    values = state.astype(F32).reshape(cols, streams, unit, channels)
    for item in range(streams):
        wide = jnp.concatenate([values[col, item] for col in range(cols)], axis=1)
        wide = wide.astype(BF16).reshape(unit // frames, frames, cols * channels)
        out_ref[first + item] = wide


def place_rows(clips_ref, offsets_ref, table, bias, out_ref, slab, owned, frames):
    streams, unit, _ = out_ref.shape
    table_rows = table.shape[1]
    row = lax.div(lax.broadcasted_iota(jnp.int32, (unit, table_rows), 0), jnp.int32(frames))
    wanted = lax.broadcasted_iota(jnp.int32, (unit, table_rows), 1) - row
    for stream in range(streams):
        micro = stream // owned
        offset = offsets_ref[micro, clips_ref[micro, slab * owned + stream % owned]]
        hot = jnp.where(wanted == offset, 1.0, 0.0).astype(BF16)
        out_ref[stream] = dot_last(hot, table) + bias


def first_kernel(block, frames, count, first, *refs):
    streams, unit = block
    latent_refs = refs[:count]
    place_ref, in_weight_ref, *operands = refs[count:-1]
    state_ref = refs[-1]

    @pl.when(lax.axis_index("section") == 0)
    def _():
        size, width = state_ref.shape
        cols = size // (streams * unit)
        parts = []
        for col in range(cols):
            for ref in latent_refs:
                for item in range(ref.shape[0]):
                    parts.append(ref[item, pl.ds(col * unit, unit), :].astype(F32))
        total = conv3_narrow(jnp.concatenate(parts, axis=0), in_weight_ref[...], block, frames)
        placed = place_ref[pl.ds(first, streams)]
        placed = placed.reshape(1, streams * unit, width)
        total = (total.reshape(cols, streams * unit, width) + placed).reshape(size, width)
        state = total.astype(BF16).astype(F32)
        state_ref[...] = unet_layer(state, operands, block, frames)


def later_kernel(index, block, frames, before_ref, kept_ref, *refs):
    del kept_ref
    *operands, state_ref = refs

    @pl.when(lax.axis_index("section") == index)
    def _():
        state_ref[...] = unet_layer(before_ref[...].astype(F32), operands, block, frames)


def last_kernel(block, frames, first, crossed, before_ref, kept_ref, *refs):
    streams = block[0]
    operands = refs[1:-3] if first else refs[:-3]
    out_ref, wide_ref, sem = refs[-3:]
    section = lax.axis_index("section")
    last = section == lax.axis_size("section") - 1

    @pl.when(last)
    def _():
        state = unet_layer(before_ref[...].astype(F32), operands, block, frames)
        write_output(wide_ref, state, 0, block, frames)

    @pl.when(jnp.logical_not(last))
    def _():
        state = kept_ref[...].astype(F32)
        if crossed:
            state = jnp.where(section < 2, before_ref[...].astype(F32), state)
        write_output(wide_ref, state, 0, block, frames)

    copy = pltpu.make_async_copy(wide_ref, out_ref.at[pl.ds(first, streams)], sem)
    copy.start()
    copy.wait()


def select_kernel(
    section_axis, slab_axis, owned, crossed,
    clips_ref, offsets_ref, features_ref, table_ref, bias_ref, keep_ref, give_ref, place_ref,
):
    section = lax.axis_index(section_axis)
    slab = lax.axis_index(slab_axis)
    for step in range(keep_ref.shape[0]):
        for half, out_ref in enumerate((keep_ref, give_ref)):
            for item in range(owned):
                other = half if step == 0 else 1 - half
                slot = (slab ^ (2 * step + other)) * owned + item
                out_ref[step, item] = features_ref[clips_ref[section, slot]]
    bias = bias_ref[...].reshape(1, -1)
    frames = features_ref.shape[2]
    worker = slab ^ 1 if crossed else slab
    place_rows(clips_ref, offsets_ref, table_ref[...], bias, place_ref, worker, owned, frames)


def exchange(features, slot_clips, row_offsets, table, bias, place_shape, slab_count, owned):
    steps = slab_count // 2
    shape = jax.ShapeDtypeStruct((steps, owned) + features.shape[1:], BF16)
    keep, give, place = pl.pallas_call(
        functools.partial(select_kernel, "section", "slab", owned, crosses()),
        out_shape=[shape, shape, jax.ShapeDtypeStruct(place_shape, F32)],
        in_specs=[smem()] * 2 + [vmem()] * 3,
        out_specs=[vmem()] * 3,
        name="select",
    )(slot_clips, row_offsets, features, table, bias)
    got = swap_cores(give)
    pieces = [jnp.stack([keep[step], got[step]]) for step in range(steps)]
    for step in range(1, steps):
        pairs = [(slab, slab ^ (2 * step + 1)) for slab in range(slab_count)]
        pieces[step] = lax.ppermute(pieces[step], "slab", pairs)
    return pieces, got, place


ROUTES = {
    (0, 1): ((1, False), (3, False), (2, True), (0, False)),
    (1, 2): ((1, True), (2, True), (0, True), (3, True)),
    (2, 3): ((0, True), (1, True), (3, False), (2, False)),
}


def crosses():
    return lax.axis_size("section") == 4 and lax.axis_size("slab") % 2 == 0


def send(value, routes):
    if not any(cross for _, cross in routes):
        return lax.ppermute(value, "section", [(s, target) for s, (target, _) in enumerate(routes)])
    slabs = lax.axis_size("slab")
    pairs = []
    for s, (target, cross) in enumerate(routes):
        pairs += [(s * slabs + slab, target * slabs + (slab ^ 1 if cross else slab)) for slab in range(slabs)]
    return lax.ppermute(value, ("section", "slab"), pairs)


def swap_cores(value):
    return lax.ppermute(value, "slab", [(slab, slab ^ 1) for slab in range(lax.axis_size("slab"))])


def hop(value, source, target):
    count = lax.axis_size("section")
    if crosses():
        return send(value, ROUTES[source, target])
    if count & (count - 1):
        return lax.ppermute(value, "section", [(source, target)])
    return lax.ppermute(value, "section", [(s, s ^ source ^ target) for s in range(count)])


def gather_first(value):
    count = lax.axis_size("section")
    if count & (count - 1):
        return [value] + [hop(value, other, 0) for other in range(1, count)]
    if count == 4:
        own = swap_cores(value) if crosses() else value
        return [own] + [send(value, [(s ^ k, crosses()) for s in range(4)]) for k in (1, 2, 3)]
    parts = [value]
    step = 1
    while step < count:
        held = parts[0] if len(parts) == 1 else jnp.concatenate(parts, axis=0)
        parts.append(lax.ppermute(held, "section", [(s, s ^ step) for s in range(count)]))
        step *= 2
    return parts


def per_device(
    features, vae_weight, vae_gain, vae_shift, vae_bias, latent_weight, latent_bias, slot_clips, row_offsets,
    in_weight, in_bias, pos_table, unet_gain, unet_shift, unet_weight, unet_bias,
):
    section_count = lax.axis_size("section")
    slab_count = lax.axis_size("slab")
    _, clip_total, slab_rows, frames, cols, channels = features.shape
    owned = clip_total // slab_count
    row_total = slab_rows * slab_count
    width = unet_weight.shape[-1]
    lat_rows, lat_cols = row_total // 2, cols // 2
    unit = lat_rows * frames

    place_shape = (section_count * owned, unit, width)
    pieces, got, place = exchange(
        features[0], slot_clips, row_offsets, pos_table.T, in_bias, place_shape, slab_count, owned
    )
    vae_same, unet_same = pl.pallas_call(
        groups_kernel,
        out_shape=[jax.ShapeDtypeStruct((size, size), BF16) for size in (channels, width)],
        in_specs=[pl.BlockSpec(memory_space=pl.ANY)],
        out_specs=[vmem()] * 2,
        compiler_params=params(GROUPS_VMEM),
        cost_estimate=pl.CostEstimate(flops=GROUPS_FLOPS, bytes_accessed=0, transcendentals=0),
        name="groups",
    )(got)
    latent = encode(
        pieces, vae_weight, vae_gain.reshape(1, -1), vae_shift.reshape(1, -1), vae_bias.reshape(1, -1),
        latent_weight.T, latent_bias.reshape(1, -1), vae_same,
    )
    latents = gather_first(latent)

    if section_count == 4:
        parts = [latents[first:last] for first, last in zip((0,) + CUTS, CUTS + (4,))]
    elif section_count & (section_count - 1):
        parts = [latents]
    else:
        parts = [latents[:-1], latents[-1:]]
    layer = [unet_weight[0], unet_gain, unet_shift, unet_bias, unet_same]
    blocks, firsts, states, arrived = [], [], [], []
    for part in parts:
        streams = sum(array.shape[0] for array in part)
        firsts.append(sum(block[0] for block in blocks))
        blocks.append((streams, unit))
        operands = part + [place, in_weight.reshape(-1, width)] + layer
        state = pl.pallas_call(
            functools.partial(first_kernel, blocks[-1], frames, len(part), firsts[-1]),
            out_shape=jax.ShapeDtypeStruct((lat_cols * streams * unit, width), BF16),
            in_specs=[vmem()] * len(operands),
            out_specs=vmem(),
            compiler_params=params(),
            name="first_block",
        )(*operands)
        states.append(state)
        arrived.append(hop(state, 0, 1))
    for index in range(1, section_count - 1):
        for chunk, block in enumerate(blocks):
            states[chunk] = pl.pallas_call(
                functools.partial(later_kernel, index, block, frames),
                out_shape=jax.ShapeDtypeStruct(states[chunk].shape, BF16),
                in_specs=[vmem()] * (2 + len(layer)),
                out_specs=vmem(),
                input_output_aliases={1: 0},
                compiler_params=params(),
                name="later_block",
            )(arrived[chunk], states[chunk], *layer)
            arrived[chunk] = hop(states[chunk], index, index + 1)
    hbm = pl.BlockSpec(memory_space=pltpu.HBM)
    out_shape = jax.ShapeDtypeStruct((section_count * owned, lat_rows, frames, lat_cols * width), BF16)
    out = None
    for chunk, block in enumerate(blocks):
        operands = [arrived[chunk], states[chunk]] + ([out] if chunk else []) + layer
        specs = [vmem()] * len(operands)
        if chunk:
            specs[2] = hbm
        out = pl.pallas_call(
            functools.partial(last_kernel, block, frames, firsts[chunk], crosses()),
            out_shape=out_shape,
            in_specs=specs,
            out_specs=hbm,
            scratch_shapes=[pltpu.VMEM((block[0],) + out_shape.shape[1:], BF16), pltpu.SemaphoreType.DMA],
            input_output_aliases={2: 0} if chunk else {},
            compiler_params=params(),
            name="last_block",
        )(*operands)
    return out.reshape(1, section_count, owned, lat_rows, frames, lat_cols * width)


def solution(mesh):
    return jax.shard_map(
        per_device,
        mesh=mesh,
        in_specs=(
            P("section", None, "slab", None, None, None),
            P(),
            P(),
            P(),
            P(),
            P(),
            P(),
            P(),
            P(),
            P(),
            P(),
            P(),
            P("section", None),
            P("section", None),
            P("section", None, None, None, None),
            P("section", None),
        ),
        out_specs=P("section", None, "slab", None, None, None),
        check_vma=False,
    )
```

```python
import functools

import jax
import jax.numpy as jnp
from jax import lax
from jax.experimental import pallas as pl
from jax.experimental.pallas import tpu as pltpu
from jax.sharding import PartitionSpec as P

GROUPS = 32
LANES = 128
CUTS = (2,)
EPS = 1e-06
VMEM_LIMIT = 32 * 1024 * 1024
GROUPS_VMEM = 4 * 1024 * 1024
GROUPS_FLOPS = 12_000_000_000
F32 = jnp.float32
BF16 = jnp.bfloat16


def vmem():
    return pl.BlockSpec(memory_space=pltpu.VMEM)


def smem():
    return pl.BlockSpec(memory_space=pltpu.SMEM)


def params(limit=VMEM_LIMIT):
    return pltpu.CompilerParams(vmem_limit_bytes=limit)


def same_group(channels):
    size = channels // GROUPS

    def group_of(axis):
        index = lax.broadcasted_iota(jnp.int32, (channels, channels), axis).astype(F32)
        return jnp.floor((index + 0.5) * (1.0 / size))

    return jnp.where(group_of(0) == group_of(1), 1.0, 0.0).astype(BF16)


def groups_kernel(after_ref, *out_refs):
    del after_ref
    for out_ref in out_refs:
        out_ref[...] = same_group(out_ref.shape[0])


def group_sums(rows, same):
    high = rows.astype(BF16)
    rest = rows - high.astype(F32)
    middle = rest.astype(BF16)
    low = (rest - middle.astype(F32)).astype(BF16)
    total = jnp.dot(high, same, preferred_element_type=F32)
    total += jnp.dot(middle, same, preferred_element_type=F32)
    total += jnp.dot(low, same, preferred_element_type=F32)
    return total


def dot_last(left, right):
    return lax.dot_general(left, right, (((1,), (1,)), ((), ())), preferred_element_type=F32)


def silu(value):
    return 0.5 * value * (1.0 + jnp.tanh(0.5 * value))


def encode_kernel(slab_axis, *refs):
    (
        weight_ref, gain_ref, shift_ref, bias_ref, lat_weight_ref, lat_bias_ref, same_ref,
        out_ref, x_ref, pool_ref,
    ) = refs[-10:]
    pieces = refs[:-10]
    slab_rows = pieces[0].shape[2]
    items, frames, row_count, cols, channels = x_ref.shape
    for step, piece_ref in zip(piece_order(len(pieces)), pieces):
        for half in range(2):
            source = lax.axis_index(slab_axis) ^ (2 * step + (half if step == 0 else 1 - half))
            for item in range(items):
                for frame in range(frames):
                    piece = piece_ref[half, item, :, frame].astype(F32)
                    x_ref[item, frame, pl.ds(source * slab_rows, slab_rows)] = piece
    size = frames * row_count * cols
    plane = row_count * cols
    lat_rows, lat_cols = row_count // 2, cols // 2
    for item in range(items):
        x = x_ref[item].reshape(size, channels)
        sums = jnp.concatenate(
            [jnp.sum(x, axis=0, keepdims=True), jnp.sum(x * x, axis=0, keepdims=True)]
            + [jnp.zeros((6, channels), F32)],
            axis=0,
        )
        sums = group_sums(sums, same_ref[...]) * (1.0 / (size * (channels // GROUPS)))
        mean = sums[0:1]
        inverse = lax.rsqrt(sums[1:2] - mean * mean + EPS)
        act = silu((x - mean) * inverse * gain_ref[...] + shift_ref[...])
        column = lax.broadcasted_iota(jnp.int32, (size, 1), 0) & (cols - 1)
        taps = [
            jnp.where(column == 0, 0.0, pltpu.roll(act, 1, 0)),
            act,
            jnp.where(column == cols - 1, 0.0, pltpu.roll(act, size - 1, 0)),
        ]
        wide = jnp.concatenate(taps, axis=1).reshape(frames, row_count, cols, 3 * channels)
        edge = jnp.zeros((frames, 1, cols, 3 * channels), F32)
        wide = jnp.concatenate([edge, wide, edge], axis=1)
        total, still = x + bias_ref[...], None
        for row_tap in range(3):
            window = wide[:, row_tap : row_tap + row_count].reshape(size, 3 * channels).astype(BF16)
            weights = [weight_ref[time, row_tap].reshape(3 * channels, channels) for time in range(3)]
            total += jnp.dot(window, weights[2], preferred_element_type=F32)
            for weight in weights[:2]:
                term = jnp.dot(window[:plane], weight, preferred_element_type=F32)
                still = term if still is None else still + term
        paired = total.reshape(frames, lat_rows, 2, cols, channels)
        paired = paired + still.reshape(1, lat_rows, 2, cols, channels)
        merged = paired[:, :, 0] + paired[:, :, 1]
        halves = []
        for part in range(channels // LANES):
            for row in range(lat_rows):
                for frame in range(frames):
                    block = merged[frame, row, :, part * LANES : (part + 1) * LANES]
                    pool_ref[part, pl.ds((row * frames + frame) * cols, cols), :] = block
            picked = []
            for col in range(lat_cols):
                left = pool_ref[part, pl.ds(2 * col, lat_rows * frames, stride=cols), :]
                right = pool_ref[part, pl.ds(2 * col + 1, lat_rows * frames, stride=cols), :]
                picked.append((left + right) * 0.25)
            halves.append(jnp.concatenate(picked, axis=0))
        pooled = jnp.concatenate(halves, axis=1).astype(BF16)
        latent = dot_last(pooled, lat_weight_ref[...])
        out_ref[item] = (latent + lat_bias_ref[...]).astype(BF16)


def piece_order(steps):
    return (2, 3, 1, 0) if steps == 4 else tuple(range(steps))[::-1]


def encode(pieces, *operands):
    _, items, slab_rows, frames, cols, channels = pieces[0].shape
    row_count = 2 * len(pieces) * slab_rows
    lat_rows, lat_cols = row_count // 2, cols // 2
    return pl.pallas_call(
        functools.partial(encode_kernel, "slab"),
        out_shape=jax.ShapeDtypeStruct((items, lat_cols * lat_rows * frames, operands[-2].shape[1]), BF16),
        in_specs=[vmem()] * (len(pieces) + len(operands)),
        out_specs=vmem(),
        scratch_shapes=[
            pltpu.VMEM((items, frames, row_count, cols, channels), F32),
            pltpu.VMEM((channels // LANES, lat_rows * frames * cols, LANES), F32),
        ],
        compiler_params=params(),
        name="encode",
    )(*[pieces[step] for step in piece_order(len(pieces))], *operands)


def shifted(value, unit, frames):
    size = value.shape[0]
    place = lax.broadcasted_iota(jnp.int32, (size, 1), 0) & (unit - 1)
    return (
        jnp.where(place < frames, 0.0, pltpu.roll(value, frames, 0)),
        value,
        jnp.where(place >= unit - frames, 0.0, pltpu.roll(value, size - frames, 0)),
    )


def conv3(value, weight_ref, block, frames):
    streams, unit = block
    edge = streams * unit
    wide = jnp.concatenate(shifted(value, unit, frames), axis=1).astype(BF16)
    terms = []
    for col_tap, window in enumerate((wide[:-edge], wide, wide[edge:])):
        weight = jnp.concatenate([weight_ref[row_tap, col_tap] for row_tap in range(3)], axis=0)
        terms.append(jnp.dot(window, weight, preferred_element_type=F32))
    left, total, right = terms
    zeros = jnp.zeros((edge, total.shape[1]), F32)
    return total + jnp.concatenate([zeros, left], axis=0) + jnp.concatenate([right, zeros], axis=0)


def conv3_narrow(value, weight, block, frames):
    streams, unit = block
    size, channels = value.shape
    edge = streams * unit
    zeros = jnp.zeros((edge, channels), F32)
    windows = []
    for moved in shifted(value, unit, frames):
        padded = jnp.concatenate([zeros, moved, zeros], axis=0)
        for col_tap in range(3):
            windows.append(padded[col_tap * edge : col_tap * edge + size])
    window = jnp.concatenate(windows, axis=1).astype(BF16)
    return jnp.dot(window, weight, preferred_element_type=F32)


def unet_layer(state, operands, block, frames):
    weight_ref, gain_ref, shift_ref, bias_ref, same_ref = operands
    streams, unit = block
    size, channels = state.shape
    cols = size // (streams * unit)
    values = state.reshape(cols, streams, unit, channels)
    rows = []
    for item in range(streams):
        own = values[:, item].reshape(cols * unit, channels)
        rows.append(jnp.sum(own, axis=0, keepdims=True))
        rows.append(jnp.sum(own * own, axis=0, keepdims=True))
    rows.extend([jnp.zeros((1, channels), F32)] * (-len(rows) % 8))
    sums = group_sums(jnp.concatenate(rows, axis=0), same_ref[...])
    sums = sums * (1.0 / (cols * unit * (channels // GROUPS)))
    normed = []
    for item in range(streams):
        mean = sums[2 * item : 2 * item + 1]
        inverse = lax.rsqrt(sums[2 * item + 1 : 2 * item + 2] - mean * mean + EPS)
        scaled = (values[:, item : item + 1] - mean) * inverse * gain_ref[...]
        normed.append(scaled + shift_ref[...])
    act = silu(jnp.concatenate(normed, axis=1).reshape(size, channels))
    total = conv3(act, weight_ref, block, frames)
    return (state + total + bias_ref[...]).astype(BF16)


def write_output(out_ref, state, first, block, frames):
    streams, unit = block
    channels = state.shape[1]
    cols = state.shape[0] // (streams * unit)
    values = state.astype(F32).reshape(cols, streams, unit, channels)
    for item in range(streams):
        wide = jnp.concatenate([values[col, item] for col in range(cols)], axis=1)
        wide = wide.astype(BF16).reshape(unit // frames, frames, cols * channels)
        out_ref[first + item] = wide


def place_rows(clips_ref, offsets_ref, table, bias, out_ref, slab, owned, frames):
    streams, unit, _ = out_ref.shape
    table_rows = table.shape[1]
    row = lax.div(lax.broadcasted_iota(jnp.int32, (unit, table_rows), 0), jnp.int32(frames))
    wanted = lax.broadcasted_iota(jnp.int32, (unit, table_rows), 1) - row
    for stream in range(streams):
        micro = stream // owned
        offset = offsets_ref[micro, clips_ref[micro, slab * owned + stream % owned]]
        hot = jnp.where(wanted == offset, 1.0, 0.0).astype(BF16)
        out_ref[stream] = dot_last(hot, table) + bias


def first_kernel(block, frames, count, first, *refs):
    streams, unit = block
    latent_refs = refs[:count]
    place_ref, in_weight_ref, *operands = refs[count:-1]
    state_ref = refs[-1]

    @pl.when(lax.axis_index("section") == 0)
    def _():
        size, width = state_ref.shape
        cols = size // (streams * unit)
        parts = []
        for col in range(cols):
            for ref in latent_refs:
                for item in range(ref.shape[0]):
                    parts.append(ref[item, pl.ds(col * unit, unit), :].astype(F32))
        total = conv3_narrow(jnp.concatenate(parts, axis=0), in_weight_ref[...], block, frames)
        placed = place_ref[pl.ds(first, streams)]
        placed = placed.reshape(1, streams * unit, width)
        total = (total.reshape(cols, streams * unit, width) + placed).reshape(size, width)
        state = total.astype(BF16).astype(F32)
        state_ref[...] = unet_layer(state, operands, block, frames)


def later_kernel(index, block, frames, before_ref, kept_ref, *refs):
    del kept_ref
    *operands, state_ref = refs

    @pl.when(lax.axis_index("section") == index)
    def _():
        state_ref[...] = unet_layer(before_ref[...].astype(F32), operands, block, frames)


def last_kernel(block, frames, first, crossed, before_ref, kept_ref, *refs):
    streams = block[0]
    operands = refs[1:-3] if first else refs[:-3]
    out_ref, wide_ref, sem = refs[-3:]
    section = lax.axis_index("section")
    last = section == lax.axis_size("section") - 1

    @pl.when(last)
    def _():
        state = unet_layer(before_ref[...].astype(F32), operands, block, frames)
        write_output(wide_ref, state, 0, block, frames)

    @pl.when(jnp.logical_not(last))
    def _():
        state = kept_ref[...].astype(F32)
        if crossed:
            state = jnp.where(section < 2, before_ref[...].astype(F32), state)
        write_output(wide_ref, state, 0, block, frames)

    copy = pltpu.make_async_copy(wide_ref, out_ref.at[pl.ds(first, streams)], sem)
    copy.start()
    copy.wait()


def select_kernel(
    section_axis, slab_axis, owned, crossed,
    clips_ref, offsets_ref, features_ref, table_ref, bias_ref, keep_ref, give_ref, place_ref,
):
    section = lax.axis_index(section_axis)
    slab = lax.axis_index(slab_axis)
    for step in range(keep_ref.shape[0]):
        for half, out_ref in enumerate((keep_ref, give_ref)):
            for item in range(owned):
                other = half if step == 0 else 1 - half
                slot = (slab ^ (2 * step + other)) * owned + item
                out_ref[step, item] = features_ref[clips_ref[section, slot]]
    bias = bias_ref[...].reshape(1, -1)
    frames = features_ref.shape[2]
    worker = slab ^ 1 if crossed else slab
    place_rows(clips_ref, offsets_ref, table_ref[...], bias, place_ref, worker, owned, frames)


def exchange(features, slot_clips, row_offsets, table, bias, place_shape, slab_count, owned):
    steps = slab_count // 2
    shape = jax.ShapeDtypeStruct((steps, owned) + features.shape[1:], BF16)
    keep, give, place = pl.pallas_call(
        functools.partial(select_kernel, "section", "slab", owned, crosses()),
        out_shape=[shape, shape, jax.ShapeDtypeStruct(place_shape, F32)],
        in_specs=[smem()] * 2 + [vmem()] * 3,
        out_specs=[vmem()] * 3,
        name="select",
    )(slot_clips, row_offsets, features, table, bias)
    got = swap_cores(give)
    pieces = [jnp.stack([keep[step], got[step]]) for step in range(steps)]
    for step in range(1, steps):
        pairs = [(slab, slab ^ (2 * step + 1)) for slab in range(slab_count)]
        pieces[step] = lax.ppermute(pieces[step], "slab", pairs)
    return pieces, got, place


ROUTES = {
    (0, 1): ((1, False), (3, False), (2, True), (0, False)),
    (1, 2): ((0, True), (2, True), (3, True), (1, True)),
    (2, 3): ((0, True), (1, True), (3, False), (2, False)),
}


def crosses():
    return lax.axis_size("section") == 4 and lax.axis_size("slab") % 2 == 0


def send(value, routes):
    if not any(cross for _, cross in routes):
        return lax.ppermute(value, "section", [(s, target) for s, (target, _) in enumerate(routes)])
    slabs = lax.axis_size("slab")
    pairs = []
    for s, (target, cross) in enumerate(routes):
        pairs += [(s * slabs + slab, target * slabs + (slab ^ 1 if cross else slab)) for slab in range(slabs)]
    return lax.ppermute(value, ("section", "slab"), pairs)


def swap_cores(value):
    return lax.ppermute(value, "slab", [(slab, slab ^ 1) for slab in range(lax.axis_size("slab"))])


def hop(value, source, target):
    count = lax.axis_size("section")
    if crosses():
        return send(value, ROUTES[source, target])
    if count & (count - 1):
        return lax.ppermute(value, "section", [(source, target)])
    return lax.ppermute(value, "section", [(s, s ^ source ^ target) for s in range(count)])


def gather_first(value):
    count = lax.axis_size("section")
    if count & (count - 1):
        return [value] + [hop(value, other, 0) for other in range(1, count)]
    if count == 4:
        own = swap_cores(value) if crosses() else value
        return [own] + [send(value, [(s ^ k, crosses()) for s in range(4)]) for k in (1, 2, 3)]
    parts = [value]
    step = 1
    while step < count:
        held = parts[0] if len(parts) == 1 else jnp.concatenate(parts, axis=0)
        parts.append(lax.ppermute(held, "section", [(s, s ^ step) for s in range(count)]))
        step *= 2
    return parts


def per_device(
    features, vae_weight, vae_gain, vae_shift, vae_bias, latent_weight, latent_bias, slot_clips, row_offsets,
    in_weight, in_bias, pos_table, unet_gain, unet_shift, unet_weight, unet_bias,
):
    section_count = lax.axis_size("section")
    slab_count = lax.axis_size("slab")
    _, clip_total, slab_rows, frames, cols, channels = features.shape
    owned = clip_total // slab_count
    row_total = slab_rows * slab_count
    width = unet_weight.shape[-1]
    lat_rows, lat_cols = row_total // 2, cols // 2
    unit = lat_rows * frames

    place_shape = (section_count * owned, unit, width)
    pieces, got, place = exchange(
        features[0], slot_clips, row_offsets, pos_table.T, in_bias, place_shape, slab_count, owned
    )
    vae_same, unet_same = pl.pallas_call(
        groups_kernel,
        out_shape=[jax.ShapeDtypeStruct((size, size), BF16) for size in (channels, width)],
        in_specs=[pl.BlockSpec(memory_space=pl.ANY)],
        out_specs=[vmem()] * 2,
        compiler_params=params(GROUPS_VMEM),
        cost_estimate=pl.CostEstimate(flops=GROUPS_FLOPS, bytes_accessed=0, transcendentals=0),
        name="groups",
    )(got)
    latent = encode(
        pieces, vae_weight, vae_gain.reshape(1, -1), vae_shift.reshape(1, -1), vae_bias.reshape(1, -1),
        latent_weight.T, latent_bias.reshape(1, -1), vae_same,
    )
    latents = gather_first(latent)

    if section_count == 4:
        parts = [latents[first:last] for first, last in zip((0,) + CUTS, CUTS + (4,))]
    elif section_count & (section_count - 1):
        parts = [latents]
    else:
        parts = [latents[:-1], latents[-1:]]
    layer = [unet_weight[0], unet_gain, unet_shift, unet_bias, unet_same]
    blocks, firsts, states, arrived = [], [], [], []
    for part in parts:
        streams = sum(array.shape[0] for array in part)
        firsts.append(sum(block[0] for block in blocks))
        blocks.append((streams, unit))
        operands = part + [place, in_weight.reshape(-1, width)] + layer
        state = pl.pallas_call(
            functools.partial(first_kernel, blocks[-1], frames, len(part), firsts[-1]),
            out_shape=jax.ShapeDtypeStruct((lat_cols * streams * unit, width), BF16),
            in_specs=[vmem()] * len(operands),
            out_specs=vmem(),
            compiler_params=params(),
            name="first_block",
        )(*operands)
        states.append(state)
        arrived.append(hop(state, 0, 1))
    for index in range(1, section_count - 1):
        for chunk, block in enumerate(blocks):
            states[chunk] = pl.pallas_call(
                functools.partial(later_kernel, index, block, frames),
                out_shape=jax.ShapeDtypeStruct(states[chunk].shape, BF16),
                in_specs=[vmem()] * (2 + len(layer)),
                out_specs=vmem(),
                input_output_aliases={1: 0},
                compiler_params=params(),
                name="later_block",
            )(arrived[chunk], states[chunk], *layer)
            arrived[chunk] = hop(states[chunk], index, index + 1)
    hbm = pl.BlockSpec(memory_space=pltpu.HBM)
    out_shape = jax.ShapeDtypeStruct((section_count * owned, lat_rows, frames, lat_cols * width), BF16)
    out = None
    for chunk, block in enumerate(blocks):
        operands = [arrived[chunk], states[chunk]] + ([out] if chunk else []) + layer
        specs = [vmem()] * len(operands)
        if chunk:
            specs[2] = hbm
        out = pl.pallas_call(
            functools.partial(last_kernel, block, frames, firsts[chunk], crosses()),
            out_shape=out_shape,
            in_specs=specs,
            out_specs=hbm,
            scratch_shapes=[pltpu.VMEM((block[0],) + out_shape.shape[1:], BF16), pltpu.SemaphoreType.DMA],
            input_output_aliases={2: 0} if chunk else {},
            compiler_params=params(),
            name="last_block",
        )(*operands)
    return out.reshape(1, section_count, owned, lat_rows, frames, lat_cols * width)


def solution(mesh):
    return jax.shard_map(
        per_device,
        mesh=mesh,
        in_specs=(
            P("section", None, "slab", None, None, None),
            P(),
            P(),
            P(),
            P(),
            P(),
            P(),
            P(),
            P(),
            P(),
            P(),
            P(),
            P("section", None),
            P("section", None),
            P("section", None, None, None, None),
            P("section", None),
        ),
        out_specs=P("section", None, "slab", None, None, None),
        check_vma=False,
    )
```

```python
import functools

import jax
import jax.numpy as jnp
from jax import lax
from jax.experimental import pallas as pl
from jax.experimental.pallas import tpu as pltpu
from jax.sharding import PartitionSpec as P

GROUPS = 32
LANES = 128
CUTS = (2,)
EPS = 1e-06
VMEM_LIMIT = 32 * 1024 * 1024
GROUPS_VMEM = 4 * 1024 * 1024
GROUPS_FLOPS = 12_000_000_000
F32 = jnp.float32
BF16 = jnp.bfloat16


def vmem():
    return pl.BlockSpec(memory_space=pltpu.VMEM)


def smem():
    return pl.BlockSpec(memory_space=pltpu.SMEM)


def params(limit=VMEM_LIMIT):
    return pltpu.CompilerParams(vmem_limit_bytes=limit)


def same_group(channels):
    size = channels // GROUPS

    def group_of(axis):
        index = lax.broadcasted_iota(jnp.int32, (channels, channels), axis).astype(F32)
        return jnp.floor((index + 0.5) * (1.0 / size))

    return jnp.where(group_of(0) == group_of(1), 1.0, 0.0).astype(BF16)


def groups_kernel(after_ref, *out_refs):
    del after_ref
    for out_ref in out_refs:
        out_ref[...] = same_group(out_ref.shape[0])


def group_sums(rows, same):
    high = rows.astype(BF16)
    rest = rows - high.astype(F32)
    middle = rest.astype(BF16)
    low = (rest - middle.astype(F32)).astype(BF16)
    total = jnp.dot(high, same, preferred_element_type=F32)
    total += jnp.dot(middle, same, preferred_element_type=F32)
    total += jnp.dot(low, same, preferred_element_type=F32)
    return total


def dot_last(left, right):
    return lax.dot_general(left, right, (((1,), (1,)), ((), ())), preferred_element_type=F32)


def silu(value):
    return 0.5 * value * (1.0 + jnp.tanh(0.5 * value))


def encode_kernel(slab_axis, *refs):
    (
        weight_ref, gain_ref, shift_ref, bias_ref, lat_weight_ref, lat_bias_ref, same_ref,
        out_ref, x_ref, pool_ref,
    ) = refs[-10:]
    pieces = refs[:-10]
    slab_rows = pieces[0].shape[2]
    items, frames, row_count, cols, channels = x_ref.shape
    for step, piece_ref in zip(piece_order(len(pieces)), pieces):
        for half in range(2):
            source = lax.axis_index(slab_axis) ^ (2 * step + (half if step == 0 else 1 - half))
            for item in range(items):
                for frame in range(frames):
                    piece = piece_ref[half, item, :, frame].astype(F32)
                    x_ref[item, frame, pl.ds(source * slab_rows, slab_rows)] = piece
    size = frames * row_count * cols
    plane = row_count * cols
    lat_rows, lat_cols = row_count // 2, cols // 2
    for item in range(items):
        x = x_ref[item].reshape(size, channels)
        sums = jnp.concatenate(
            [jnp.sum(x, axis=0, keepdims=True), jnp.sum(x * x, axis=0, keepdims=True)]
            + [jnp.zeros((6, channels), F32)],
            axis=0,
        )
        sums = group_sums(sums, same_ref[...]) * (1.0 / (size * (channels // GROUPS)))
        mean = sums[0:1]
        inverse = lax.rsqrt(sums[1:2] - mean * mean + EPS)
        act = silu((x - mean) * (inverse * gain_ref[...]) + shift_ref[...])
        column = lax.broadcasted_iota(jnp.int32, (size, 1), 0) & (cols - 1)
        taps = [
            jnp.where(column == 0, 0.0, pltpu.roll(act, 1, 0)),
            act,
            jnp.where(column == cols - 1, 0.0, pltpu.roll(act, size - 1, 0)),
        ]
        wide = jnp.concatenate(taps, axis=1).reshape(frames, row_count, cols, 3 * channels)
        edge = jnp.zeros((frames, 1, cols, 3 * channels), F32)
        wide = jnp.concatenate([edge, wide, edge], axis=1)
        total, still = x + bias_ref[...], None
        for row_tap in range(3):
            window = wide[:, row_tap : row_tap + row_count].reshape(size, 3 * channels).astype(BF16)
            weights = [weight_ref[time, row_tap].reshape(3 * channels, channels) for time in range(3)]
            total += jnp.dot(window, weights[2], preferred_element_type=F32)
            for weight in weights[:2]:
                term = jnp.dot(window[:plane], weight, preferred_element_type=F32)
                still = term if still is None else still + term
        paired = total.reshape(frames, lat_rows, 2, cols, channels)
        paired = paired + still.reshape(1, lat_rows, 2, cols, channels)
        merged = paired[:, :, 0] + paired[:, :, 1]
        halves = []
        for part in range(channels // LANES):
            for row in range(lat_rows):
                for frame in range(frames):
                    block = merged[frame, row, :, part * LANES : (part + 1) * LANES]
                    pool_ref[part, pl.ds((row * frames + frame) * cols, cols), :] = block
            picked = []
            for col in range(lat_cols):
                left = pool_ref[part, pl.ds(2 * col, lat_rows * frames, stride=cols), :]
                right = pool_ref[part, pl.ds(2 * col + 1, lat_rows * frames, stride=cols), :]
                picked.append((left + right) * 0.25)
            halves.append(jnp.concatenate(picked, axis=0))
        pooled = jnp.concatenate(halves, axis=1).astype(BF16)
        latent = dot_last(pooled, lat_weight_ref[...])
        out_ref[item] = (latent + lat_bias_ref[...]).astype(BF16)


def piece_order(steps):
    return (2, 3, 1, 0) if steps == 4 else tuple(range(steps))[::-1]


def encode(pieces, *operands):
    _, items, slab_rows, frames, cols, channels = pieces[0].shape
    row_count = 2 * len(pieces) * slab_rows
    lat_rows, lat_cols = row_count // 2, cols // 2
    return pl.pallas_call(
        functools.partial(encode_kernel, "slab"),
        out_shape=jax.ShapeDtypeStruct((items, lat_cols * lat_rows * frames, operands[-2].shape[1]), BF16),
        in_specs=[vmem()] * (len(pieces) + len(operands)),
        out_specs=vmem(),
        scratch_shapes=[
            pltpu.VMEM((items, frames, row_count, cols, channels), F32),
            pltpu.VMEM((channels // LANES, lat_rows * frames * cols, LANES), F32),
        ],
        compiler_params=params(),
        name="encode",
    )(*[pieces[step] for step in piece_order(len(pieces))], *operands)


def shifted(value, unit, frames):
    size = value.shape[0]
    place = lax.broadcasted_iota(jnp.int32, (size, 1), 0) & (unit - 1)
    return (
        jnp.where(place < frames, 0.0, pltpu.roll(value, frames, 0)),
        value,
        jnp.where(place >= unit - frames, 0.0, pltpu.roll(value, size - frames, 0)),
    )


def conv3(value, weight_ref, block, frames):
    streams, unit = block
    edge = streams * unit
    wide = jnp.concatenate(shifted(value, unit, frames), axis=1).astype(BF16)
    terms = []
    for col_tap, window in enumerate((wide[:-edge], wide, wide[edge:])):
        weight = jnp.concatenate([weight_ref[row_tap, col_tap] for row_tap in range(3)], axis=0)
        terms.append(jnp.dot(window, weight, preferred_element_type=F32))
    left, total, right = terms
    zeros = jnp.zeros((edge, total.shape[1]), F32)
    return total + jnp.concatenate([zeros, left], axis=0) + jnp.concatenate([right, zeros], axis=0)


def conv3_narrow(value, weight, block, frames):
    streams, unit = block
    size, channels = value.shape
    edge = streams * unit
    zeros = jnp.zeros((edge, channels), F32)
    windows = []
    for moved in shifted(value, unit, frames):
        padded = jnp.concatenate([zeros, moved, zeros], axis=0)
        for col_tap in range(3):
            windows.append(padded[col_tap * edge : col_tap * edge + size])
    window = jnp.concatenate(windows, axis=1).astype(BF16)
    return jnp.dot(window, weight, preferred_element_type=F32)


def unet_layer(state, operands, block, frames):
    weight_ref, gain_ref, shift_ref, bias_ref, same_ref = operands
    streams, unit = block
    size, channels = state.shape
    cols = size // (streams * unit)
    values = state.reshape(cols, streams, unit, channels)
    rows = []
    for item in range(streams):
        own = values[:, item].reshape(cols * unit, channels)
        rows.append(jnp.sum(own, axis=0, keepdims=True))
        rows.append(jnp.sum(own * own, axis=0, keepdims=True))
    rows.extend([jnp.zeros((1, channels), F32)] * (-len(rows) % 8))
    sums = group_sums(jnp.concatenate(rows, axis=0), same_ref[...])
    sums = sums * (1.0 / (cols * unit * (channels // GROUPS)))
    normed = []
    for item in range(streams):
        mean = sums[2 * item : 2 * item + 1]
        inverse = lax.rsqrt(sums[2 * item + 1 : 2 * item + 2] - mean * mean + EPS)
        factor = inverse * gain_ref[...]
        normed.append((values[:, item : item + 1] - mean) * factor + shift_ref[...])
    act = silu(jnp.concatenate(normed, axis=1).reshape(size, channels))
    total = conv3(act, weight_ref, block, frames)
    return (state + total + bias_ref[...]).astype(BF16)


def write_output(out_ref, state, first, block, frames):
    streams, unit = block
    channels = state.shape[1]
    cols = state.shape[0] // (streams * unit)
    values = state.astype(F32).reshape(cols, streams, unit, channels)
    for item in range(streams):
        wide = jnp.concatenate([values[col, item] for col in range(cols)], axis=1)
        wide = wide.astype(BF16).reshape(unit // frames, frames, cols * channels)
        out_ref[first + item] = wide


def place_rows(clips_ref, offsets_ref, table, bias, out_ref, slab, owned, frames):
    streams, unit, _ = out_ref.shape
    table_rows = table.shape[1]
    row = lax.div(lax.broadcasted_iota(jnp.int32, (unit, table_rows), 0), jnp.int32(frames))
    wanted = lax.broadcasted_iota(jnp.int32, (unit, table_rows), 1) - row
    for stream in range(streams):
        micro = stream // owned
        offset = offsets_ref[micro, clips_ref[micro, slab * owned + stream % owned]]
        hot = jnp.where(wanted == offset, 1.0, 0.0).astype(BF16)
        out_ref[stream] = dot_last(hot, table) + bias


def first_kernel(block, frames, count, first, *refs):
    streams, unit = block
    latent_refs = refs[:count]
    place_ref, in_weight_ref, *operands = refs[count:-1]
    state_ref = refs[-1]

    @pl.when(lax.axis_index("section") == 0)
    def _():
        size, width = state_ref.shape
        cols = size // (streams * unit)
        parts = []
        for col in range(cols):
            for ref in latent_refs:
                for item in range(ref.shape[0]):
                    parts.append(ref[item, pl.ds(col * unit, unit), :].astype(F32))
        total = conv3_narrow(jnp.concatenate(parts, axis=0), in_weight_ref[...], block, frames)
        placed = place_ref[pl.ds(first, streams)]
        placed = placed.reshape(1, streams * unit, width)
        total = (total.reshape(cols, streams * unit, width) + placed).reshape(size, width)
        state = total.astype(BF16).astype(F32)
        state_ref[...] = unet_layer(state, operands, block, frames)


def later_kernel(index, block, frames, before_ref, kept_ref, *refs):
    del kept_ref
    *operands, state_ref = refs

    @pl.when(lax.axis_index("section") == index)
    def _():
        state_ref[...] = unet_layer(before_ref[...].astype(F32), operands, block, frames)


def last_kernel(block, frames, first, crossed, before_ref, kept_ref, *refs):
    streams = block[0]
    operands = refs[1:-3] if first else refs[:-3]
    out_ref, wide_ref, sem = refs[-3:]
    section = lax.axis_index("section")
    last = section == lax.axis_size("section") - 1

    @pl.when(last)
    def _():
        state = unet_layer(before_ref[...].astype(F32), operands, block, frames)
        write_output(wide_ref, state, 0, block, frames)

    @pl.when(jnp.logical_not(last))
    def _():
        state = kept_ref[...].astype(F32)
        if crossed:
            state = jnp.where(section < 2, before_ref[...].astype(F32), state)
        write_output(wide_ref, state, 0, block, frames)

    copy = pltpu.make_async_copy(wide_ref, out_ref.at[pl.ds(first, streams)], sem)
    copy.start()
    copy.wait()


def select_kernel(
    section_axis, slab_axis, owned, crossed,
    clips_ref, offsets_ref, features_ref, table_ref, bias_ref, keep_ref, give_ref, place_ref,
):
    section = lax.axis_index(section_axis)
    slab = lax.axis_index(slab_axis)
    for step in range(keep_ref.shape[0]):
        for half, out_ref in enumerate((keep_ref, give_ref)):
            for item in range(owned):
                other = half if step == 0 else 1 - half
                slot = (slab ^ (2 * step + other)) * owned + item
                out_ref[step, item] = features_ref[clips_ref[section, slot]]
    bias = bias_ref[...].reshape(1, -1)
    frames = features_ref.shape[2]
    worker = slab ^ 1 if crossed else slab
    place_rows(clips_ref, offsets_ref, table_ref[...], bias, place_ref, worker, owned, frames)


def exchange(features, slot_clips, row_offsets, table, bias, place_shape, slab_count, owned):
    steps = slab_count // 2
    shape = jax.ShapeDtypeStruct((steps, owned) + features.shape[1:], BF16)
    keep, give, place = pl.pallas_call(
        functools.partial(select_kernel, "section", "slab", owned, crosses()),
        out_shape=[shape, shape, jax.ShapeDtypeStruct(place_shape, F32)],
        in_specs=[smem()] * 2 + [vmem()] * 3,
        out_specs=[vmem()] * 3,
        name="select",
    )(slot_clips, row_offsets, features, table, bias)
    got = swap_cores(give)
    pieces = [jnp.stack([keep[step], got[step]]) for step in range(steps)]
    for step in range(1, steps):
        pairs = [(slab, slab ^ (2 * step + 1)) for slab in range(slab_count)]
        pieces[step] = lax.ppermute(pieces[step], "slab", pairs)
    return pieces, got, place


ROUTES = {
    (0, 1): ((1, False), (3, False), (2, True), (0, False)),
    (1, 2): ((0, True), (2, True), (3, True), (1, True)),
    (2, 3): ((0, True), (1, True), (3, False), (2, False)),
}


def crosses():
    return lax.axis_size("section") == 4 and lax.axis_size("slab") % 2 == 0


def send(value, routes):
    if not any(cross for _, cross in routes):
        return lax.ppermute(value, "section", [(s, target) for s, (target, _) in enumerate(routes)])
    slabs = lax.axis_size("slab")
    pairs = []
    for s, (target, cross) in enumerate(routes):
        pairs += [(s * slabs + slab, target * slabs + (slab ^ 1 if cross else slab)) for slab in range(slabs)]
    return lax.ppermute(value, ("section", "slab"), pairs)


def swap_cores(value):
    return lax.ppermute(value, "slab", [(slab, slab ^ 1) for slab in range(lax.axis_size("slab"))])


def hop(value, source, target):
    count = lax.axis_size("section")
    if crosses():
        return send(value, ROUTES[source, target])
    if count & (count - 1):
        return lax.ppermute(value, "section", [(source, target)])
    return lax.ppermute(value, "section", [(s, s ^ source ^ target) for s in range(count)])


def gather_first(value):
    count = lax.axis_size("section")
    if count & (count - 1):
        return [value] + [hop(value, other, 0) for other in range(1, count)]
    if count == 4:
        own = swap_cores(value) if crosses() else value
        return [own] + [send(value, [(s ^ k, crosses()) for s in range(4)]) for k in (1, 2, 3)]
    parts = [value]
    step = 1
    while step < count:
        held = parts[0] if len(parts) == 1 else jnp.concatenate(parts, axis=0)
        parts.append(lax.ppermute(held, "section", [(s, s ^ step) for s in range(count)]))
        step *= 2
    return parts


def per_device(
    features, vae_weight, vae_gain, vae_shift, vae_bias, latent_weight, latent_bias, slot_clips, row_offsets,
    in_weight, in_bias, pos_table, unet_gain, unet_shift, unet_weight, unet_bias,
):
    section_count = lax.axis_size("section")
    slab_count = lax.axis_size("slab")
    _, clip_total, slab_rows, frames, cols, channels = features.shape
    owned = clip_total // slab_count
    row_total = slab_rows * slab_count
    width = unet_weight.shape[-1]
    lat_rows, lat_cols = row_total // 2, cols // 2
    unit = lat_rows * frames

    place_shape = (section_count * owned, unit, width)
    pieces, got, place = exchange(
        features[0], slot_clips, row_offsets, pos_table.T, in_bias, place_shape, slab_count, owned
    )
    vae_same, unet_same = pl.pallas_call(
        groups_kernel,
        out_shape=[jax.ShapeDtypeStruct((size, size), BF16) for size in (channels, width)],
        in_specs=[pl.BlockSpec(memory_space=pl.ANY)],
        out_specs=[vmem()] * 2,
        compiler_params=params(GROUPS_VMEM),
        cost_estimate=pl.CostEstimate(flops=GROUPS_FLOPS, bytes_accessed=0, transcendentals=0),
        name="groups",
    )(got)
    latent = encode(
        pieces, vae_weight, vae_gain.reshape(1, -1), vae_shift.reshape(1, -1), vae_bias.reshape(1, -1),
        latent_weight.T, latent_bias.reshape(1, -1), vae_same,
    )
    latents = gather_first(latent)

    if section_count == 4:
        parts = [latents[first:last] for first, last in zip((0,) + CUTS, CUTS + (4,))]
    elif section_count & (section_count - 1):
        parts = [latents]
    else:
        parts = [latents[:-1], latents[-1:]]
    layer = [unet_weight[0], unet_gain, unet_shift, unet_bias, unet_same]
    blocks, firsts, states, arrived = [], [], [], []
    for part in parts:
        streams = sum(array.shape[0] for array in part)
        firsts.append(sum(block[0] for block in blocks))
        blocks.append((streams, unit))
        operands = part + [place, in_weight.reshape(-1, width)] + layer
        state = pl.pallas_call(
            functools.partial(first_kernel, blocks[-1], frames, len(part), firsts[-1]),
            out_shape=jax.ShapeDtypeStruct((lat_cols * streams * unit, width), BF16),
            in_specs=[vmem()] * len(operands),
            out_specs=vmem(),
            compiler_params=params(),
            name="first_block",
        )(*operands)
        states.append(state)
        arrived.append(hop(state, 0, 1))
    for index in range(1, section_count - 1):
        for chunk, block in enumerate(blocks):
            states[chunk] = pl.pallas_call(
                functools.partial(later_kernel, index, block, frames),
                out_shape=jax.ShapeDtypeStruct(states[chunk].shape, BF16),
                in_specs=[vmem()] * (2 + len(layer)),
                out_specs=vmem(),
                input_output_aliases={1: 0},
                compiler_params=params(),
                name="later_block",
            )(arrived[chunk], states[chunk], *layer)
            arrived[chunk] = hop(states[chunk], index, index + 1)
    hbm = pl.BlockSpec(memory_space=pltpu.HBM)
    out_shape = jax.ShapeDtypeStruct((section_count * owned, lat_rows, frames, lat_cols * width), BF16)
    out = None
    for chunk, block in enumerate(blocks):
        operands = [arrived[chunk], states[chunk]] + ([out] if chunk else []) + layer
        specs = [vmem()] * len(operands)
        if chunk:
            specs[2] = hbm
        out = pl.pallas_call(
            functools.partial(last_kernel, block, frames, firsts[chunk], crosses()),
            out_shape=out_shape,
            in_specs=specs,
            out_specs=hbm,
            scratch_shapes=[pltpu.VMEM((block[0],) + out_shape.shape[1:], BF16), pltpu.SemaphoreType.DMA],
            input_output_aliases={2: 0} if chunk else {},
            compiler_params=params(),
            name="last_block",
        )(*operands)
    return out.reshape(1, section_count, owned, lat_rows, frames, lat_cols * width)


def solution(mesh):
    return jax.shard_map(
        per_device,
        mesh=mesh,
        in_specs=(
            P("section", None, "slab", None, None, None),
            P(),
            P(),
            P(),
            P(),
            P(),
            P(),
            P(),
            P(),
            P(),
            P(),
            P(),
            P("section", None),
            P("section", None),
            P("section", None, None, None, None),
            P("section", None),
        ),
        out_specs=P("section", None, "slab", None, None, None),
        check_vma=False,
    )
```
